32 devices in a mesh: tm: 4 (over z), chan: 8 (over y, x, core).
Axes of the slice: x: 2, y: 2, z: 4, core: 2. Of those that a mesh axis runs over, the one named last changes fastest.
Arguments:
- phase_step: float32 [8, 256, 32768], P(None, 'tm', 'chan'), may hold values from -3.1416 to 3.1416, as said below
- wrap_count: int32 [8, 256, 32768], P(None, 'tm', 'chan'), may hold values from -1 to 1
- coupling: float32 [8], replicated, may hold values from 0.5 to 2
- filter_taps: float32 [8, 128], replicated, may hold values from -0.06 to 0.06
Outputs:
- strain: float32 [8, 256, 32768], P(None, 'tm', 'chan')
The draws below stay inside these ranges and needn't reach their ends.
Inputs may be any that keep to these rules, and one draw needn't show every extreme that they name: `phase_step`: wrapped phase differences, within -pi to pi.
All inputs are finite; a program needn't handle non-finite values.
Results may differ from the reference program's by a relative error of at most 0.00007.
Values sent between devices are 32-bit elements; how exact they have to be, the bound alone decides.
No kernel may reach another device: no remote copies, remote signals or barrier semaphores. Data moves between devices by JAX's collectives and lax.ppermute only.
A program may use at most 128 MiB of HBM per device.

```python
import math
import jax
import jax.numpy as jnp
from jax import lax

CABLES = 8
TAPS = 128
CHANNELS = 32768
TIME = 256


def draw_phase_step(key, part):
    first_key = jax.random.fold_in(key, 11)
    second_key = jax.random.fold_in(key, 23)
    channel_ramp = 1.0 + 2.0 * jnp.arange(CHANNELS, dtype=jnp.float32) / (CHANNELS - 1)
    common = jax.random.uniform(first_key, (1, TIME, 1), jnp.float32, -0.7, 0.7)
    noise = jax.random.uniform(second_key, (CABLES, TIME, CHANNELS), jnp.float32, -1.0, 1.0)
    return common * channel_ramp[None, None, :] + noise


def set_ends(drawn, stream_key, low, top_value):
    longest = drawn.shape.index(max(drawn.shape))
    spots = []
    for shift in (0, 1):
        where = [jax.random.randint(jax.random.fold_in(stream_key, axis), (), 0, length) for axis, length in enumerate(drawn.shape)]
        where[longest] = (where[longest] + shift) % drawn.shape[longest]
        spots.append(tuple(where))
    return drawn.at[spots[0]].set(low).at[spots[1]].set(top_value)


def normal_values(own_key, extent, scale, bound, kind=jnp.bfloat16):
    values = scale * jax.random.normal(own_key, extent, jnp.float32)
    return jnp.clip(values, min=-bound, max=bound).astype(kind)


def setup_inputs(seed: int = 0) -> dict:
    seeds = jax.random.split(jax.random.key(seed), 5)
    return {
        "phase_step": draw_phase_step(jax.random.fold_in(seeds[4], 71), 0),
        "wrap_count": set_ends(jax.random.randint(seeds[1], (CABLES, TIME, CHANNELS), -1, 2), jax.random.fold_in(seeds[1], 1), -1, 1).astype(jnp.int32),
        "coupling": jnp.clip(jnp.exp(jax.random.uniform(seeds[2], (CABLES,), jnp.float32, math.log(0.5), math.log(2.0))), 0.5, 2.0),
        "filter_taps": normal_values(seeds[3], (CABLES, TAPS), 0.01, 0.06, jnp.float32),
    }


two_pi = 2.0 * math.pi


def spatial_filter(padded, filter_taps):
    stacked = jnp.transpose(padded, (1, 0, 2))
    kernel = filter_taps[:, None, :]
    result = lax.conv_general_dilated(stacked, kernel, (1,), "VALID", feature_group_count=filter_taps.shape[0], precision=lax.Precision.HIGHEST)
    return jnp.transpose(result, (1, 0, 2))


def reference(phase_step, wrap_count, coupling, filter_taps):
    increment = phase_step + two_pi * wrap_count.astype(jnp.float32)
    unwrapped = jnp.cumsum(increment, axis=1)
    population = phase_step.shape[0] * phase_step.shape[2]
    common = jnp.sum(unwrapped, axis=(0, 2)) / population
    leveled = unwrapped - coupling[:, None, None] * common[None, :, None]
    half = TAPS // 2
    padded = jnp.pad(leveled, ((0, 0), (0, 0), (half, half - 1)))
    filtered = spatial_filter(padded, filter_taps)
    return (leveled - filtered) * (1.0 / (4.0 * two_pi))
```

```python
import functools
import math

import jax
import jax.numpy as jnp
from jax import lax
from jax.experimental import pallas as pl
from jax.experimental.pallas import tpu as pltpu
from jax.sharding import PartitionSpec as P

two_pi = 2.0 * math.pi
LANES = 128
SUBLANES = 8


def shifted_down(value, amount):
    rows = lax.broadcasted_iota(jnp.int32, value.shape, 0)
    return jnp.where(rows >= amount, pltpu.roll(value, amount, 0), 0.0)


def scanned(pieces):
    sums, carry = [], None
    for value in pieces:
        amount = 1
        while amount < SUBLANES:
            value = value + shifted_down(value, amount)
            amount *= 2
        if carry is not None:
            value = value + carry
        carry = jnp.broadcast_to(value[SUBLANES - 1 :, :], value.shape)
        sums.append(value)
    return sums


def store_split(high_ref, low_ref, cable, block, sums):
    for pair in range(0, len(sums), 2):
        both = jnp.concatenate(sums[pair : pair + 2], axis=0)
        high = both.astype(jnp.bfloat16)
        low = (both - high.astype(jnp.float32)).astype(jnp.bfloat16)
        rows = pl.ds(pair * SUBLANES, 2 * SUBLANES)
        high_ref[cable, block, rows, :] = high
        low_ref[cable, block, rows, :] = low


def unwrap_kernel(
    phase_hbm, wrap_hbm, left_ref, right_ref, taps_ref,
    high_ref, low_ref, totals_ref, sums_ref, weight_ref,
    phase_ref, wrap_ref, sem,
):
    cables, time, width = phase_hbm.shape
    blocks = width // LANES
    groups = time // SUBLANES

    def copies(cable):
        return (
            pltpu.make_async_copy(phase_hbm.at[cable], phase_ref.at[cable], sem.at[0, cable]),
            pltpu.make_async_copy(wrap_hbm.at[cable], wrap_ref.at[cable], sem.at[1, cable]),
        )

    for cable in range(cables):
        for copy in copies(cable):
            copy.start()

    outputs = lax.broadcasted_iota(jnp.int32, (LANES, LANES), 0)
    inputs = lax.broadcasted_iota(jnp.int32, (LANES, LANES), 1)
    centre = (lax.broadcasted_iota(jnp.int32, (1, LANES), 1) == LANES // 2).astype(jnp.float32)

    @pl.loop(0, cables)
    def _(cable):
        row = (centre - taps_ref[pl.ds(cable, 1), :]) * (1.0 / (4.0 * two_pi))
        circulant = pltpu.roll(
            jnp.broadcast_to(row, (LANES, LANES)), 0, 1, stride=1, stride_axis=0
        )
        first = jnp.where(inputs >= outputs, circulant, 0.0).T
        second = jnp.where(inputs < outputs, circulant, 0.0).T
        band = jnp.concatenate([first, second], axis=1)
        high = band.astype(jnp.bfloat16)
        low = (band - high.astype(jnp.float32)).astype(jnp.bfloat16)
        for place, part in enumerate((high, high, low, low)):
            weight_ref[cable, pl.ds(place * LANES, LANES), :] = part
        for edge_ref, block in ((left_ref, 0), (right_ref, blocks + 1)):
            sums = scanned(
                [edge_ref[cable, pl.ds(i * SUBLANES, SUBLANES), :] for i in range(groups)]
            )
            store_split(high_ref, low_ref, cable, block, sums)
            totals_ref[pl.ds(block * cables + cable, 1), :] = sums[-1][SUBLANES - 1 :, :]

    def cable_step(cable, accumulated):
        for copy in copies(cable):
            copy.wait()

        def block_step(block, accumulated):
            lanes = pl.ds(pl.multiple_of(block * LANES, LANES), LANES)
            pieces = []
            for i in range(groups):
                rows = pl.ds(i * SUBLANES, SUBLANES)
                turns = wrap_ref[cable, rows, lanes].astype(jnp.float32)
                pieces.append(phase_ref[cable, rows, lanes] + two_pi * turns)
            sums = scanned(pieces)
            store_split(high_ref, low_ref, cable, block + 1, sums)
            totals_ref[pl.ds((block + 1) * cables + cable, 1), :] = sums[-1][SUBLANES - 1 :, :]
            return tuple(a + b for a, b in zip(accumulated, sums))

        return lax.fori_loop(0, blocks, block_step, accumulated, unroll=4)

    zeros = tuple(jnp.zeros((SUBLANES, LANES), jnp.float32) for _ in range(groups))
    accumulated = lax.fori_loop(0, cables, cable_step, zeros)
    lane = lax.broadcasted_iota(jnp.int32, (SUBLANES, LANES), 1)
    tile = jnp.zeros((SUBLANES, LANES), jnp.float32)
    for i, value in enumerate(accumulated):
        tile = jnp.where(lane == i, jnp.sum(value, axis=1, keepdims=True), tile)
    sums_ref[...] = tile


def filter_kernel(high_ref, low_ref, weight_ref, local_ref):
    cables, extended, time, _ = high_ref.shape
    half = LANES // 2
    lane = lax.broadcasted_iota(jnp.int32, (time, LANES), 1)

    @pl.loop(0, cables)
    def _(cable):
        weight = weight_ref[cable]
        high = high_ref[cable].reshape(extended * time, LANES)
        low = low_ref[cable].reshape(extended * time, LANES)
        product = jnp.dot(
            jnp.concatenate([high, low, high, low], axis=1),
            weight,
            preferred_element_type=jnp.float32,
        )
        previous = None
        for block in range(extended - 1):
            here = product[block * time : (block + 1) * time, :LANES]
            there = product[(block + 1) * time : (block + 2) * time, LANES:]
            rolled = pltpu.roll(here + there, half, 1)
            if block > 0:
                local_ref[cable, block - 1] = jnp.where(lane < half, previous, rolled)
            previous = rolled


def level_kernel(
    population, local_ref, weight_ref, offsets_refs, sums_ref, coupling_ref, place_ref, out_hbm,
    stage_ref, bias_ref, slope_ref, sem,
):
    cables, blocks, time, _ = local_ref.shape
    groups = time // SUBLANES
    extended = blocks + 2
    half = LANES // 2
    position, steps = place_ref[0], sums_ref.shape[0]
    is_first, is_last = place_ref[1], place_ref[2]

    own = jnp.zeros((SUBLANES, LANES), jnp.float32)
    before = jnp.zeros((SUBLANES, LANES), jnp.float32)
    for step in range(steps):
        gathered = jnp.sum(sums_ref[step], axis=0)
        own = own + jnp.where(position == step, gathered, 0.0)
        before = before + jnp.where(position > step, gathered, 0.0)
    earlier = before[SUBLANES - 1 :, groups - 1 : groups]
    common = (own + earlier) * (1.0 / population)
    columns = [
        jnp.broadcast_to(common[:, i : i + 1], (SUBLANES, LANES)) for i in range(groups)
    ]
    padded = -(-(extended + 1) // SUBLANES) * SUBLANES
    row = lax.broadcasted_iota(jnp.int32, (padded, LANES), 0)
    lane = lax.broadcasted_iota(jnp.int32, (padded, LANES), 1)
    inside_first = jnp.where((row == 0) & (is_first == 1), 0.0, 1.0)
    inside_last = jnp.where((row == extended - 2) & (is_last == 1), 0.0, 1.0)

    def merged(value):
        rolled = pltpu.roll(value, half, 1)
        return jnp.where(lane < half, rolled, pltpu.roll(rolled, padded - 1, 0))

    def cable_step(cable, carry):
        offset = None
        for ref in offsets_refs:
            value = ref[pl.ds(cable, extended, stride=cables), :]
            offset = value if offset is None else offset + value
        offset = jnp.concatenate(
            [offset, jnp.ones((padded - extended, LANES), jnp.float32)], axis=0
        )
        high = offset.astype(jnp.bfloat16)
        low = (offset - high.astype(jnp.float32)).astype(jnp.bfloat16)
        product = jnp.dot(
            jnp.concatenate([high, low, high, low], axis=1),
            weight_ref[cable],
            preferred_element_type=jnp.float32,
        )
        here, there = product[:, :LANES], product[:, LANES:]
        bias_ref[...] = merged(here + pltpu.roll(there, padded - 1, 0))
        ones_here = here[extended : extended + 1, :]
        ones_there = there[extended : extended + 1, :]
        slope_ref[...] = merged(ones_here * inside_first + ones_there * inside_last)
        scale = coupling_ref[cable]
        shifts = [scale * column for column in columns]

        def block_step(block, carry):
            lanes = pl.ds(pl.multiple_of(block * LANES, LANES), LANES)
            bias = jnp.broadcast_to(bias_ref[pl.ds(block, 1), :], (SUBLANES, LANES))
            slope = jnp.broadcast_to(slope_ref[pl.ds(block, 1), :], (SUBLANES, LANES))
            for i in range(groups):
                value = local_ref[cable, block, pl.ds(i * SUBLANES, SUBLANES), :]
                stage_ref[cable, pl.ds(i * SUBLANES, SUBLANES), lanes] = value + (
                    bias - shifts[i] * slope
                )
            return carry

        lax.fori_loop(0, blocks, block_step, 0, unroll=4)
        pltpu.make_async_copy(stage_ref.at[cable], out_hbm.at[cable], sem.at[cable]).start()
        return carry

    lax.fori_loop(0, cables, cable_step, 0)
    for cable in range(cables):
        pltpu.make_async_copy(stage_ref.at[cable], out_hbm.at[cable], sem.at[cable]).wait()


def edge_increment(phase_step, wrap_count, start):
    phase = lax.slice_in_dim(phase_step, start, start + LANES, axis=2)
    turns = lax.slice_in_dim(wrap_count, start, start + LANES, axis=2)
    return phase + two_pi * turns.astype(jnp.float32)


def shards(phase_step, wrap_count, coupling, filter_taps):
    cables, time, width = phase_step.shape
    blocks = width // LANES
    extended = blocks + 2
    groups = time // SUBLANES
    steps, places = lax.axis_size("tm"), lax.axis_size("chan")
    step, place = lax.axis_index("tm"), lax.axis_index("chan")

    forward = [(i, i + 1) for i in range(places - 1)]
    backward = [(target, source) for source, target in forward]
    left = lax.ppermute(
        edge_increment(phase_step, wrap_count, width - LANES), "chan", forward
    )
    right = lax.ppermute(edge_increment(phase_step, wrap_count, 0), "chan", backward)

    whole = pl.BlockSpec(memory_space=pltpu.VMEM)
    outside = pl.BlockSpec(memory_space=pl.ANY)
    scalars = pl.BlockSpec(memory_space=pltpu.SMEM)
    high, low, totals, sums, weight = pl.pallas_call(
        unwrap_kernel,
        out_shape=(
            pltpu.VMEM((cables, extended, time, LANES), jnp.bfloat16),
            pltpu.VMEM((cables, extended, time, LANES), jnp.bfloat16),
            jax.ShapeDtypeStruct((extended * cables, LANES), jnp.float32),
            jax.ShapeDtypeStruct((SUBLANES, LANES), jnp.float32),
            pltpu.VMEM((cables, 4 * LANES, 2 * LANES), jnp.bfloat16),
        ),
        in_specs=[outside, outside, whole, whole, whole],
        out_specs=[whole] * 5,
        scratch_shapes=[
            pltpu.VMEM((cables, time, width), jnp.float32),
            pltpu.VMEM((cables, time, width), jnp.int32),
            pltpu.SemaphoreType.DMA((2, cables)),
        ],
        compiler_params=pltpu.CompilerParams(vmem_limit_bytes=40 << 20),
        name="unwrap",
    )(phase_step, wrap_count, left, right, filter_taps)

    received = []
    running = totals
    reach = 1
    while reach < steps:
        later = [(i, i + reach) for i in range(steps - reach)]
        received.append(lax.ppermute(running, "tm", later))
        running = running + received[-1]
        reach *= 2

    copies = jnp.broadcast_to(sums[None], (steps * places, SUBLANES, LANES))
    gathered = lax.all_to_all(copies, ("tm", "chan"), 0, 0, tiled=True)
    gathered = gathered.reshape(steps, places, SUBLANES, LANES)

    local = pl.pallas_call(
        filter_kernel,
        out_shape=pltpu.VMEM((cables, blocks, time, LANES), jnp.float32),
        in_specs=[whole] * 3,
        out_specs=whole,
        compiler_params=pltpu.CompilerParams(vmem_limit_bytes=24 << 20),
        cost_estimate=pl.CostEstimate(
            flops=2 * cables * extended * time * 512 * 256, bytes_accessed=1 << 20, transcendentals=0
        ),
        name="filter",
    )(high, low, weight)

    marks = jnp.stack([step, (place == 0).astype(jnp.int32), (place == places - 1).astype(jnp.int32)])
    population = cables * width * places
    return pl.pallas_call(
        functools.partial(level_kernel, population),
        out_shape=jax.ShapeDtypeStruct(phase_step.shape, jnp.float32),
        in_specs=[whole, whole, [whole] * len(received), whole, scalars, scalars],
        out_specs=outside,
        scratch_shapes=[
            pltpu.VMEM((cables, time, width), jnp.float32),
            pltpu.VMEM((-(-(extended + 1) // SUBLANES) * SUBLANES, LANES), jnp.float32),
            pltpu.VMEM((-(-(extended + 1) // SUBLANES) * SUBLANES, LANES), jnp.float32),
            pltpu.SemaphoreType.DMA((cables,)),
        ],
        compiler_params=pltpu.CompilerParams(vmem_limit_bytes=24 << 20),
        name="level",
    )(local, weight, received, gathered, coupling, marks)


def solution(mesh):
    placed = (P(None, "tm", "chan"), P(None, "tm", "chan"), P(), P())
    return jax.shard_map(
        shards, mesh=mesh, in_specs=placed, out_specs=P(None, "tm", "chan"), check_vma=False
    )
```

```python
import functools
import math

import jax
import jax.numpy as jnp
from jax import lax
from jax.experimental import pallas as pl
from jax.experimental.pallas import tpu as pltpu
from jax.sharding import PartitionSpec as P

two_pi = 2.0 * math.pi
LANES = 128
SUBLANES = 8


def shifted_down(value, amount):
    rows = lax.broadcasted_iota(jnp.int32, value.shape, 0)
    return jnp.where(rows >= amount, pltpu.roll(value, amount, 0), 0.0)


def scanned(pieces):
    sums, carry = [], None
    for value in pieces:
        amount = 1
        while amount < SUBLANES:
            value = value + shifted_down(value, amount)
            amount *= 2
        if carry is not None:
            value = value + carry
        carry = jnp.broadcast_to(value[SUBLANES - 1 :, :], value.shape)
        sums.append(value)
    return sums


def store_split(high_ref, low_ref, cable, block, sums):
    for pair in range(0, len(sums), 2):
        both = jnp.concatenate(sums[pair : pair + 2], axis=0)
        high = both.astype(jnp.bfloat16)
        low = (both - high.astype(jnp.float32)).astype(jnp.bfloat16)
        rows = pl.ds(pair * SUBLANES, 2 * SUBLANES)
        high_ref[cable, block, rows, :] = high
        low_ref[cable, block, rows, :] = low


def edges_kernel(phase_hbm, wrap_hbm, inner_ref, outer_ref, phase_ref, wrap_ref, sem):
    width = phase_hbm.shape[2]
    is_even = lax.rem(lax.axis_index("chan"), 2) == 0
    lowest = 0
    highest = width - LANES
    starts = (jnp.where(is_even, highest, lowest), jnp.where(is_even, lowest, highest))
    copies = []
    for side, start in enumerate(starts):
        lanes = pl.ds(pl.multiple_of(start, LANES), LANES)
        for kind, (source, target) in enumerate(((phase_hbm, phase_ref), (wrap_hbm, wrap_ref))):
            copies.append(
                pltpu.make_async_copy(source.at[:, :, lanes], target.at[side], sem.at[kind, side])
            )
    for copy in copies:
        copy.start()
    for copy in copies:
        copy.wait()
    for side, target in enumerate((inner_ref, outer_ref)):
        target[...] = phase_ref[side] + two_pi * wrap_ref[side].astype(jnp.float32)


def unwrap_kernel(
    phase_hbm, wrap_hbm, inner_ref, outer_ref, taps_ref,
    high_ref, low_ref, totals_ref, sums_ref, weight_ref,
    phase_ref, wrap_ref, sem,
):
    cables, time, width = phase_hbm.shape
    blocks = width // LANES
    groups = time // SUBLANES

    def copies(cable):
        return (
            pltpu.make_async_copy(phase_hbm.at[cable], phase_ref.at[cable], sem.at[0, cable]),
            pltpu.make_async_copy(wrap_hbm.at[cable], wrap_ref.at[cable], sem.at[1, cable]),
        )

    for cable in range(cables):
        for copy in copies(cable):
            copy.start()

    is_even = lax.rem(lax.axis_index("chan"), 2) == 0
    outputs = lax.broadcasted_iota(jnp.int32, (LANES, LANES), 0)
    inputs = lax.broadcasted_iota(jnp.int32, (LANES, LANES), 1)
    centre = (lax.broadcasted_iota(jnp.int32, (1, LANES), 1) == LANES // 2).astype(jnp.float32)

    @pl.loop(0, cables)
    def _(cable):
        row = (centre - taps_ref[pl.ds(cable, 1), :]) * (1.0 / (4.0 * two_pi))
        circulant = pltpu.roll(
            jnp.broadcast_to(row, (LANES, LANES)), 0, 1, stride=1, stride_axis=0
        )
        first = jnp.where(inputs >= outputs, circulant, 0.0).T
        second = jnp.where(inputs < outputs, circulant, 0.0).T
        band = jnp.concatenate([first, second], axis=1)
        high = band.astype(jnp.bfloat16)
        low = (band - high.astype(jnp.float32)).astype(jnp.bfloat16)
        for place, part in enumerate((high, high, low, low)):
            weight_ref[cable, pl.ds(place * LANES, LANES), :] = part
        for flip, block in ((is_even, 0), (jnp.logical_not(is_even), blocks + 1)):
            pieces = []
            for i in range(groups):
                rows = pl.ds(i * SUBLANES, SUBLANES)
                pieces.append(
                    jnp.where(flip, outer_ref[cable, rows, :], inner_ref[cable, rows, :])
                )
            sums = scanned(pieces)
            store_split(high_ref, low_ref, cable, block, sums)
            totals_ref[pl.ds(block * cables + cable, 1), :] = sums[-1][SUBLANES - 1 :, :]

    def cable_step(cable, accumulated):
        for copy in copies(cable):
            copy.wait()

        def block_step(block, accumulated):
            lanes = pl.ds(pl.multiple_of(block * LANES, LANES), LANES)
            pieces = []
            for i in range(groups):
                rows = pl.ds(i * SUBLANES, SUBLANES)
                turns = wrap_ref[cable, rows, lanes].astype(jnp.float32)
                pieces.append(phase_ref[cable, rows, lanes] + two_pi * turns)
            sums = scanned(pieces)
            store_split(high_ref, low_ref, cable, block + 1, sums)
            totals_ref[pl.ds((block + 1) * cables + cable, 1), :] = sums[-1][SUBLANES - 1 :, :]
            return tuple(a + b for a, b in zip(accumulated, sums))

        return lax.fori_loop(0, blocks, block_step, accumulated, unroll=4)

    zeros = tuple(jnp.zeros((SUBLANES, LANES), jnp.float32) for _ in range(groups))
    accumulated = lax.fori_loop(0, cables, cable_step, zeros)
    lane = lax.broadcasted_iota(jnp.int32, (SUBLANES, LANES), 1)
    tile = jnp.zeros((SUBLANES, LANES), jnp.float32)
    for i, value in enumerate(accumulated):
        tile = jnp.where(lane == i, jnp.sum(value, axis=1, keepdims=True), tile)
    sums_ref[...] = tile


def filter_kernel(high_ref, low_ref, weight_ref, local_ref):
    cables, extended, time, _ = high_ref.shape
    half = LANES // 2
    lane = lax.broadcasted_iota(jnp.int32, (time, LANES), 1)

    @pl.loop(0, cables)
    def _(cable):
        weight = weight_ref[cable]
        high = high_ref[cable].reshape(extended * time, LANES)
        low = low_ref[cable].reshape(extended * time, LANES)
        product = jnp.dot(
            jnp.concatenate([high, low, high, low], axis=1),
            weight,
            preferred_element_type=jnp.float32,
        )
        previous = None
        for block in range(extended - 1):
            here = product[block * time : (block + 1) * time, :LANES]
            there = product[(block + 1) * time : (block + 2) * time, LANES:]
            rolled = pltpu.roll(here + there, half, 1)
            if block > 0:
                local_ref[cable, block - 1] = jnp.where(lane < half, previous, rolled)
            previous = rolled


def level_kernel(
    population, local_ref, weight_ref, swapped_refs, sums_ref, coupling_ref,
    out_hbm, stage_ref, offset_ref, bias_ref, slope_ref, sem,
):
    cables, blocks, time, _ = local_ref.shape
    groups = time // SUBLANES
    extended = blocks + 2
    half = LANES // 2
    step, place = lax.axis_index("tm"), lax.axis_index("chan")
    is_first = place == 0
    is_last = place == lax.axis_size("chan") - 1

    offset = jnp.zeros(offset_ref.shape, jnp.float32)
    for bit, ref in enumerate(swapped_refs):
        offset = offset + jnp.where((step & (1 << bit)) != 0, ref[...], 0.0)
    offset_ref[...] = offset
    earlier = offset[extended * cables + SUBLANES - 1 :, groups - 1 : groups]
    common = (sums_ref[...] + earlier) * (1.0 / population)
    columns = [
        jnp.broadcast_to(common[:, i : i + 1], (SUBLANES, LANES)) for i in range(groups)
    ]
    padded = -(-(extended + 1) // SUBLANES) * SUBLANES
    row = lax.broadcasted_iota(jnp.int32, (padded, LANES), 0)
    lane = lax.broadcasted_iota(jnp.int32, (padded, LANES), 1)
    inside_first = jnp.where((row == 0) & is_first, 0.0, 1.0)
    inside_last = jnp.where((row == extended - 2) & is_last, 0.0, 1.0)

    def merged(value):
        rolled = pltpu.roll(value, half, 1)
        return jnp.where(lane < half, rolled, pltpu.roll(rolled, padded - 1, 0))

    def cable_step(cable, carry):
        offset = offset_ref[pl.ds(cable, extended, stride=cables), :]
        offset = jnp.concatenate(
            [offset, jnp.ones((padded - extended, LANES), jnp.float32)], axis=0
        )
        high = offset.astype(jnp.bfloat16)
        low = (offset - high.astype(jnp.float32)).astype(jnp.bfloat16)
        product = jnp.dot(
            jnp.concatenate([high, low, high, low], axis=1),
            weight_ref[cable],
            preferred_element_type=jnp.float32,
        )
        here, there = product[:, :LANES], product[:, LANES:]
        bias_ref[...] = merged(here + pltpu.roll(there, padded - 1, 0))
        ones_here = here[extended : extended + 1, :]
        ones_there = there[extended : extended + 1, :]
        slope_ref[...] = merged(ones_here * inside_first + ones_there * inside_last)
        scale = coupling_ref[cable]
        shifts = [scale * column for column in columns]

        def block_step(block, carry):
            lanes = pl.ds(pl.multiple_of(block * LANES, LANES), LANES)
            bias = jnp.broadcast_to(bias_ref[pl.ds(block, 1), :], (SUBLANES, LANES))
            slope = jnp.broadcast_to(slope_ref[pl.ds(block, 1), :], (SUBLANES, LANES))
            for i in range(groups):
                value = local_ref[cable, block, pl.ds(i * SUBLANES, SUBLANES), :]
                stage_ref[cable, pl.ds(i * SUBLANES, SUBLANES), lanes] = value + (
                    bias - shifts[i] * slope
                )
            return carry

        lax.fori_loop(0, blocks, block_step, 0, unroll=4)
        pltpu.make_async_copy(stage_ref.at[cable], out_hbm.at[cable], sem.at[cable]).start()
        return carry

    lax.fori_loop(0, cables, cable_step, 0)
    for cable in range(cables):
        pltpu.make_async_copy(stage_ref.at[cable], out_hbm.at[cable], sem.at[cable]).wait()


def swapped(value, axis, bit):
    return lax.ppermute(value, axis, [(i, i ^ bit) for i in range(lax.axis_size(axis))])


def shards(phase_step, wrap_count, coupling, filter_taps):
    cables, time, width = phase_step.shape
    blocks = width // LANES
    extended = blocks + 2
    phase_step = pltpu.with_memory_space_constraint(phase_step, pltpu.HBM)
    wrap_count = pltpu.with_memory_space_constraint(wrap_count, pltpu.HBM)
    steps, places = lax.axis_size("tm"), lax.axis_size("chan")

    whole = pl.BlockSpec(memory_space=pltpu.VMEM)
    outside = pl.BlockSpec(memory_space=pl.ANY)
    scalars = pl.BlockSpec(memory_space=pltpu.SMEM)
    inner, outer = pl.pallas_call(
        edges_kernel,
        out_shape=[pltpu.VMEM((cables, time, LANES), jnp.float32)] * 2,
        in_specs=[outside] * 2,
        out_specs=[whole] * 2,
        scratch_shapes=[
            pltpu.VMEM((2, cables, time, LANES), jnp.float32),
            pltpu.VMEM((2, cables, time, LANES), jnp.int32),
            pltpu.SemaphoreType.DMA((2, 2)),
        ],
        compiler_params=pltpu.CompilerParams(vmem_limit_bytes=8 << 20),
        name="edges",
    )(phase_step, wrap_count)
    inner = swapped(inner, "chan", 1)
    outer = lax.ppermute(
        outer,
        "chan",
        [(i, i + 1) for i in range(1, places - 1, 2)] + [(i + 1, i) for i in range(1, places - 1, 2)],
    )

    high, low, totals, sums, weight = pl.pallas_call(
        unwrap_kernel,
        out_shape=(
            pltpu.VMEM((cables, extended, time, LANES), jnp.bfloat16),
            pltpu.VMEM((cables, extended, time, LANES), jnp.bfloat16),
            jax.ShapeDtypeStruct((extended * cables, LANES), jnp.float32),
            jax.ShapeDtypeStruct((SUBLANES, LANES), jnp.float32),
            pltpu.VMEM((cables, 4 * LANES, 2 * LANES), jnp.bfloat16),
        ),
        in_specs=[outside, outside, whole, whole, whole],
        out_specs=[whole] * 5,
        scratch_shapes=[
            pltpu.VMEM((cables, time, width), jnp.float32),
            pltpu.VMEM((cables, time, width), jnp.int32),
            pltpu.SemaphoreType.DMA((2, cables)),
        ],
        compiler_params=pltpu.CompilerParams(vmem_limit_bytes=40 << 20),
        name="unwrap",
    )(phase_step, wrap_count, inner, outer, filter_taps)

    for bit in range(places.bit_length() - 1):
        sums = sums + swapped(sums, "chan", 1 << bit)
    received = []
    running = jnp.concatenate([totals, sums], axis=0)
    for bit in range(steps.bit_length() - 1):
        received.append(swapped(running, "tm", 1 << bit))
        running = running + received[-1]

    local = pl.pallas_call(
        filter_kernel,
        out_shape=pltpu.VMEM((cables, blocks, time, LANES), jnp.float32),
        in_specs=[whole] * 3,
        out_specs=whole,
        compiler_params=pltpu.CompilerParams(vmem_limit_bytes=24 << 20),
        cost_estimate=pl.CostEstimate(
            flops=2 * cables * extended * time * 512 * 256, bytes_accessed=1 << 20, transcendentals=0
        ),
        name="filter",
    )(high, low, weight)

    population = cables * width * places
    return pl.pallas_call(
        functools.partial(level_kernel, population),
        out_shape=jax.ShapeDtypeStruct(phase_step.shape, jnp.float32),
        in_specs=[whole, whole, [whole] * len(received), whole, scalars],
        out_specs=outside,
        scratch_shapes=[
            pltpu.VMEM((cables, time, width), jnp.float32),
            pltpu.VMEM((extended * cables + SUBLANES, LANES), jnp.float32),
            pltpu.VMEM((-(-(extended + 1) // SUBLANES) * SUBLANES, LANES), jnp.float32),
            pltpu.VMEM((-(-(extended + 1) // SUBLANES) * SUBLANES, LANES), jnp.float32),
            pltpu.SemaphoreType.DMA((cables,)),
        ],
        compiler_params=pltpu.CompilerParams(vmem_limit_bytes=24 << 20),
        name="level",
    )(local, weight, received, sums, coupling)


def solution(mesh):
    placed = (P(None, "tm", "chan"), P(None, "tm", "chan"), P(), P())
    return jax.shard_map(
        shards, mesh=mesh, in_specs=placed, out_specs=P(None, "tm", "chan"), check_vma=False
    )
```

```python
import functools
import math

import jax
import jax.numpy as jnp
from jax import lax
from jax.experimental import pallas as pl
from jax.experimental.pallas import tpu as pltpu
from jax.sharding import PartitionSpec as P

two_pi = 2.0 * math.pi
LANES = 128
HALF = LANES // 2
SUBLANES = 8


def shifted_down(value, amount):
    rows = lax.broadcasted_iota(jnp.int32, value.shape, 0)
    return jnp.where(rows >= amount, pltpu.roll(value, amount, 0), 0.0)


def scanned(pieces):
    sums, carry = [], None
    for value in pieces:
        amount = 1
        while amount < SUBLANES:
            value = value + shifted_down(value, amount)
            amount *= 2
        if carry is not None:
            value = value + carry
        carry = jnp.broadcast_to(value[SUBLANES - 1 :, :], value.shape)
        sums.append(value)
    return sums


def split(value):
    high = value.astype(jnp.bfloat16)
    return high, (value - high.astype(jnp.float32)).astype(jnp.bfloat16)


def store_split(high_ref, low_ref, cable, block, sums):
    for pair in range(0, len(sums), 2):
        rows = pl.ds(pair * SUBLANES, 2 * SUBLANES)
        high, low = split(jnp.concatenate(sums[pair : pair + 2], axis=0))
        high_ref[cable, block, rows, :] = high
        low_ref[cable, block, rows, :] = low


def edges_kernel(phase_hbm, wrap_hbm, inner_ref, outer_ref, phase_ref, wrap_ref, sem):
    cables, time, width = phase_hbm.shape
    is_even = lax.rem(lax.axis_index("chan"), 2) == 0
    sends_last = (is_even, jnp.logical_not(is_even))
    copies = []
    for side, last in enumerate(sends_last):
        lanes = pl.ds(pl.multiple_of(jnp.where(last, width - LANES, 0), LANES), LANES)
        for kind, (source, target) in enumerate(((phase_hbm, phase_ref), (wrap_hbm, wrap_ref))):
            copies.append(
                pltpu.make_async_copy(source.at[:, :, lanes], target.at[side], sem.at[kind, side])
            )
    for copy in copies:
        copy.start()
    for copy in copies:
        copy.wait()
    lane = lax.broadcasted_iota(jnp.int32, (time, LANES), 1)
    for side, (last, target) in enumerate(zip(sends_last, (inner_ref, outer_ref))):
        for cable in range(cables // 2):
            low, high = (
                phase_ref[side, c] + two_pi * wrap_ref[side, c].astype(jnp.float32)
                for c in (cable, cable + cables // 2)
            )
            low = jnp.where(last, pltpu.roll(low, HALF, 1), low)
            high = jnp.where(last, high, pltpu.roll(high, HALF, 1))
            target[cable] = jnp.where(lane < HALF, low, high)


def unwrap_kernel(
    phase_hbm, wrap_hbm, taps_ref,
    high_ref, low_ref, totals_ref, sums_ref, weight_ref,
    phase_ref, wrap_ref, sem,
):
    cables, time, width = phase_hbm.shape
    blocks = width // LANES
    groups = time // SUBLANES

    def copies(cable):
        return (
            pltpu.make_async_copy(phase_hbm.at[cable], phase_ref.at[cable], sem.at[0, cable]),
            pltpu.make_async_copy(wrap_hbm.at[cable], wrap_ref.at[cable], sem.at[1, cable]),
        )

    for cable in range(cables):
        for copy in copies(cable):
            copy.start()

    outputs = lax.broadcasted_iota(jnp.int32, (LANES, LANES), 0)
    inputs = lax.broadcasted_iota(jnp.int32, (LANES, LANES), 1)
    centre = (lax.broadcasted_iota(jnp.int32, (1, LANES), 1) == HALF).astype(jnp.float32)

    @pl.loop(0, cables)
    def _(cable):
        row = (centre - taps_ref[pl.ds(cable, 1), :]) * (1.0 / (4.0 * two_pi))
        circulant = pltpu.roll(
            jnp.broadcast_to(row, (LANES, LANES)), 0, 1, stride=1, stride_axis=0
        )
        first = jnp.where(inputs >= outputs, circulant, 0.0).T
        second = jnp.where(inputs < outputs, circulant, 0.0).T
        high, low = split(jnp.concatenate([first, second], axis=1))
        for place, part in enumerate((high, high, low, low)):
            weight_ref[cable, pl.ds(place * LANES, LANES), :] = part

    def cable_step(cable, accumulated):
        for copy in copies(cable):
            copy.wait()

        def block_step(block, accumulated):
            lanes = pl.ds(pl.multiple_of(block * LANES, LANES), LANES)
            pieces = []
            for i in range(groups):
                rows = pl.ds(i * SUBLANES, SUBLANES)
                turns = wrap_ref[cable, rows, lanes].astype(jnp.float32)
                pieces.append(phase_ref[cable, rows, lanes] + two_pi * turns)
            sums = scanned(pieces)
            store_split(high_ref, low_ref, cable, block, sums)
            totals_ref[pl.ds(block * cables + cable, 1), :] = sums[-1][SUBLANES - 1 :, :]
            return tuple(a + b for a, b in zip(accumulated, sums))

        return lax.fori_loop(0, blocks, block_step, accumulated, unroll=4)

    zeros = tuple(jnp.zeros((SUBLANES, LANES), jnp.float32) for _ in range(groups))
    accumulated = lax.fori_loop(0, cables, cable_step, zeros)
    lane = lax.broadcasted_iota(jnp.int32, (SUBLANES, LANES), 1)
    tile = jnp.zeros((SUBLANES, LANES), jnp.float32)
    for i, value in enumerate(accumulated):
        tile = jnp.where(lane == i, jnp.sum(value, axis=1, keepdims=True), tile)
    sums_ref[...] = tile


def halo_kernel(inner_ref, outer_ref, high_ref, low_ref, totals_ref):
    pairs, time, _ = inner_ref.shape
    cables = 2 * pairs
    groups = time // SUBLANES
    is_even = lax.rem(lax.axis_index("chan"), 2) == 0
    for pair in range(pairs):
        inner, outer = (
            scanned([ref[pair, pl.ds(i * SUBLANES, SUBLANES), :] for i in range(groups)])
            for ref in (inner_ref, outer_ref)
        )
        right = [jnp.where(is_even, a, b) for a, b in zip(inner, outer)]
        left = [jnp.where(is_even, b, a) for a, b in zip(inner, outer)]
        for block, sums, moved in ((0, right, pair + pairs), (1, left, pair)):
            for cable in (pair, pair + pairs):
                placed = [pltpu.roll(v, HALF, 1) for v in sums] if cable == moved else sums
                store_split(high_ref, low_ref, cable, block, placed)
                totals_ref[pl.ds(block * cables + cable, 1), :] = placed[-1][SUBLANES - 1 :, :]


def filter_kernel(first, high_ref, low_ref, halo_high_ref, halo_low_ref, weight_ref, local_ref):
    _, blocks, time, _ = high_ref.shape
    lane = lax.broadcasted_iota(jnp.int32, (time, LANES), 1)

    @pl.loop(0, local_ref.shape[0])
    def _(index):
        cable = first + index
        high, low = (
            jnp.concatenate(
                [main[cable].reshape(blocks * time, LANES), halo[cable].reshape(2 * time, LANES)],
                axis=0,
            )
            for main, halo in ((high_ref, halo_high_ref), (low_ref, halo_low_ref))
        )
        product = jnp.dot(
            jnp.concatenate([high, low, high, low], axis=1),
            weight_ref[cable],
            preferred_element_type=jnp.float32,
        )

        def rolled(block):
            here = block if block >= 0 else blocks + 1
            there = block + 1
            return pltpu.roll(
                product[here * time : (here + 1) * time, :LANES]
                + product[there * time : (there + 1) * time, LANES:],
                HALF,
                1,
            )

        previous = rolled(-1)
        for block in range(blocks):
            following = rolled(block)
            local_ref[index, block] = jnp.where(lane < HALF, previous, following)
            previous = following


def level_kernel(
    population, local_refs, weight_ref, totals_refs, sums_ref, earlier_refs, coupling_ref,
    out_hbm, stage_ref, offset_ref, sem,
):
    share, blocks, time, _ = local_refs[0].shape
    cables = out_hbm.shape[0]
    groups = time // SUBLANES
    step, place = lax.axis_index("tm"), lax.axis_index("chan")
    inside_left = jnp.where(place == 0, 0.0, 1.0)
    inside_right = jnp.where(place == lax.axis_size("chan") - 1, 0.0, 1.0)

    def from_earlier(refs):
        value = jnp.zeros(refs[0].shape, jnp.float32)
        for bit, ref in enumerate(refs):
            value = value + jnp.where((step & (1 << bit)) != 0, ref[...], 0.0)
        return value

    offset_ref[...] = from_earlier(totals_refs)
    earlier = from_earlier(earlier_refs)[SUBLANES - 1 :, groups - 1 : groups]
    common = (sums_ref[...] + earlier) * (1.0 / population)
    columns = [
        jnp.broadcast_to(common[:, i : i + 1], (SUBLANES, LANES)) for i in range(groups)
    ]
    used = blocks + 2
    padded = -(-(used + 1) // SUBLANES) * SUBLANES
    row = lax.broadcasted_iota(jnp.int32, (padded, LANES), 0)
    lane = lax.broadcasted_iota(jnp.int32, (padded, LANES), 1)

    def filtered_offset(cable):
        offset = jnp.concatenate(
            [
                offset_ref[pl.ds(cable, used, stride=cables), :],
                jnp.ones((padded - used, LANES), jnp.float32),
            ],
            axis=0,
        )
        high, low = split(offset)
        product = jnp.dot(
            jnp.concatenate([high, low, high, low], axis=1),
            weight_ref[cable],
            preferred_element_type=jnp.float32,
        )
        here, there = product[:, :LANES], product[:, LANES:]
        left = pltpu.roll(here[used - 1 : used] + there[:1], HALF, 1)
        following = pltpu.roll(here + pltpu.roll(there, padded - 1, 0), HALF, 1)
        previous = jnp.where(row == 0, left, pltpu.roll(following, 1, 0))
        bias = jnp.where(lane < HALF, previous, following)
        here, there = here[used : used + 1], there[used : used + 1]
        middle = pltpu.roll(here + there, HALF, 1)
        first = pltpu.roll(here * inside_left + there, HALF, 1)
        last = pltpu.roll(here + there * inside_right, HALF, 1)
        first = jnp.where(lane[:1] < HALF, first, middle)
        last = jnp.where(lane[:1] < HALF, middle, last)
        return bias, first, middle, last

    carry = filtered_offset(0)
    for part, local_ref in enumerate(local_refs):

        def cable_step(index, carry, part=part, local_ref=local_ref):
            cable = part * share + index
            following = filtered_offset(jnp.minimum(cable + 1, cables - 1))
            bias, first, middle, last = carry
            shifts = [coupling_ref[cable] * column for column in columns]
            inner = [shift * middle for shift in shifts]
            for block in range(blocks):
                lanes = pl.ds(block * LANES, LANES)
                added = jnp.broadcast_to(bias[block : block + 1, :], (SUBLANES, LANES))
                if block == 0:
                    slopes = [shift * first for shift in shifts]
                elif block == blocks - 1:
                    slopes = [shift * last for shift in shifts]
                else:
                    slopes = inner
                for i in range(groups):
                    rows = pl.ds(i * SUBLANES, SUBLANES)
                    stage_ref[cable, rows, lanes] = local_ref[index, block, rows, :] + (
                        added - slopes[i]
                    )
            pltpu.make_async_copy(stage_ref.at[cable], out_hbm.at[cable], sem.at[cable]).start()
            return following

        carry = lax.fori_loop(0, share, cable_step, carry)
    for cable in range(cables):
        pltpu.make_async_copy(stage_ref.at[cable], out_hbm.at[cable], sem.at[cable]).wait()


def swapped(value, axis, bit):
    return lax.ppermute(value, axis, [(i, i ^ bit) for i in range(lax.axis_size(axis))])


def shards(phase_step, wrap_count, coupling, filter_taps):
    cables, time, width = phase_step.shape
    blocks = width // LANES
    steps, places = lax.axis_size("tm"), lax.axis_size("chan")
    population = cables * width * places
    parts = 4
    share = cables // parts
    phase_step = pltpu.with_memory_space_constraint(phase_step, pltpu.HBM)
    wrap_count = pltpu.with_memory_space_constraint(wrap_count, pltpu.HBM)
    whole = pl.BlockSpec(memory_space=pltpu.VMEM)
    outside = pl.BlockSpec(memory_space=pl.ANY)
    scalars = pl.BlockSpec(memory_space=pltpu.SMEM)

    inner, outer = pl.pallas_call(
        edges_kernel,
        out_shape=[pltpu.VMEM((cables // 2, time, LANES), jnp.float32)] * 2,
        in_specs=[outside] * 2,
        out_specs=[whole] * 2,
        scratch_shapes=[
            pltpu.VMEM((2, cables, time, LANES), jnp.float32),
            pltpu.VMEM((2, cables, time, LANES), jnp.int32),
            pltpu.SemaphoreType.DMA((2, 2)),
        ],
        compiler_params=pltpu.CompilerParams(vmem_limit_bytes=8 << 20),
        name="edges",
    )(phase_step, wrap_count)
    odd_pairs = [(i, i + 1) for i in range(1, places - 1, 2)]
    outer = lax.ppermute(outer, "chan", odd_pairs + [(b, a) for a, b in odd_pairs])
    inner = swapped(inner, "chan", 1)

    high, low, totals, sums, weight = pl.pallas_call(
        unwrap_kernel,
        out_shape=(
            pltpu.VMEM((cables, blocks, time, LANES), jnp.bfloat16),
            pltpu.VMEM((cables, blocks, time, LANES), jnp.bfloat16),
            pltpu.VMEM((blocks * cables, LANES), jnp.float32),
            pltpu.VMEM((SUBLANES, LANES), jnp.float32),
            pltpu.VMEM((cables, 4 * LANES, 2 * LANES), jnp.bfloat16),
        ),
        in_specs=[outside, outside, whole],
        out_specs=[whole] * 5,
        scratch_shapes=[
            pltpu.VMEM((cables, time, width), jnp.float32),
            pltpu.VMEM((cables, time, width), jnp.int32),
            pltpu.SemaphoreType.DMA((2, cables)),
        ],
        compiler_params=pltpu.CompilerParams(vmem_limit_bytes=40 << 20),
        cost_estimate=pl.CostEstimate(
            flops=0, bytes_accessed=2 * phase_step.size * 4, transcendentals=0
        ),
        name="unwrap",
    )(phase_step, wrap_count, filter_taps)

    halo_high, halo_low, halo_totals = pl.pallas_call(
        halo_kernel,
        out_shape=(
            pltpu.VMEM((cables, 2, time, LANES), jnp.bfloat16),
            pltpu.VMEM((cables, 2, time, LANES), jnp.bfloat16),
            pltpu.VMEM((2 * cables, LANES), jnp.float32),
        ),
        in_specs=[whole] * 2,
        out_specs=[whole] * 3,
        compiler_params=pltpu.CompilerParams(vmem_limit_bytes=8 << 20),
        name="halo",
    )(inner, outer)

    def filtered(part, weight):
        return pl.pallas_call(
            functools.partial(filter_kernel, part * share),
            out_shape=pltpu.VMEM((share, blocks, time, LANES), jnp.float32),
            in_specs=[whole] * 5,
            out_specs=whole,
            compiler_params=pltpu.CompilerParams(vmem_limit_bytes=16 << 20),
            cost_estimate=pl.CostEstimate(
                flops=2 * share * (blocks + 2) * time * 8 * LANES * LANES,
                bytes_accessed=1 << 20,
                transcendentals=0,
            ),
            name="filter",
        )(high, low, halo_high, halo_low, weight)

    running = jnp.concatenate([totals, halo_totals], axis=0)
    received = [swapped(running, "tm", 1)]
    sums, halo_totals = lax.optimization_barrier((sums, halo_totals))
    rounds = [("chan", 1 << bit) for bit in range(places.bit_length() - 1)]
    rounds += [("tm", 1 << bit) for bit in range(steps.bit_length() - 1)]
    local, received_sums, chan_sums, mark = [], [], sums, sums
    for number, (axis, bit) in enumerate(rounds):
        incoming = swapped(sums, axis, bit)
        if len(local) < parts:
            tied, mark = lax.optimization_barrier((weight, mark))
            part = filtered(len(local), tied)
            incoming, part = lax.optimization_barrier((incoming, part))
            local.append(part)
        if number % 2 == 1 and 1 << len(received) < steps:
            running = running + received[-1]
            running, incoming = lax.optimization_barrier((running, incoming))
            received.append(swapped(running, "tm", 1 << len(received)))
        if axis == "tm":
            received_sums.append(incoming)
        sums = mark = sums + incoming
        if axis == "chan":
            chan_sums = sums
    while len(local) < parts:
        local.append(filtered(len(local), weight))

    return pl.pallas_call(
        functools.partial(level_kernel, population),
        out_shape=jax.ShapeDtypeStruct(phase_step.shape, jnp.float32),
        in_specs=[
            [whole] * parts, whole, [whole] * len(received), whole, [whole] * len(received), scalars
        ],
        out_specs=outside,
        scratch_shapes=[
            pltpu.VMEM((cables, time, width), jnp.float32),
            pltpu.VMEM(((blocks + 2) * cables, LANES), jnp.float32),
            pltpu.SemaphoreType.DMA((cables,)),
        ],
        compiler_params=pltpu.CompilerParams(vmem_limit_bytes=24 << 20),
        name="level",
    )(local, weight, received, chan_sums, received_sums, coupling)


def solution(mesh):
    placed = (P(None, "tm", "chan"), P(None, "tm", "chan"), P(), P())
    return jax.shard_map(
        shards, mesh=mesh, in_specs=placed, out_specs=P(None, "tm", "chan"), check_vma=False
    )
```

```python
import functools
import math

import jax
import jax.numpy as jnp
from jax import lax
from jax.experimental import pallas as pl
from jax.experimental.pallas import tpu as pltpu
from jax.sharding import PartitionSpec as P

two_pi = 2.0 * math.pi
LANES = 128
HALF = LANES // 2
SUBLANES = 8


def shifted_down(value, amount):
    rows = lax.broadcasted_iota(jnp.int32, value.shape, 0)
    return jnp.where(rows >= amount, pltpu.roll(value, amount, 0), 0.0)


def scanned(pieces):
    sums, carry = [], None
    for value in pieces:
        amount = 1
        while amount < SUBLANES:
            value = value + shifted_down(value, amount)
            amount *= 2
        if carry is not None:
            value = value + carry
        carry = jnp.broadcast_to(value[SUBLANES - 1 :, :], value.shape)
        sums.append(value)
    return sums


def split(value):
    high = value.astype(jnp.bfloat16)
    return high, (value - high.astype(jnp.float32)).astype(jnp.bfloat16)


def store_split(high_ref, low_ref, cable, block, sums):
    for pair in range(0, len(sums), 2):
        rows = pl.ds(pair * SUBLANES, 2 * SUBLANES)
        high, low = split(jnp.concatenate(sums[pair : pair + 2], axis=0))
        high_ref[cable, block, rows, :] = high
        low_ref[cable, block, rows, :] = low


def edges_kernel(phase_hbm, wrap_hbm, inner_ref, outer_ref, phase_ref, wrap_ref, sem):
    cables, time, width = phase_hbm.shape
    is_even = lax.rem(lax.axis_index("chan"), 2) == 0
    sends_last = (is_even, jnp.logical_not(is_even))
    copies = []
    for side, last in enumerate(sends_last):
        lanes = pl.ds(pl.multiple_of(jnp.where(last, width - LANES, 0), LANES), LANES)
        for kind, (source, target) in enumerate(((phase_hbm, phase_ref), (wrap_hbm, wrap_ref))):
            copies.append(
                pltpu.make_async_copy(source.at[:, :, lanes], target.at[side], sem.at[kind, side])
            )
    for copy in copies:
        copy.start()
    for copy in copies:
        copy.wait()
    lane = lax.broadcasted_iota(jnp.int32, (time, LANES), 1)
    for side, (last, target) in enumerate(zip(sends_last, (inner_ref, outer_ref))):
        for cable in range(cables // 2):
            low, high = (
                phase_ref[side, c] + two_pi * wrap_ref[side, c].astype(jnp.float32)
                for c in (cable, cable + cables // 2)
            )
            low = jnp.where(last, pltpu.roll(low, HALF, 1), low)
            high = jnp.where(last, high, pltpu.roll(high, HALF, 1))
            target[cable] = jnp.where(lane < HALF, low, high)


def unwrap_kernel(
    phase_hbm, wrap_hbm, taps_ref,
    high_ref, low_ref, totals_ref, sums_ref, weight_ref,
    phase_ref, wrap_ref, sem,
):
    cables, time, width = phase_hbm.shape
    blocks = width // LANES
    groups = time // SUBLANES

    def copies(cable):
        return (
            pltpu.make_async_copy(phase_hbm.at[cable], phase_ref.at[cable], sem.at[0, cable]),
            pltpu.make_async_copy(wrap_hbm.at[cable], wrap_ref.at[cable], sem.at[1, cable]),
        )

    for cable in range(cables):
        for copy in copies(cable):
            copy.start()

    outputs = lax.broadcasted_iota(jnp.int32, (LANES, LANES), 0)
    inputs = lax.broadcasted_iota(jnp.int32, (LANES, LANES), 1)
    centre = (lax.broadcasted_iota(jnp.int32, (1, LANES), 1) == HALF).astype(jnp.float32)

    @pl.loop(0, cables)
    def _(cable):
        row = (centre - taps_ref[pl.ds(cable, 1), :]) * (1.0 / (4.0 * two_pi))
        circulant = pltpu.roll(
            jnp.broadcast_to(row, (LANES, LANES)), 0, 1, stride=1, stride_axis=0
        )
        first = jnp.where(inputs >= outputs, circulant, 0.0).T
        second = jnp.where(inputs < outputs, circulant, 0.0).T
        high, low = split(jnp.concatenate([first, second], axis=1))
        for place, part in enumerate((high, high, low, low)):
            weight_ref[cable, pl.ds(place * LANES, LANES), :] = part

    def cable_step(cable, accumulated):
        for copy in copies(cable):
            copy.wait()

        def block_step(block, accumulated):
            lanes = pl.ds(pl.multiple_of(block * LANES, LANES), LANES)
            pieces = []
            for i in range(groups):
                rows = pl.ds(i * SUBLANES, SUBLANES)
                turns = wrap_ref[cable, rows, lanes].astype(jnp.float32)
                pieces.append(phase_ref[cable, rows, lanes] + two_pi * turns)
            sums = scanned(pieces)
            store_split(high_ref, low_ref, cable, block, sums)
            totals_ref[pl.ds(block * cables + cable, 1), :] = sums[-1][SUBLANES - 1 :, :]
            return tuple(a + b for a, b in zip(accumulated, sums))

        return lax.fori_loop(0, blocks, block_step, accumulated, unroll=4)

    zeros = tuple(jnp.zeros((SUBLANES, LANES), jnp.float32) for _ in range(groups))
    accumulated = lax.fori_loop(0, cables, cable_step, zeros)
    lane = lax.broadcasted_iota(jnp.int32, (SUBLANES, LANES), 1)
    tile = jnp.zeros((SUBLANES, LANES), jnp.float32)
    for i, value in enumerate(accumulated):
        tile = jnp.where(lane == i, jnp.sum(value, axis=1, keepdims=True), tile)
    sums_ref[...] = tile


def halo_kernel(inner_ref, outer_ref, high_ref, low_ref, totals_ref):
    pairs, time, _ = inner_ref.shape
    cables = 2 * pairs
    groups = time // SUBLANES
    is_even = lax.rem(lax.axis_index("chan"), 2) == 0
    for pair in range(pairs):
        inner, outer = (
            scanned([ref[pair, pl.ds(i * SUBLANES, SUBLANES), :] for i in range(groups)])
            for ref in (inner_ref, outer_ref)
        )
        right = [jnp.where(is_even, a, b) for a, b in zip(inner, outer)]
        left = [jnp.where(is_even, b, a) for a, b in zip(inner, outer)]
        for block, sums, moved in ((0, right, pair + pairs), (1, left, pair)):
            for cable in (pair, pair + pairs):
                placed = [pltpu.roll(v, HALF, 1) for v in sums] if cable == moved else sums
                store_split(high_ref, low_ref, cable, block, placed)
                totals_ref[pl.ds(block * cables + cable, 1), :] = placed[-1][SUBLANES - 1 :, :]


def filter_kernel(first, high_ref, low_ref, halo_high_ref, halo_low_ref, weight_ref, local_ref):
    _, blocks, time, _ = high_ref.shape
    lane = lax.broadcasted_iota(jnp.int32, (time, LANES), 1)

    @pl.loop(0, local_ref.shape[0])
    def _(index):
        cable = first + index
        high, low = (
            jnp.concatenate(
                [main[cable].reshape(blocks * time, LANES), halo[cable].reshape(2 * time, LANES)],
                axis=0,
            )
            for main, halo in ((high_ref, halo_high_ref), (low_ref, halo_low_ref))
        )
        product = jnp.dot(
            jnp.concatenate([high, low, high, low], axis=1),
            weight_ref[cable],
            preferred_element_type=jnp.float32,
        )

        def rolled(block):
            here = block if block >= 0 else blocks + 1
            there = block + 1
            return pltpu.roll(
                product[here * time : (here + 1) * time, :LANES]
                + product[there * time : (there + 1) * time, LANES:],
                HALF,
                1,
            )

        previous = rolled(-1)
        for block in range(blocks):
            following = rolled(block)
            local_ref[index, block] = jnp.where(lane < HALF, previous, following)
            previous = following


def level_kernel(
    population, local_refs, weight_ref, totals_refs, sums_ref, earlier_refs, coupling_ref,
    out_hbm, stage_ref, offset_ref, sem,
):
    share, blocks, time, _ = local_refs[0].shape
    cables = out_hbm.shape[0]
    groups = time // SUBLANES
    step, place = lax.axis_index("tm"), lax.axis_index("chan")
    inside_left = jnp.where(place == 0, 0.0, 1.0)
    inside_right = jnp.where(place == lax.axis_size("chan") - 1, 0.0, 1.0)

    def from_earlier(refs):
        value = jnp.zeros(refs[0].shape, jnp.float32)
        for bit, ref in enumerate(refs):
            value = value + jnp.where((step & (1 << bit)) != 0, ref[...], 0.0)
        return value

    offset_ref[...] = from_earlier(totals_refs)
    earlier = from_earlier(earlier_refs)[SUBLANES - 1 :, groups - 1 : groups]
    common = (sums_ref[...] + earlier) * (1.0 / population)
    columns = [
        jnp.broadcast_to(common[:, i : i + 1], (SUBLANES, LANES)) for i in range(groups)
    ]
    used = blocks + 2
    padded = -(-(used + 1) // SUBLANES) * SUBLANES
    row = lax.broadcasted_iota(jnp.int32, (padded, LANES), 0)
    lane = lax.broadcasted_iota(jnp.int32, (padded, LANES), 1)

    def filtered_offset(cable):
        offset = jnp.concatenate(
            [
                offset_ref[pl.ds(cable, used, stride=cables), :],
                jnp.ones((padded - used, LANES), jnp.float32),
            ],
            axis=0,
        )
        high, low = split(offset)
        product = jnp.dot(
            jnp.concatenate([high, low, high, low], axis=1),
            weight_ref[cable],
            preferred_element_type=jnp.float32,
        )
        here, there = product[:, :LANES], product[:, LANES:]
        left = pltpu.roll(here[used - 1 : used] + there[:1], HALF, 1)
        following = pltpu.roll(here + pltpu.roll(there, padded - 1, 0), HALF, 1)
        previous = jnp.where(row == 0, left, pltpu.roll(following, 1, 0))
        bias = jnp.where(lane < HALF, previous, following)
        here, there = here[used : used + 1], there[used : used + 1]
        middle = pltpu.roll(here + there, HALF, 1)
        first = pltpu.roll(here * inside_left + there, HALF, 1)
        last = pltpu.roll(here + there * inside_right, HALF, 1)
        first = jnp.where(lane[:1] < HALF, first, middle)
        last = jnp.where(lane[:1] < HALF, middle, last)
        return bias, first, middle, last

    carry = filtered_offset(0)
    for part, local_ref in enumerate(local_refs):

        def cable_step(index, carry, part=part, local_ref=local_ref):
            cable = part * share + index
            following = filtered_offset(jnp.minimum(cable + 1, cables - 1))
            bias, first, middle, last = carry
            shifts = [coupling_ref[cable] * column for column in columns]
            inner = [shift * middle for shift in shifts]
            for block in range(blocks):
                lanes = pl.ds(block * LANES, LANES)
                added = jnp.broadcast_to(bias[block : block + 1, :], (SUBLANES, LANES))
                if block == 0:
                    slopes = [shift * first for shift in shifts]
                elif block == blocks - 1:
                    slopes = [shift * last for shift in shifts]
                else:
                    slopes = inner
                for i in range(groups):
                    rows = pl.ds(i * SUBLANES, SUBLANES)
                    stage_ref[cable, rows, lanes] = local_ref[index, block, rows, :] + (
                        added - slopes[i]
                    )
            pltpu.make_async_copy(stage_ref.at[cable], out_hbm.at[cable], sem.at[cable]).start()
            return following

        carry = lax.fori_loop(0, share, cable_step, carry)
    for cable in range(cables):
        pltpu.make_async_copy(stage_ref.at[cable], out_hbm.at[cable], sem.at[cable]).wait()


def swapped(value, axis, bit):
    return lax.ppermute(value, axis, [(i, i ^ bit) for i in range(lax.axis_size(axis))])


def passed_on(value, bit):
    steps = lax.axis_size("tm")
    pairs = [
        (i, i ^ bit) for i in range(steps) if i & bit == 0 or (i ^ bit) | (2 * bit - 1) < steps - 1
    ]
    return lax.ppermute(value, "tm", pairs)


def shards(phase_step, wrap_count, coupling, filter_taps):
    cables, time, width = phase_step.shape
    blocks = width // LANES
    steps, places = lax.axis_size("tm"), lax.axis_size("chan")
    population = cables * width * places
    parts = 4
    share = cables // parts
    phase_step = pltpu.with_memory_space_constraint(phase_step, pltpu.HBM)
    wrap_count = pltpu.with_memory_space_constraint(wrap_count, pltpu.HBM)
    whole = pl.BlockSpec(memory_space=pltpu.VMEM)
    outside = pl.BlockSpec(memory_space=pl.ANY)
    scalars = pl.BlockSpec(memory_space=pltpu.SMEM)

    inner, outer = pl.pallas_call(
        edges_kernel,
        out_shape=[pltpu.VMEM((cables // 2, time, LANES), jnp.float32)] * 2,
        in_specs=[outside] * 2,
        out_specs=[whole] * 2,
        scratch_shapes=[
            pltpu.VMEM((2, cables, time, LANES), jnp.float32),
            pltpu.VMEM((2, cables, time, LANES), jnp.int32),
            pltpu.SemaphoreType.DMA((2, 2)),
        ],
        compiler_params=pltpu.CompilerParams(vmem_limit_bytes=8 << 20),
        name="edges",
    )(phase_step, wrap_count)
    odd_pairs = [(i, i + 1) for i in range(1, places - 1, 2)]
    outer = lax.ppermute(outer, "chan", odd_pairs + [(b, a) for a, b in odd_pairs])
    inner = swapped(inner, "chan", 1)

    high, low, totals, sums, weight = pl.pallas_call(
        unwrap_kernel,
        out_shape=(
            pltpu.VMEM((cables, blocks, time, LANES), jnp.bfloat16),
            pltpu.VMEM((cables, blocks, time, LANES), jnp.bfloat16),
            pltpu.VMEM((blocks * cables, LANES), jnp.float32),
            pltpu.VMEM((SUBLANES, LANES), jnp.float32),
            pltpu.VMEM((cables, 4 * LANES, 2 * LANES), jnp.bfloat16),
        ),
        in_specs=[outside, outside, whole],
        out_specs=[whole] * 5,
        scratch_shapes=[
            pltpu.VMEM((cables, time, width), jnp.float32),
            pltpu.VMEM((cables, time, width), jnp.int32),
            pltpu.SemaphoreType.DMA((2, cables)),
        ],
        compiler_params=pltpu.CompilerParams(vmem_limit_bytes=40 << 20),
        cost_estimate=pl.CostEstimate(
            flops=0, bytes_accessed=2 * phase_step.size * 4, transcendentals=0
        ),
        name="unwrap",
    )(phase_step, wrap_count, filter_taps)

    halo_high, halo_low, halo_totals = pl.pallas_call(
        halo_kernel,
        out_shape=(
            pltpu.VMEM((cables, 2, time, LANES), jnp.bfloat16),
            pltpu.VMEM((cables, 2, time, LANES), jnp.bfloat16),
            pltpu.VMEM((2 * cables, LANES), jnp.float32),
        ),
        in_specs=[whole] * 2,
        out_specs=[whole] * 3,
        compiler_params=pltpu.CompilerParams(vmem_limit_bytes=8 << 20),
        name="halo",
    )(inner, outer)

    def filtered(part, weight):
        return pl.pallas_call(
            functools.partial(filter_kernel, part * share),
            out_shape=pltpu.VMEM((share, blocks, time, LANES), jnp.float32),
            in_specs=[whole] * 5,
            out_specs=whole,
            compiler_params=pltpu.CompilerParams(vmem_limit_bytes=16 << 20),
            cost_estimate=pl.CostEstimate(
                flops=2 * share * (blocks + 2) * time * 8 * LANES * LANES,
                bytes_accessed=1 << 20,
                transcendentals=0,
            ),
            name="filter",
        )(high, low, halo_high, halo_low, weight)

    running = jnp.concatenate([totals, halo_totals], axis=0)
    received = [passed_on(running, 1)]
    sums, halo_totals = lax.optimization_barrier((sums, halo_totals))
    rounds = [("chan", 1 << bit) for bit in range(places.bit_length() - 1)]
    rounds += [("tm", 1 << bit) for bit in range(steps.bit_length() - 1)]
    local, received_sums, chan_sums, mark = [], [], sums, sums
    for number, (axis, bit) in enumerate(rounds):
        incoming = passed_on(sums, bit) if axis == "tm" else swapped(sums, axis, bit)
        if len(local) < parts:
            tied, mark = lax.optimization_barrier((weight, mark))
            part = filtered(len(local), tied)
            incoming, part = lax.optimization_barrier((incoming, part))
            local.append(part)
        if number % 2 == 1 and 1 << len(received) < steps:
            running = running + received[-1]
            running, incoming = lax.optimization_barrier((running, incoming))
            received.append(passed_on(running, 1 << len(received)))
        if axis == "tm":
            received_sums.append(incoming)
        sums = mark = sums + incoming
        if axis == "chan":
            chan_sums = sums
    while len(local) < parts:
        local.append(filtered(len(local), weight))

    return pl.pallas_call(
        functools.partial(level_kernel, population),
        out_shape=jax.ShapeDtypeStruct(phase_step.shape, jnp.float32),
        in_specs=[
            [whole] * parts, whole, [whole] * len(received), whole, [whole] * len(received), scalars
        ],
        out_specs=outside,
        scratch_shapes=[
            pltpu.VMEM((cables, time, width), jnp.float32),
            pltpu.VMEM(((blocks + 2) * cables, LANES), jnp.float32),
            pltpu.SemaphoreType.DMA((cables,)),
        ],
        compiler_params=pltpu.CompilerParams(vmem_limit_bytes=24 << 20),
        name="level",
    )(local, weight, received, chan_sums, received_sums, coupling)


def solution(mesh):
    placed = (P(None, "tm", "chan"), P(None, "tm", "chan"), P(), P())
    return jax.shard_map(
        shards, mesh=mesh, in_specs=placed, out_specs=P(None, "tm", "chan"), check_vma=False
    )
```

```python
import functools
import math

import jax
import jax.numpy as jnp
from jax import lax
from jax.experimental import pallas as pl
from jax.experimental.pallas import tpu as pltpu
from jax.sharding import PartitionSpec as P

two_pi = 2.0 * math.pi
LANES = 128
HALF = LANES // 2
SUBLANES = 8


def shifted_down(value, amount):
    rows = lax.broadcasted_iota(jnp.int32, value.shape, 0)
    return jnp.where(rows >= amount, pltpu.roll(value, amount, 0), 0.0)


def scanned(pieces):
    sums, carry = [], None
    for value in pieces:
        amount = 1
        while amount < SUBLANES:
            value = value + shifted_down(value, amount)
            amount *= 2
        if carry is not None:
            value = value + carry
        carry = jnp.broadcast_to(value[SUBLANES - 1 :, :], value.shape)
        sums.append(value)
    return sums


def split(value):
    high = value.astype(jnp.bfloat16)
    return high, (value - high.astype(jnp.float32)).astype(jnp.bfloat16)


def store_split(high_ref, low_ref, cable, block, sums):
    for pair in range(0, len(sums), 2):
        rows = pl.ds(pair * SUBLANES, 2 * SUBLANES)
        high, low = split(jnp.concatenate(sums[pair : pair + 2], axis=0))
        high_ref[cable, block, rows, :] = high
        low_ref[cable, block, rows, :] = low


def edges_kernel(phase_hbm, wrap_hbm, inner_ref, outer_ref, phase_ref, wrap_ref, sem):
    cables, time, width = phase_hbm.shape
    is_even = lax.rem(lax.axis_index("chan"), 2) == 0
    sends_last = (is_even, jnp.logical_not(is_even))
    copies = []
    for side, last in enumerate(sends_last):
        lanes = pl.ds(pl.multiple_of(jnp.where(last, width - LANES, 0), LANES), LANES)
        for kind, (source, target) in enumerate(((phase_hbm, phase_ref), (wrap_hbm, wrap_ref))):
            copies.append(
                pltpu.make_async_copy(source.at[:, :, lanes], target.at[side], sem.at[kind, side])
            )
    for copy in copies:
        copy.start()
    for copy in copies:
        copy.wait()
    lane = lax.broadcasted_iota(jnp.int32, (time, LANES), 1)
    for side, (last, target) in enumerate(zip(sends_last, (inner_ref, outer_ref))):
        for cable in range(cables // 2):
            low, high = (
                phase_ref[side, c] + two_pi * wrap_ref[side, c].astype(jnp.float32)
                for c in (cable, cable + cables // 2)
            )
            low = jnp.where(last, pltpu.roll(low, HALF, 1), low)
            high = jnp.where(last, high, pltpu.roll(high, HALF, 1))
            target[cable] = jnp.where(lane < HALF, low, high)


def unwrap_kernel(
    phase_hbm, wrap_hbm, taps_ref,
    high_ref, low_ref, totals_ref, sums_ref, weight_ref,
    phase_ref, wrap_ref, sem,
):
    cables, time, width = phase_hbm.shape
    blocks = width // LANES
    groups = time // SUBLANES

    def copies(cable):
        return (
            pltpu.make_async_copy(phase_hbm.at[cable], phase_ref.at[cable], sem.at[0, cable]),
            pltpu.make_async_copy(wrap_hbm.at[cable], wrap_ref.at[cable], sem.at[1, cable]),
        )

    for cable in range(cables):
        for copy in copies(cable):
            copy.start()

    outputs = lax.broadcasted_iota(jnp.int32, (LANES, LANES), 0)
    inputs = lax.broadcasted_iota(jnp.int32, (LANES, LANES), 1)
    centre = (lax.broadcasted_iota(jnp.int32, (1, LANES), 1) == HALF).astype(jnp.float32)

    @pl.loop(0, cables)
    def _(cable):
        row = (centre - taps_ref[pl.ds(cable, 1), :]) * (1.0 / (4.0 * two_pi))
        circulant = pltpu.roll(
            jnp.broadcast_to(row, (LANES, LANES)), 0, 1, stride=1, stride_axis=0
        )
        first = jnp.where(inputs >= outputs, circulant, 0.0).T
        second = jnp.where(inputs < outputs, circulant, 0.0).T
        high, low = split(jnp.concatenate([first, second], axis=1))
        for place, part in enumerate((high, high, low, low)):
            weight_ref[cable, pl.ds(place * LANES, LANES), :] = part

    def cable_step(cable, accumulated):
        for copy in copies(cable):
            copy.wait()

        def block_step(block, accumulated):
            lanes = pl.ds(pl.multiple_of(block * LANES, LANES), LANES)
            pieces = []
            for i in range(groups):
                rows = pl.ds(i * SUBLANES, SUBLANES)
                turns = wrap_ref[cable, rows, lanes].astype(jnp.float32)
                pieces.append(phase_ref[cable, rows, lanes] + two_pi * turns)
            sums = scanned(pieces)
            store_split(high_ref, low_ref, cable, block, sums)
            totals_ref[pl.ds(block * cables + cable, 1), :] = sums[-1][SUBLANES - 1 :, :]
            return tuple(a + b for a, b in zip(accumulated, sums))

        return lax.fori_loop(0, blocks, block_step, accumulated, unroll=4)

    zeros = tuple(jnp.zeros((SUBLANES, LANES), jnp.float32) for _ in range(groups))
    accumulated = lax.fori_loop(0, cables, cable_step, zeros)
    lane = lax.broadcasted_iota(jnp.int32, (SUBLANES, LANES), 1)
    tile = jnp.zeros((SUBLANES, LANES), jnp.float32)
    for i, value in enumerate(accumulated):
        tile = jnp.where(lane == i, jnp.sum(value, axis=1, keepdims=True), tile)
    sums_ref[...] = tile


def halo_kernel(inner_ref, outer_ref, high_ref, low_ref, totals_ref):
    pairs, time, _ = inner_ref.shape
    cables = 2 * pairs
    groups = time // SUBLANES
    place = lax.axis_index("chan")
    is_even = lax.rem(place, 2) == 0
    at_end = (place == 0) | (place == lax.axis_size("chan") - 1)
    for pair in range(pairs):
        inner, outer = (
            scanned([ref[pair, pl.ds(i * SUBLANES, SUBLANES), :] for i in range(groups)])
            for ref in (inner_ref, outer_ref)
        )
        outer = [jnp.where(at_end, 0.0, value) for value in outer]
        right = [jnp.where(is_even, a, b) for a, b in zip(inner, outer)]
        left = [jnp.where(is_even, b, a) for a, b in zip(inner, outer)]
        for block, sums, moved in ((0, right, pair + pairs), (1, left, pair)):
            for cable in (pair, pair + pairs):
                placed = [pltpu.roll(v, HALF, 1) for v in sums] if cable == moved else sums
                store_split(high_ref, low_ref, cable, block, placed)
                totals_ref[pl.ds(block * cables + cable, 1), :] = placed[-1][SUBLANES - 1 :, :]


def filter_kernel(first, high_ref, low_ref, halo_high_ref, halo_low_ref, weight_ref, local_ref):
    _, blocks, time, _ = high_ref.shape
    lane = lax.broadcasted_iota(jnp.int32, (time, LANES), 1)

    @pl.loop(0, local_ref.shape[0])
    def _(index):
        cable = first + index
        high, low = (
            jnp.concatenate(
                [main[cable].reshape(blocks * time, LANES), halo[cable].reshape(2 * time, LANES)],
                axis=0,
            )
            for main, halo in ((high_ref, halo_high_ref), (low_ref, halo_low_ref))
        )
        product = jnp.dot(
            jnp.concatenate([high, low, high, low], axis=1),
            weight_ref[cable],
            preferred_element_type=jnp.float32,
        )

        def rolled(block):
            here = block if block >= 0 else blocks + 1
            there = block + 1
            return pltpu.roll(
                product[here * time : (here + 1) * time, :LANES]
                + product[there * time : (there + 1) * time, LANES:],
                HALF,
                1,
            )

        previous = rolled(-1)
        for block in range(blocks):
            following = rolled(block)
            local_ref[index, block] = jnp.where(lane < HALF, previous, following)
            previous = following


def level_kernel(
    population, local_refs, weight_ref, totals_refs, sums_ref, earlier_refs, coupling_ref,
    out_hbm, stage_ref, offset_ref, sem,
):
    share, blocks, time, _ = local_refs[0].shape
    cables = out_hbm.shape[0]
    groups = time // SUBLANES
    step, place = lax.axis_index("tm"), lax.axis_index("chan")
    inside_left = jnp.where(place == 0, 0.0, 1.0)
    inside_right = jnp.where(place == lax.axis_size("chan") - 1, 0.0, 1.0)

    def from_earlier(refs):
        value = jnp.zeros(refs[0].shape, jnp.float32)
        for bit, ref in enumerate(refs):
            value = value + jnp.where((step & (1 << bit)) != 0, ref[...], 0.0)
        return value

    offset_ref[...] = from_earlier(totals_refs)
    earlier = from_earlier(earlier_refs)[SUBLANES - 1 :, groups - 1 : groups]
    common = (sums_ref[...] + earlier) * (1.0 / population)
    columns = [
        jnp.broadcast_to(common[:, i : i + 1], (SUBLANES, LANES)) for i in range(groups)
    ]
    used = blocks + 2
    padded = -(-(used + 1) // SUBLANES) * SUBLANES
    row = lax.broadcasted_iota(jnp.int32, (padded, LANES), 0)
    lane = lax.broadcasted_iota(jnp.int32, (padded, LANES), 1)

    def filtered_offset(cable):
        offset = jnp.concatenate(
            [
                offset_ref[pl.ds(cable, used, stride=cables), :],
                jnp.ones((padded - used, LANES), jnp.float32),
            ],
            axis=0,
        )
        high, low = split(offset)
        product = jnp.dot(
            jnp.concatenate([high, low, high, low], axis=1),
            weight_ref[cable],
            preferred_element_type=jnp.float32,
        )
        here, there = product[:, :LANES], product[:, LANES:]
        left = pltpu.roll(here[used - 1 : used] + there[:1], HALF, 1)
        following = pltpu.roll(here + pltpu.roll(there, padded - 1, 0), HALF, 1)
        previous = jnp.where(row == 0, left, pltpu.roll(following, 1, 0))
        bias = jnp.where(lane < HALF, previous, following)
        here, there = here[used : used + 1], there[used : used + 1]
        middle = pltpu.roll(here + there, HALF, 1)
        first = pltpu.roll(here * inside_left + there, HALF, 1)
        last = pltpu.roll(here + there * inside_right, HALF, 1)
        first = jnp.where(lane[:1] < HALF, first, middle)
        last = jnp.where(lane[:1] < HALF, middle, last)
        return bias, first, middle, last

    carry = filtered_offset(0)
    for part, local_ref in enumerate(local_refs):

        def cable_step(index, carry, part=part, local_ref=local_ref):
            cable = part * share + index
            following = filtered_offset(jnp.minimum(cable + 1, cables - 1))
            bias, first, middle, last = carry
            shifts = [coupling_ref[cable] * column for column in columns]
            inner = [shift * middle for shift in shifts]
            for block in range(blocks):
                lanes = pl.ds(block * LANES, LANES)
                added = jnp.broadcast_to(bias[block : block + 1, :], (SUBLANES, LANES))
                if block == 0:
                    slopes = [shift * first for shift in shifts]
                elif block == blocks - 1:
                    slopes = [shift * last for shift in shifts]
                else:
                    slopes = inner
                for i in range(groups):
                    rows = pl.ds(i * SUBLANES, SUBLANES)
                    stage_ref[cable, rows, lanes] = local_ref[index, block, rows, :] + (
                        added - slopes[i]
                    )
            pltpu.make_async_copy(stage_ref.at[cable], out_hbm.at[cable], sem.at[cable]).start()
            return following

        carry = lax.fori_loop(0, share, cable_step, carry)
    for cable in range(cables):
        pltpu.make_async_copy(stage_ref.at[cable], out_hbm.at[cable], sem.at[cable]).wait()


def swapped(value, axis, bit):
    return lax.ppermute(value, axis, [(i, i ^ bit) for i in range(lax.axis_size(axis))])


def shards(phase_step, wrap_count, coupling, filter_taps):
    cables, time, width = phase_step.shape
    blocks = width // LANES
    steps, places = lax.axis_size("tm"), lax.axis_size("chan")
    population = cables * width * places
    parts = 4
    share = cables // parts
    phase_step = pltpu.with_memory_space_constraint(phase_step, pltpu.HBM)
    wrap_count = pltpu.with_memory_space_constraint(wrap_count, pltpu.HBM)
    whole = pl.BlockSpec(memory_space=pltpu.VMEM)
    outside = pl.BlockSpec(memory_space=pl.ANY)
    scalars = pl.BlockSpec(memory_space=pltpu.SMEM)

    inner, outer = pl.pallas_call(
        edges_kernel,
        out_shape=[pltpu.VMEM((cables // 2, time, LANES), jnp.float32)] * 2,
        in_specs=[outside] * 2,
        out_specs=[whole] * 2,
        scratch_shapes=[
            pltpu.VMEM((2, cables, time, LANES), jnp.float32),
            pltpu.VMEM((2, cables, time, LANES), jnp.int32),
            pltpu.SemaphoreType.DMA((2, 2)),
        ],
        compiler_params=pltpu.CompilerParams(vmem_limit_bytes=8 << 20),
        name="edges",
    )(phase_step, wrap_count)
    outer_pairs = [(i, (i + (1 if i % 2 else -1)) % places) for i in range(places)]
    outer = lax.ppermute(outer, "chan", outer_pairs)
    inner = swapped(inner, "chan", 1)

    high, low, totals, sums, weight = pl.pallas_call(
        unwrap_kernel,
        out_shape=(
            pltpu.VMEM((cables, blocks, time, LANES), jnp.bfloat16),
            pltpu.VMEM((cables, blocks, time, LANES), jnp.bfloat16),
            pltpu.VMEM((blocks * cables, LANES), jnp.float32),
            pltpu.VMEM((SUBLANES, LANES), jnp.float32),
            pltpu.VMEM((cables, 4 * LANES, 2 * LANES), jnp.bfloat16),
        ),
        in_specs=[outside, outside, whole],
        out_specs=[whole] * 5,
        scratch_shapes=[
            pltpu.VMEM((cables, time, width), jnp.float32),
            pltpu.VMEM((cables, time, width), jnp.int32),
            pltpu.SemaphoreType.DMA((2, cables)),
        ],
        compiler_params=pltpu.CompilerParams(vmem_limit_bytes=40 << 20),
        cost_estimate=pl.CostEstimate(
            flops=0, bytes_accessed=2 * phase_step.size * 4, transcendentals=0
        ),
        name="unwrap",
    )(phase_step, wrap_count, filter_taps)

    halo_high, halo_low, halo_totals = pl.pallas_call(
        halo_kernel,
        out_shape=(
            pltpu.VMEM((cables, 2, time, LANES), jnp.bfloat16),
            pltpu.VMEM((cables, 2, time, LANES), jnp.bfloat16),
            pltpu.VMEM((2 * cables, LANES), jnp.float32),
        ),
        in_specs=[whole] * 2,
        out_specs=[whole] * 3,
        compiler_params=pltpu.CompilerParams(vmem_limit_bytes=8 << 20),
        name="halo",
    )(inner, outer)

    def filtered(part, weight):
        return pl.pallas_call(
            functools.partial(filter_kernel, part * share),
            out_shape=pltpu.VMEM((share, blocks, time, LANES), jnp.float32),
            in_specs=[whole] * 5,
            out_specs=whole,
            compiler_params=pltpu.CompilerParams(vmem_limit_bytes=16 << 20),
            cost_estimate=pl.CostEstimate(
                flops=2 * share * (blocks + 2) * time * 8 * LANES * LANES,
                bytes_accessed=1 << 20,
                transcendentals=0,
            ),
            name="filter",
        )(high, low, halo_high, halo_low, weight)

    running = jnp.concatenate([totals, halo_totals], axis=0)
    received = [swapped(running, "tm", 1)]
    sums, halo_totals = lax.optimization_barrier((sums, halo_totals))
    rounds = [("chan", 1 << bit) for bit in range(places.bit_length() - 1)]
    rounds += [("tm", 1 << bit) for bit in range(steps.bit_length() - 1)]
    local, received_sums, chan_sums, mark = [], [], sums, sums
    for number, (axis, bit) in enumerate(rounds):
        if number > 1 and number % 2 == 0 and 1 << len(received) < steps:
            running = running + received[-1]
            received.append(swapped(running, "tm", 1 << len(received)))
            sums, running = lax.optimization_barrier((sums, running))
        incoming = swapped(sums, axis, bit)
        if len(local) < parts:
            tied, mark = lax.optimization_barrier((weight, mark))
            part = filtered(len(local), tied)
            incoming, part = lax.optimization_barrier((incoming, part))
            local.append(part)
        if axis == "tm":
            received_sums.append(incoming)
        sums = mark = sums + incoming
        if axis == "chan":
            chan_sums = sums
    while 1 << len(received) < steps:
        running = running + received[-1]
        received.append(swapped(running, "tm", 1 << len(received)))
    while len(local) < parts:
        local.append(filtered(len(local), weight))

    return pl.pallas_call(
        functools.partial(level_kernel, population),
        out_shape=jax.ShapeDtypeStruct(phase_step.shape, jnp.float32),
        in_specs=[
            [whole] * parts, whole, [whole] * len(received), whole, [whole] * len(received), scalars
        ],
        out_specs=outside,
        scratch_shapes=[
            pltpu.VMEM((cables, time, width), jnp.float32),
            pltpu.VMEM(((blocks + 2) * cables, LANES), jnp.float32),
            pltpu.SemaphoreType.DMA((cables,)),
        ],
        compiler_params=pltpu.CompilerParams(vmem_limit_bytes=24 << 20),
        name="level",
    )(local, weight, received, chan_sums, received_sums, coupling)


def solution(mesh):
    placed = (P(None, "tm", "chan"), P(None, "tm", "chan"), P(), P())
    return jax.shard_map(
        shards, mesh=mesh, in_specs=placed, out_specs=P(None, "tm", "chan"), check_vma=False
    )
```

```python
import functools
import math

import jax
import jax.numpy as jnp
from jax import lax
from jax.experimental import pallas as pl
from jax.experimental.pallas import tpu as pltpu
from jax.sharding import PartitionSpec as P

two_pi = 2.0 * math.pi
LANES = 128
HALF = LANES // 2
SUBLANES = 8
CHUNKS = 2


def shifted_down(value, amount):
    rows = lax.broadcasted_iota(jnp.int32, value.shape, 0)
    return jnp.where(rows >= amount, pltpu.roll(value, amount, 0), 0.0)


def scanned(pieces):
    sums, carry = [], None
    for value in pieces:
        amount = 1
        while amount < SUBLANES:
            value = value + shifted_down(value, amount)
            amount *= 2
        if carry is not None:
            value = value + carry
        carry = jnp.broadcast_to(value[SUBLANES - 1 :, :], value.shape)
        sums.append(value)
    return sums


def split(value):
    high = value.astype(jnp.bfloat16)
    return high, (value - high.astype(jnp.float32)).astype(jnp.bfloat16)


def store_split(high_ref, low_ref, cable, block, sums):
    for pair in range(0, len(sums), 2):
        rows = pl.ds(pair * SUBLANES, 2 * SUBLANES)
        high, low = split(jnp.concatenate(sums[pair : pair + 2], axis=0))
        high_ref[cable, block, rows, :] = high
        low_ref[cable, block, rows, :] = low


def edges_kernel(phase_hbm, wrap_hbm, inner_ref, outer_ref, phase_ref, wrap_ref, sem):
    cables, time, width = phase_hbm.shape
    is_even = lax.rem(lax.axis_index("chan"), 2) == 0
    sends_last = (is_even, jnp.logical_not(is_even))
    copies = []
    for side, last in enumerate(sends_last):
        lanes = pl.ds(pl.multiple_of(jnp.where(last, width - LANES, 0), LANES), LANES)
        for kind, (source, target) in enumerate(((phase_hbm, phase_ref), (wrap_hbm, wrap_ref))):
            copies.append(
                pltpu.make_async_copy(source.at[:, :, lanes], target.at[side], sem.at[kind, side])
            )
    for copy in copies:
        copy.start()
    for copy in copies:
        copy.wait()
    lane = lax.broadcasted_iota(jnp.int32, (time, LANES), 1)
    for side, (last, target) in enumerate(zip(sends_last, (inner_ref, outer_ref))):
        for cable in range(cables // 2):
            low, high = (
                phase_ref[side, c] + two_pi * wrap_ref[side, c].astype(jnp.float32)
                for c in (cable, cable + cables // 2)
            )
            low = jnp.where(last, pltpu.roll(low, HALF, 1), low)
            high = jnp.where(last, high, pltpu.roll(high, HALF, 1))
            target[cable] = jnp.where(lane < HALF, low, high)


def unwrap_kernel(
    phase_hbm, wrap_hbm, taps_ref,
    high_ref, low_ref, totals_ref, sums_ref, weight_ref,
    phase_ref, wrap_ref, sem,
):
    cables, time, width = phase_hbm.shape
    blocks = width // LANES
    groups = time // SUBLANES

    span = width // CHUNKS

    def copies(chunk):
        cable, lanes = chunk // CHUNKS, pl.ds(pl.multiple_of(chunk % CHUNKS * span, span), span)
        return (
            pltpu.make_async_copy(
                phase_hbm.at[cable, :, lanes], phase_ref.at[cable, :, lanes], sem.at[0, chunk]
            ),
            pltpu.make_async_copy(
                wrap_hbm.at[cable, :, lanes], wrap_ref.at[cable, :, lanes], sem.at[1, chunk]
            ),
        )

    for chunk in range(cables * CHUNKS):
        for copy in copies(chunk):
            copy.start()

    outputs = lax.broadcasted_iota(jnp.int32, (LANES, LANES), 0)
    inputs = lax.broadcasted_iota(jnp.int32, (LANES, LANES), 1)
    centre = (lax.broadcasted_iota(jnp.int32, (1, LANES), 1) == HALF).astype(jnp.float32)

    @pl.loop(0, cables)
    def _(cable):
        row = (centre - taps_ref[pl.ds(cable, 1), :]) * (1.0 / (4.0 * two_pi))
        circulant = pltpu.roll(
            jnp.broadcast_to(row, (LANES, LANES)), 0, 1, stride=1, stride_axis=0
        )
        first = jnp.where(inputs >= outputs, circulant, 0.0).T
        second = jnp.where(inputs < outputs, circulant, 0.0).T
        high, low = split(jnp.concatenate([first, second], axis=1))
        for place, part in enumerate((high, high, low, low)):
            weight_ref[cable, pl.ds(place * LANES, LANES), :] = part

    def chunk_step(chunk, accumulated):
        for copy in copies(chunk):
            copy.wait()
        cable = chunk // CHUNKS
        start = chunk % CHUNKS * (blocks // CHUNKS)

        def block_step(index, accumulated):
            block = start + index
            lanes = pl.ds(pl.multiple_of(block * LANES, LANES), LANES)
            pieces = []
            for i in range(groups):
                rows = pl.ds(i * SUBLANES, SUBLANES)
                turns = wrap_ref[cable, rows, lanes].astype(jnp.float32)
                pieces.append(phase_ref[cable, rows, lanes] + two_pi * turns)
            sums = scanned(pieces)
            store_split(high_ref, low_ref, cable, block, sums)
            totals_ref[pl.ds(block * cables + cable, 1), :] = sums[-1][SUBLANES - 1 :, :]
            return tuple(a + b for a, b in zip(accumulated, sums))

        return lax.fori_loop(0, blocks // CHUNKS, block_step, accumulated, unroll=4)

    zeros = tuple(jnp.zeros((SUBLANES, LANES), jnp.float32) for _ in range(groups))
    accumulated = lax.fori_loop(0, cables * CHUNKS, chunk_step, zeros)
    lane = lax.broadcasted_iota(jnp.int32, (SUBLANES, LANES), 1)
    tile = jnp.zeros((SUBLANES, LANES), jnp.float32)
    for i, value in enumerate(accumulated):
        tile = jnp.where(lane == i, jnp.sum(value, axis=1, keepdims=True), tile)
    sums_ref[...] = tile


def halo_kernel(inner_ref, outer_ref, high_ref, low_ref, totals_ref):
    pairs, time, _ = inner_ref.shape
    cables = 2 * pairs
    groups = time // SUBLANES
    place = lax.axis_index("chan")
    is_even = lax.rem(place, 2) == 0
    at_end = (place == 0) | (place == lax.axis_size("chan") - 1)
    for pair in range(pairs):
        inner, outer = (
            scanned([ref[pair, pl.ds(i * SUBLANES, SUBLANES), :] for i in range(groups)])
            for ref in (inner_ref, outer_ref)
        )
        outer = [jnp.where(at_end, 0.0, value) for value in outer]
        right = [jnp.where(is_even, a, b) for a, b in zip(inner, outer)]
        left = [jnp.where(is_even, b, a) for a, b in zip(inner, outer)]
        for block, sums, moved in ((0, right, pair + pairs), (1, left, pair)):
            for cable in (pair, pair + pairs):
                placed = [pltpu.roll(v, HALF, 1) for v in sums] if cable == moved else sums
                store_split(high_ref, low_ref, cable, block, placed)
                totals_ref[pl.ds(block * cables + cable, 1), :] = placed[-1][SUBLANES - 1 :, :]


def filter_kernel(first, high_ref, low_ref, halo_high_ref, halo_low_ref, weight_ref, local_ref):
    _, blocks, time, _ = high_ref.shape
    lane = lax.broadcasted_iota(jnp.int32, (time, LANES), 1)

    @pl.loop(0, local_ref.shape[0])
    def _(index):
        cable = first + index
        high, low = (
            jnp.concatenate(
                [main[cable].reshape(blocks * time, LANES), halo[cable].reshape(2 * time, LANES)],
                axis=0,
            )
            for main, halo in ((high_ref, halo_high_ref), (low_ref, halo_low_ref))
        )
        product = jnp.dot(
            jnp.concatenate([high, low, high, low], axis=1),
            weight_ref[cable],
            preferred_element_type=jnp.float32,
        )

        def rolled(block):
            here = block if block >= 0 else blocks + 1
            there = block + 1
            return pltpu.roll(
                product[here * time : (here + 1) * time, :LANES]
                + product[there * time : (there + 1) * time, LANES:],
                HALF,
                1,
            )

        previous = rolled(-1)
        for block in range(blocks):
            following = rolled(block)
            local_ref[index, block] = jnp.where(lane < HALF, previous, following)
            previous = following


def level_kernel(
    population, local_refs, weight_ref, totals_refs, sums_ref, earlier_refs, coupling_ref,
    out_hbm, stage_ref, offset_ref, sem,
):
    _, blocks, time, _ = local_refs[0].shape
    span = blocks * LANES // CHUNKS
    cables = out_hbm.shape[0]
    groups = time // SUBLANES
    step, place = lax.axis_index("tm"), lax.axis_index("chan")
    inside_left = jnp.where(place == 0, 0.0, 1.0)
    inside_right = jnp.where(place == lax.axis_size("chan") - 1, 0.0, 1.0)

    def from_earlier(refs):
        value = jnp.zeros(refs[0].shape, jnp.float32)
        for bit, ref in enumerate(refs):
            value = value + jnp.where((step & (1 << bit)) != 0, ref[...], 0.0)
        return value

    offset_ref[...] = from_earlier(totals_refs)
    earlier = from_earlier(earlier_refs)[SUBLANES - 1 :, groups - 1 : groups]
    common = (sums_ref[...] + earlier) * (1.0 / population)
    columns = [
        jnp.broadcast_to(common[:, i : i + 1], (SUBLANES, LANES)) for i in range(groups)
    ]
    used = blocks + 2
    padded = -(-(used + 1) // SUBLANES) * SUBLANES
    row = lax.broadcasted_iota(jnp.int32, (padded, LANES), 0)
    lane = lax.broadcasted_iota(jnp.int32, (padded, LANES), 1)

    def filtered_offset(cable):
        offset = jnp.concatenate(
            [
                offset_ref[pl.ds(cable, used, stride=cables), :],
                jnp.ones((padded - used, LANES), jnp.float32),
            ],
            axis=0,
        )
        high, low = split(offset)
        product = jnp.dot(
            jnp.concatenate([high, low, high, low], axis=1),
            weight_ref[cable],
            preferred_element_type=jnp.float32,
        )
        here, there = product[:, :LANES], product[:, LANES:]
        left = pltpu.roll(here[used - 1 : used] + there[:1], HALF, 1)
        following = pltpu.roll(here + pltpu.roll(there, padded - 1, 0), HALF, 1)
        previous = jnp.where(row == 0, left, pltpu.roll(following, 1, 0))
        bias = jnp.where(lane < HALF, previous, following)
        here, there = here[used : used + 1], there[used : used + 1]
        middle = pltpu.roll(here + there, HALF, 1)
        first = pltpu.roll(here * inside_left + there, HALF, 1)
        last = pltpu.roll(here + there * inside_right, HALF, 1)
        first = jnp.where(lane[:1] < HALF, first, middle)
        last = jnp.where(lane[:1] < HALF, middle, last)
        return bias, first, middle, last

    def written(cable, chunk):
        lanes = pl.ds(chunk * span, span)
        return pltpu.make_async_copy(
            stage_ref.at[cable, :, lanes], out_hbm.at[cable, :, lanes], sem.at[cable, chunk]
        )

    carry = filtered_offset(0)
    first_cable = 0
    for local_ref in local_refs:

        def cable_step(index, carry, first_cable=first_cable, local_ref=local_ref):
            cable = first_cable + index
            following = filtered_offset(jnp.minimum(cable + 1, cables - 1))
            bias, first, middle, last = carry
            shifts = [coupling_ref[cable] * column for column in columns]
            inner = [shift * middle for shift in shifts]
            for block in range(blocks):
                lanes = pl.ds(block * LANES, LANES)
                added = jnp.broadcast_to(bias[block : block + 1, :], (SUBLANES, LANES))
                if block == 0:
                    slopes = [shift * first for shift in shifts]
                elif block == blocks - 1:
                    slopes = [shift * last for shift in shifts]
                else:
                    slopes = inner
                for i in range(groups):
                    rows = pl.ds(i * SUBLANES, SUBLANES)
                    stage_ref[cable, rows, lanes] = local_ref[index, block, rows, :] + (
                        added - slopes[i]
                    )
                if (block + 1) % (blocks // CHUNKS) == 0:
                    written(cable, block // (blocks // CHUNKS)).start()
            return following

        carry = lax.fori_loop(0, local_ref.shape[0], cable_step, carry)
        first_cable += local_ref.shape[0]
    for cable in range(cables):
        for chunk in range(CHUNKS):
            written(cable, chunk).wait()


def swapped(value, axis, bit):
    return lax.ppermute(value, axis, [(i, i ^ bit) for i in range(lax.axis_size(axis))])


def shards(phase_step, wrap_count, coupling, filter_taps):
    cables, time, width = phase_step.shape
    blocks = width // LANES
    steps, places = lax.axis_size("tm"), lax.axis_size("chan")
    population = cables * width * places
    bounds = [0, 3 * cables // 8, 5 * cables // 8, cables]
    parts = len(bounds) - 1
    phase_step = pltpu.with_memory_space_constraint(phase_step, pltpu.HBM)
    wrap_count = pltpu.with_memory_space_constraint(wrap_count, pltpu.HBM)
    whole = pl.BlockSpec(memory_space=pltpu.VMEM)
    outside = pl.BlockSpec(memory_space=pl.ANY)
    scalars = pl.BlockSpec(memory_space=pltpu.SMEM)

    inner, outer = pl.pallas_call(
        edges_kernel,
        out_shape=[pltpu.VMEM((cables // 2, time, LANES), jnp.float32)] * 2,
        in_specs=[outside] * 2,
        out_specs=[whole] * 2,
        scratch_shapes=[
            pltpu.VMEM((2, cables, time, LANES), jnp.float32),
            pltpu.VMEM((2, cables, time, LANES), jnp.int32),
            pltpu.SemaphoreType.DMA((2, 2)),
        ],
        compiler_params=pltpu.CompilerParams(vmem_limit_bytes=8 << 20),
        name="edges",
    )(phase_step, wrap_count)
    outer_pairs = [(i, (i + (1 if i % 2 else -1)) % places) for i in range(places)]
    outer = lax.ppermute(outer, "chan", outer_pairs)
    inner = swapped(inner, "chan", 1)

    high, low, totals, sums, weight = pl.pallas_call(
        unwrap_kernel,
        out_shape=(
            pltpu.VMEM((cables, blocks, time, LANES), jnp.bfloat16),
            pltpu.VMEM((cables, blocks, time, LANES), jnp.bfloat16),
            pltpu.VMEM((blocks * cables, LANES), jnp.float32),
            pltpu.VMEM((SUBLANES, LANES), jnp.float32),
            pltpu.VMEM((cables, 4 * LANES, 2 * LANES), jnp.bfloat16),
        ),
        in_specs=[outside, outside, whole],
        out_specs=[whole] * 5,
        scratch_shapes=[
            pltpu.VMEM((cables, time, width), jnp.float32),
            pltpu.VMEM((cables, time, width), jnp.int32),
            pltpu.SemaphoreType.DMA((2, cables * CHUNKS)),
        ],
        compiler_params=pltpu.CompilerParams(vmem_limit_bytes=40 << 20),
        cost_estimate=pl.CostEstimate(
            flops=0, bytes_accessed=2 * phase_step.size * 4, transcendentals=0
        ),
        name="unwrap",
    )(phase_step, wrap_count, filter_taps)

    halo_high, halo_low, halo_totals = pl.pallas_call(
        halo_kernel,
        out_shape=(
            pltpu.VMEM((cables, 2, time, LANES), jnp.bfloat16),
            pltpu.VMEM((cables, 2, time, LANES), jnp.bfloat16),
            pltpu.VMEM((2 * cables, LANES), jnp.float32),
        ),
        in_specs=[whole] * 2,
        out_specs=[whole] * 3,
        compiler_params=pltpu.CompilerParams(vmem_limit_bytes=8 << 20),
        name="halo",
    )(inner, outer)

    def filtered(part, weight):
        share = bounds[part + 1] - bounds[part]
        return pl.pallas_call(
            functools.partial(filter_kernel, bounds[part]),
            out_shape=pltpu.VMEM((share, blocks, time, LANES), jnp.float32),
            in_specs=[whole] * 5,
            out_specs=whole,
            compiler_params=pltpu.CompilerParams(vmem_limit_bytes=16 << 20),
            cost_estimate=pl.CostEstimate(
                flops=2 * share * (blocks + 2) * time * 8 * LANES * LANES,
                bytes_accessed=1 << 20,
                transcendentals=0,
            ),
            name="filter",
        )(high, low, halo_high, halo_low, weight)

    running = jnp.concatenate([totals, halo_totals], axis=0)
    received = [swapped(running, "tm", 1)]
    sums, halo_totals = lax.optimization_barrier((sums, halo_totals))
    rounds = [("chan", 1 << bit) for bit in range(places.bit_length() - 1)]
    rounds += [("tm", 1 << bit) for bit in range(steps.bit_length() - 1)]
    local, received_sums, chan_sums, ready = [], [], sums, None
    for number, (axis, bit) in enumerate(rounds):
        incoming = swapped(sums, axis, bit)
        if number % 2 == 0 and number > 0 and ready is not None:
            received.append(swapped(ready, "tm", 1 << len(received)))
            ready = None
        elif number > 0 and len(local) < parts:
            tied, sums = lax.optimization_barrier((weight, sums))
            part = filtered(len(local), tied)
            incoming, part = lax.optimization_barrier((incoming, part))
            local.append(part)
        if number % 2 == 1 and 1 << len(received) < steps:
            running = running + received[-1]
            ready, incoming = lax.optimization_barrier((running, incoming))
        if axis == "tm":
            received_sums.append(incoming)
        sums = sums + incoming
        if axis == "chan":
            chan_sums = sums
    while 1 << len(received) < steps:
        running = running + received[-1] if ready is None else ready
        ready = None
        received.append(swapped(running, "tm", 1 << len(received)))
    while len(local) < parts:
        local.append(filtered(len(local), weight))

    return pl.pallas_call(
        functools.partial(level_kernel, population),
        out_shape=jax.ShapeDtypeStruct(phase_step.shape, jnp.float32),
        in_specs=[
            [whole] * parts, whole, [whole] * len(received), whole, [whole] * len(received), scalars
        ],
        out_specs=outside,
        scratch_shapes=[
            pltpu.VMEM((cables, time, width), jnp.float32),
            pltpu.VMEM(((blocks + 2) * cables, LANES), jnp.float32),
            pltpu.SemaphoreType.DMA((cables, CHUNKS)),
        ],
        compiler_params=pltpu.CompilerParams(vmem_limit_bytes=24 << 20),
        name="level",
    )(local, weight, received, chan_sums, received_sums, coupling)


def solution(mesh):
    placed = (P(None, "tm", "chan"), P(None, "tm", "chan"), P(), P())
    return jax.shard_map(
        shards, mesh=mesh, in_specs=placed, out_specs=P(None, "tm", "chan"), check_vma=False
    )
```

```python
import functools
import math

import jax
import jax.numpy as jnp
from jax import lax
from jax.experimental import pallas as pl
from jax.experimental.pallas import tpu as pltpu
from jax.sharding import PartitionSpec as P

two_pi = 2.0 * math.pi
LANES = 128
HALF = LANES // 2
SUBLANES = 8
CHUNKS = 2


def shifted_down(value, amount):
    rows = lax.broadcasted_iota(jnp.int32, value.shape, 0)
    return jnp.where(rows >= amount, pltpu.roll(value, amount, 0), 0.0)


def scanned(pieces):
    sums, carry = [], None
    for value in pieces:
        amount = 1
        while amount < SUBLANES:
            value = value + shifted_down(value, amount)
            amount *= 2
        if carry is not None:
            value = value + carry
        carry = jnp.broadcast_to(value[SUBLANES - 1 :, :], value.shape)
        sums.append(value)
    return sums


def total(pieces):
    value = functools.reduce(jnp.add, pieces)
    return jnp.sum(value, axis=0, keepdims=True)


def split(value):
    high = value.astype(jnp.bfloat16)
    return high, (value - high.astype(jnp.float32)).astype(jnp.bfloat16)


def store_split(high_ref, low_ref, cable, block, sums):
    for pair in range(0, len(sums), 2):
        rows = pl.ds(pair * SUBLANES, 2 * SUBLANES)
        high, low = split(jnp.concatenate(sums[pair : pair + 2], axis=0))
        high_ref[cable, block, rows, :] = high
        low_ref[cable, block, rows, :] = low


def edges_kernel(phase_hbm, wrap_hbm, inner_ref, outer_ref, phase_ref, wrap_ref, sem):
    cables, time, width = phase_hbm.shape
    is_even = lax.rem(lax.axis_index("chan"), 2) == 0
    sends_last = (is_even, jnp.logical_not(is_even))
    copies = []
    for side, last in enumerate(sends_last):
        lanes = pl.ds(pl.multiple_of(jnp.where(last, width - LANES, 0), LANES), LANES)
        for kind, (source, target) in enumerate(((phase_hbm, phase_ref), (wrap_hbm, wrap_ref))):
            copies.append(
                pltpu.make_async_copy(source.at[:, :, lanes], target.at[side], sem.at[kind, side])
            )
    for copy in copies:
        copy.start()
    for copy in copies:
        copy.wait()
    lane = lax.broadcasted_iota(jnp.int32, (time, LANES), 1)
    for side, (last, target) in enumerate(zip(sends_last, (inner_ref, outer_ref))):
        for cable in range(cables // 2):
            low, high = (
                phase_ref[side, c] + two_pi * wrap_ref[side, c].astype(jnp.float32)
                for c in (cable, cable + cables // 2)
            )
            low = jnp.where(last, pltpu.roll(low, HALF, 1), low)
            high = jnp.where(last, high, pltpu.roll(high, HALF, 1))
            target[cable] = jnp.where(lane < HALF, low, high)


def increments_kernel(
    phase_ref, wrap_hbm, taps_ref, high_ref, low_ref, totals_ref, sums_ref, weight_ref, wrap_ref, sem
):
    cables, time, width = phase_ref.shape
    blocks = width // LANES
    groups = time // SUBLANES

    def copy(cable):
        return pltpu.make_async_copy(wrap_hbm.at[cable], wrap_ref.at[cable], sem.at[cable])

    for cable in range(cables):
        copy(cable).start()

    outputs = lax.broadcasted_iota(jnp.int32, (LANES, LANES), 0)
    inputs = lax.broadcasted_iota(jnp.int32, (LANES, LANES), 1)
    centre = (lax.broadcasted_iota(jnp.int32, (1, LANES), 1) == HALF).astype(jnp.float32)

    @pl.loop(0, cables)
    def _(cable):
        row = (centre - taps_ref[pl.ds(cable, 1), :]) * (1.0 / (4.0 * two_pi))
        circulant = pltpu.roll(
            jnp.broadcast_to(row, (LANES, LANES)), 0, 1, stride=1, stride_axis=0
        )
        first = jnp.where(inputs >= outputs, circulant, 0.0).T
        second = jnp.where(inputs < outputs, circulant, 0.0).T
        high, low = split(jnp.concatenate([first, second], axis=1))
        for place, part in enumerate((high, high, low, low)):
            weight_ref[cable, pl.ds(place * LANES, LANES), :] = part

    def cable_step(cable, accumulated):
        copy(cable).wait()

        def block_step(block, accumulated):
            lanes = pl.ds(pl.multiple_of(block * LANES, LANES), LANES)
            pieces = []
            for i in range(groups):
                rows = pl.ds(i * SUBLANES, SUBLANES)
                turns = wrap_ref[cable, rows, lanes].astype(jnp.float32)
                pieces.append(phase_ref[cable, rows, lanes] + two_pi * turns)
            store_split(high_ref, low_ref, cable, block, pieces)
            totals_ref[pl.ds(block * cables + cable, 1), :] = total(pieces)
            return tuple(a + b for a, b in zip(accumulated, pieces))

        return lax.fori_loop(0, blocks, block_step, accumulated, unroll=4)

    zeros = tuple(jnp.zeros((SUBLANES, LANES), jnp.float32) for _ in range(groups))
    accumulated = scanned(lax.fori_loop(0, cables, cable_step, zeros))
    lane = lax.broadcasted_iota(jnp.int32, (SUBLANES, LANES), 1)
    tile = jnp.zeros((SUBLANES, LANES), jnp.float32)
    for i, value in enumerate(accumulated):
        tile = jnp.where(lane == i, jnp.sum(value, axis=1, keepdims=True), tile)
    sums_ref[...] = tile


def halo_kernel(inner_ref, outer_ref, high_ref, low_ref, totals_ref):
    pairs, time, _ = inner_ref.shape
    cables = 2 * pairs
    groups = time // SUBLANES
    place = lax.axis_index("chan")
    is_even = lax.rem(place, 2) == 0
    at_end = (place == 0) | (place == lax.axis_size("chan") - 1)
    for pair in range(pairs):
        inner, outer = (
            [ref[pair, pl.ds(i * SUBLANES, SUBLANES), :] for i in range(groups)]
            for ref in (inner_ref, outer_ref)
        )
        outer = [jnp.where(at_end, 0.0, value) for value in outer]
        right = [jnp.where(is_even, a, b) for a, b in zip(inner, outer)]
        left = [jnp.where(is_even, b, a) for a, b in zip(inner, outer)]
        for block, pieces, moved in ((0, right, pair + pairs), (1, left, pair)):
            for cable in (pair, pair + pairs):
                placed = [pltpu.roll(v, HALF, 1) for v in pieces] if cable == moved else pieces
                store_split(high_ref, low_ref, cable, block, placed)
                totals_ref[pl.ds(block * cables + cable, 1), :] = total(placed)


def filter_kernel(first, high_ref, low_ref, halo_high_ref, halo_low_ref, weight_ref, local_ref):
    _, blocks, time, _ = high_ref.shape
    groups = time // SUBLANES
    lane = lax.broadcasted_iota(jnp.int32, (time, LANES), 1)

    @pl.loop(0, local_ref.shape[0])
    def _(index):
        cable = first + index
        high, low = (
            jnp.concatenate(
                [main[cable].reshape(blocks * time, LANES), halo[cable].reshape(2 * time, LANES)],
                axis=0,
            )
            for main, halo in ((high_ref, halo_high_ref), (low_ref, halo_low_ref))
        )
        product = jnp.dot(
            jnp.concatenate([high, low, high, low], axis=1),
            weight_ref[cable],
            preferred_element_type=jnp.float32,
        )

        def rolled(block):
            here = block if block >= 0 else blocks + 1
            there = block + 1
            return pltpu.roll(
                product[here * time : (here + 1) * time, :LANES]
                + product[there * time : (there + 1) * time, LANES:],
                HALF,
                1,
            )

        previous = rolled(-1)
        for block in range(blocks):
            following = rolled(block)
            value = jnp.where(lane < HALF, previous, following)
            pieces = [value[i * SUBLANES : (i + 1) * SUBLANES] for i in range(groups)]
            for i, piece in enumerate(scanned(pieces)):
                local_ref[index, block, pl.ds(i * SUBLANES, SUBLANES), :] = piece
            previous = following


def level_kernel(
    population, local_refs, weight_ref, totals_refs, sums_ref, earlier_refs, coupling_ref,
    out_hbm, stage_ref, offset_ref, sem,
):
    _, blocks, time, _ = local_refs[0].shape
    span = blocks * LANES // CHUNKS
    cables = out_hbm.shape[0]
    groups = time // SUBLANES
    step, place = lax.axis_index("tm"), lax.axis_index("chan")
    inside_left = jnp.where(place == 0, 0.0, 1.0)
    inside_right = jnp.where(place == lax.axis_size("chan") - 1, 0.0, 1.0)

    def from_earlier(refs):
        value = jnp.zeros(refs[0].shape, jnp.float32)
        for bit, ref in enumerate(refs):
            value = value + jnp.where((step & (1 << bit)) != 0, ref[...], 0.0)
        return value

    offset_ref[...] = from_earlier(totals_refs)
    earlier = from_earlier(earlier_refs)[SUBLANES - 1 :, groups - 1 : groups]
    common = (sums_ref[...] + earlier) * (1.0 / population)
    columns = [
        jnp.broadcast_to(common[:, i : i + 1], (SUBLANES, LANES)) for i in range(groups)
    ]
    used = blocks + 2
    padded = -(-(used + 1) // SUBLANES) * SUBLANES
    row = lax.broadcasted_iota(jnp.int32, (padded, LANES), 0)
    lane = lax.broadcasted_iota(jnp.int32, (padded, LANES), 1)

    def filtered_offset(cable):
        offset = jnp.concatenate(
            [
                offset_ref[pl.ds(cable, used, stride=cables), :],
                jnp.ones((padded - used, LANES), jnp.float32),
            ],
            axis=0,
        )
        high, low = split(offset)
        product = jnp.dot(
            jnp.concatenate([high, low, high, low], axis=1),
            weight_ref[cable],
            preferred_element_type=jnp.float32,
        )
        here, there = product[:, :LANES], product[:, LANES:]
        left = pltpu.roll(here[used - 1 : used] + there[:1], HALF, 1)
        following = pltpu.roll(here + pltpu.roll(there, padded - 1, 0), HALF, 1)
        previous = jnp.where(row == 0, left, pltpu.roll(following, 1, 0))
        bias = jnp.where(lane < HALF, previous, following)
        here, there = here[used : used + 1], there[used : used + 1]
        middle = pltpu.roll(here + there, HALF, 1)
        first = pltpu.roll(here * inside_left + there, HALF, 1)
        last = pltpu.roll(here + there * inside_right, HALF, 1)
        first = jnp.where(lane[:1] < HALF, first, middle)
        last = jnp.where(lane[:1] < HALF, middle, last)
        return bias, first, middle, last

    def written(cable, chunk):
        lanes = pl.ds(chunk * span, span)
        return pltpu.make_async_copy(
            stage_ref.at[cable, :, lanes], out_hbm.at[cable, :, lanes], sem.at[cable, chunk]
        )

    carry = filtered_offset(0)
    first_cable = 0
    for local_ref in local_refs:

        def cable_step(index, carry, first_cable=first_cable, local_ref=local_ref):
            cable = first_cable + index
            following = filtered_offset(jnp.minimum(cable + 1, cables - 1))
            bias, first, middle, last = carry
            shifts = [coupling_ref[cable] * column for column in columns]
            inner = [shift * middle for shift in shifts]
            for block in range(blocks):
                lanes = pl.ds(block * LANES, LANES)
                added = jnp.broadcast_to(bias[block : block + 1, :], (SUBLANES, LANES))
                if block == 0:
                    slopes = [shift * first for shift in shifts]
                elif block == blocks - 1:
                    slopes = [shift * last for shift in shifts]
                else:
                    slopes = inner
                for i in range(groups):
                    rows = pl.ds(i * SUBLANES, SUBLANES)
                    stage_ref[cable, rows, lanes] = local_ref[index, block, rows, :] + (
                        added - slopes[i]
                    )
                if (block + 1) % (blocks // CHUNKS) == 0:
                    written(cable, block // (blocks // CHUNKS)).start()
            return following

        carry = lax.fori_loop(0, local_ref.shape[0], cable_step, carry)
        first_cable += local_ref.shape[0]
    for cable in range(cables):
        for chunk in range(CHUNKS):
            written(cable, chunk).wait()


def swapped(value, axis, bit):
    return lax.ppermute(value, axis, [(i, i ^ bit) for i in range(lax.axis_size(axis))])


def shards(phase_step, wrap_count, coupling, filter_taps):
    cables, time, width = phase_step.shape
    blocks = width // LANES
    steps, places = lax.axis_size("tm"), lax.axis_size("chan")
    population = cables * width * places
    bounds = [0, 3 * cables // 8, 5 * cables // 8, cables]
    parts = len(bounds) - 1
    wrap_count = pltpu.with_memory_space_constraint(wrap_count, pltpu.HBM)
    whole = pl.BlockSpec(memory_space=pltpu.VMEM)
    outside = pl.BlockSpec(memory_space=pl.ANY)
    scalars = pl.BlockSpec(memory_space=pltpu.SMEM)

    inner, outer = pl.pallas_call(
        edges_kernel,
        out_shape=[pltpu.VMEM((cables // 2, time, LANES), jnp.float32)] * 2,
        in_specs=[outside] * 2,
        out_specs=[whole] * 2,
        scratch_shapes=[
            pltpu.VMEM((2, cables, time, LANES), jnp.float32),
            pltpu.VMEM((2, cables, time, LANES), jnp.int32),
            pltpu.SemaphoreType.DMA((2, 2)),
        ],
        compiler_params=pltpu.CompilerParams(vmem_limit_bytes=8 << 20),
        name="edges",
    )(pltpu.with_memory_space_constraint(phase_step, pltpu.HBM), wrap_count)
    outer_pairs = [(i, (i + (1 if i % 2 else -1)) % places) for i in range(places)]
    outer = lax.ppermute(outer, "chan", outer_pairs)
    inner = swapped(inner, "chan", 1)

    high, low, totals, sums, weight = pl.pallas_call(
        increments_kernel,
        out_shape=(
            pltpu.VMEM((cables, blocks, time, LANES), jnp.bfloat16),
            pltpu.VMEM((cables, blocks, time, LANES), jnp.bfloat16),
            pltpu.VMEM((blocks * cables, LANES), jnp.float32),
            pltpu.VMEM((SUBLANES, LANES), jnp.float32),
            pltpu.VMEM((cables, 4 * LANES, 2 * LANES), jnp.bfloat16),
        ),
        in_specs=[whole, outside, whole],
        out_specs=[whole] * 5,
        scratch_shapes=[
            pltpu.VMEM((cables, time, width), jnp.int32),
            pltpu.SemaphoreType.DMA((cables,)),
        ],
        compiler_params=pltpu.CompilerParams(vmem_limit_bytes=16 << 20),
        cost_estimate=pl.CostEstimate(
            flops=0, bytes_accessed=phase_step.size * 4, transcendentals=0
        ),
        name="increments",
    )(pltpu.with_memory_space_constraint(phase_step, pltpu.VMEM), wrap_count, filter_taps)

    halo_high, halo_low, halo_totals = pl.pallas_call(
        halo_kernel,
        out_shape=(
            pltpu.VMEM((cables, 2, time, LANES), jnp.bfloat16),
            pltpu.VMEM((cables, 2, time, LANES), jnp.bfloat16),
            pltpu.VMEM((2 * cables, LANES), jnp.float32),
        ),
        in_specs=[whole] * 2,
        out_specs=[whole] * 3,
        compiler_params=pltpu.CompilerParams(vmem_limit_bytes=8 << 20),
        name="halo",
    )(inner, outer)

    def filtered(part, weight):
        share = bounds[part + 1] - bounds[part]
        return pl.pallas_call(
            functools.partial(filter_kernel, bounds[part]),
            out_shape=pltpu.VMEM((share, blocks, time, LANES), jnp.float32),
            in_specs=[whole] * 5,
            out_specs=whole,
            compiler_params=pltpu.CompilerParams(vmem_limit_bytes=16 << 20),
            cost_estimate=pl.CostEstimate(
                flops=2 * share * (blocks + 2) * time * 8 * LANES * LANES,
                bytes_accessed=1 << 20,
                transcendentals=0,
            ),
            name="filter",
        )(high, low, halo_high, halo_low, weight)

    running = jnp.concatenate([totals, halo_totals], axis=0)
    received = [swapped(running, "tm", 1)]
    sums, halo_totals = lax.optimization_barrier((sums, halo_totals))
    rounds = [("chan", 1 << bit) for bit in range(places.bit_length() - 1)]
    rounds += [("tm", 1 << bit) for bit in range(steps.bit_length() - 1)]
    local, received_sums, chan_sums, ready = [], [], sums, None
    for number, (axis, bit) in enumerate(rounds):
        incoming = swapped(sums, axis, bit)
        if number % 2 == 0 and number > 0 and ready is not None:
            received.append(swapped(ready, "tm", 1 << len(received)))
            ready = None
        elif number > 0 and len(local) < parts:
            tied, sums = lax.optimization_barrier((weight, sums))
            part = filtered(len(local), tied)
            incoming, part = lax.optimization_barrier((incoming, part))
            local.append(part)
        if number % 2 == 1 and 1 << len(received) < steps:
            running = running + received[-1]
            ready, incoming = lax.optimization_barrier((running, incoming))
        if axis == "tm":
            received_sums.append(incoming)
        sums = sums + incoming
        if axis == "chan":
            chan_sums = sums
    while 1 << len(received) < steps:
        running = running + received[-1] if ready is None else ready
        ready = None
        received.append(swapped(running, "tm", 1 << len(received)))
    while len(local) < parts:
        local.append(filtered(len(local), weight))

    return pl.pallas_call(
        functools.partial(level_kernel, population),
        out_shape=jax.ShapeDtypeStruct(phase_step.shape, jnp.float32),
        in_specs=[
            [whole] * parts, whole, [whole] * len(received), whole, [whole] * len(received), scalars
        ],
        out_specs=outside,
        scratch_shapes=[
            pltpu.VMEM((cables, time, width), jnp.float32),
            pltpu.VMEM(((blocks + 2) * cables, LANES), jnp.float32),
            pltpu.SemaphoreType.DMA((cables, CHUNKS)),
        ],
        compiler_params=pltpu.CompilerParams(vmem_limit_bytes=24 << 20),
        name="level",
    )(local, weight, received, chan_sums, received_sums, coupling)


def solution(mesh):
    placed = (P(None, "tm", "chan"), P(None, "tm", "chan"), P(), P())
    return jax.shard_map(
        shards, mesh=mesh, in_specs=placed, out_specs=P(None, "tm", "chan"), check_vma=False
    )
```

```python
import functools
import math

import jax
import jax.numpy as jnp
from jax import lax
from jax.experimental import pallas as pl
from jax.experimental.pallas import tpu as pltpu
from jax.sharding import PartitionSpec as P

two_pi = 2.0 * math.pi
LANES = 128
HALF = LANES // 2
SUBLANES = 8
CHUNKS = 2


def shifted_down(value, amount):
    rows = lax.broadcasted_iota(jnp.int32, value.shape, 0)
    return jnp.where(rows >= amount, pltpu.roll(value, amount, 0), 0.0)


def scanned(pieces):
    sums, carry = [], None
    for value in pieces:
        amount = 1
        while amount < SUBLANES:
            value = value + shifted_down(value, amount)
            amount *= 2
        if carry is not None:
            value = value + carry
        carry = jnp.broadcast_to(value[SUBLANES - 1 :, :], value.shape)
        sums.append(value)
    return sums


def total(pieces):
    value = functools.reduce(jnp.add, pieces)
    return jnp.sum(value, axis=0, keepdims=True)


def split(value):
    high = value.astype(jnp.bfloat16)
    return high, (value - high.astype(jnp.float32)).astype(jnp.bfloat16)


def store_split(high_ref, low_ref, cable, block, sums):
    for pair in range(0, len(sums), 2):
        rows = pl.ds(pair * SUBLANES, 2 * SUBLANES)
        high, low = split(jnp.concatenate(sums[pair : pair + 2], axis=0))
        high_ref[cable, block, rows, :] = high
        low_ref[cable, block, rows, :] = low


def edges_kernel(phase_hbm, wrap_hbm, inner_ref, outer_ref, phase_ref, wrap_ref, sem):
    cables, time, width = phase_hbm.shape
    is_even = lax.rem(lax.axis_index("chan"), 2) == 0
    sends_last = (is_even, jnp.logical_not(is_even))
    copies = []
    for side, last in enumerate(sends_last):
        lanes = pl.ds(pl.multiple_of(jnp.where(last, width - LANES, 0), LANES), LANES)
        for kind, (source, target) in enumerate(((phase_hbm, phase_ref), (wrap_hbm, wrap_ref))):
            copies.append(
                pltpu.make_async_copy(source.at[:, :, lanes], target.at[side], sem.at[kind, side])
            )
    for copy in copies:
        copy.start()
    for copy in copies:
        copy.wait()
    lane = lax.broadcasted_iota(jnp.int32, (time, LANES), 1)
    for side, (last, target) in enumerate(zip(sends_last, (inner_ref, outer_ref))):
        for cable in range(cables // 2):
            low, high = (
                phase_ref[side, c] + two_pi * wrap_ref[side, c].astype(jnp.float32)
                for c in (cable, cable + cables // 2)
            )
            low = jnp.where(last, pltpu.roll(low, HALF, 1), low)
            high = jnp.where(last, high, pltpu.roll(high, HALF, 1))
            target[cable] = jnp.where(lane < HALF, low, high)


def increments_kernel(
    phase_ref, wrap_ref, taps_ref, high_ref, low_ref, totals_ref, sums_ref, weight_ref
):
    cables, time, width = phase_ref.shape
    blocks = width // LANES
    groups = time // SUBLANES

    outputs = lax.broadcasted_iota(jnp.int32, (LANES, LANES), 0)
    inputs = lax.broadcasted_iota(jnp.int32, (LANES, LANES), 1)
    centre = (lax.broadcasted_iota(jnp.int32, (1, LANES), 1) == HALF).astype(jnp.float32)

    @pl.loop(0, cables)
    def _(cable):
        row = (centre - taps_ref[pl.ds(cable, 1), :]) * (1.0 / (4.0 * two_pi))
        circulant = pltpu.roll(
            jnp.broadcast_to(row, (LANES, LANES)), 0, 1, stride=1, stride_axis=0
        )
        first = jnp.where(inputs >= outputs, circulant, 0.0).T
        second = jnp.where(inputs < outputs, circulant, 0.0).T
        high, low = split(jnp.concatenate([first, second], axis=1))
        for place, part in enumerate((high, high, low, low)):
            weight_ref[cable, pl.ds(place * LANES, LANES), :] = part

    def cable_step(cable, accumulated):
        def block_step(block, accumulated):
            lanes = pl.ds(pl.multiple_of(block * LANES, LANES), LANES)
            pieces = []
            for i in range(groups):
                rows = pl.ds(i * SUBLANES, SUBLANES)
                turns = wrap_ref[cable, rows, lanes].astype(jnp.float32)
                pieces.append(phase_ref[cable, rows, lanes] + two_pi * turns)
            store_split(high_ref, low_ref, cable, block, pieces)
            totals_ref[pl.ds(block * cables + cable, 1), :] = total(pieces)
            return tuple(a + b for a, b in zip(accumulated, pieces))

        return lax.fori_loop(0, blocks, block_step, accumulated, unroll=4)

    zeros = tuple(jnp.zeros((SUBLANES, LANES), jnp.float32) for _ in range(groups))
    accumulated = scanned(lax.fori_loop(0, cables, cable_step, zeros))
    lane = lax.broadcasted_iota(jnp.int32, (SUBLANES, LANES), 1)
    tile = jnp.zeros((SUBLANES, LANES), jnp.float32)
    for i, value in enumerate(accumulated):
        tile = jnp.where(lane == i, jnp.sum(value, axis=1, keepdims=True), tile)
    sums_ref[...] = tile


def halo_kernel(inner_ref, outer_ref, high_ref, low_ref, totals_ref):
    pairs, time, _ = inner_ref.shape
    cables = 2 * pairs
    groups = time // SUBLANES
    place = lax.axis_index("chan")
    is_even = lax.rem(place, 2) == 0
    at_end = (place == 0) | (place == lax.axis_size("chan") - 1)
    for pair in range(pairs):
        inner, outer = (
            [ref[pair, pl.ds(i * SUBLANES, SUBLANES), :] for i in range(groups)]
            for ref in (inner_ref, outer_ref)
        )
        outer = [jnp.where(at_end, 0.0, value) for value in outer]
        right = [jnp.where(is_even, a, b) for a, b in zip(inner, outer)]
        left = [jnp.where(is_even, b, a) for a, b in zip(inner, outer)]
        for block, pieces, moved in ((0, right, pair + pairs), (1, left, pair)):
            for cable in (pair, pair + pairs):
                placed = [pltpu.roll(v, HALF, 1) for v in pieces] if cable == moved else pieces
                store_split(high_ref, low_ref, cable, block, placed)
                totals_ref[pl.ds(block * cables + cable, 1), :] = total(placed)


def filter_kernel(first, high_ref, low_ref, halo_high_ref, halo_low_ref, weight_ref, local_ref):
    _, blocks, time, _ = high_ref.shape
    groups = time // SUBLANES
    lane = lax.broadcasted_iota(jnp.int32, (time, LANES), 1)

    @pl.loop(0, local_ref.shape[0])
    def _(index):
        cable = first + index
        high, low = (
            jnp.concatenate(
                [main[cable].reshape(blocks * time, LANES), halo[cable].reshape(2 * time, LANES)],
                axis=0,
            )
            for main, halo in ((high_ref, halo_high_ref), (low_ref, halo_low_ref))
        )
        product = jnp.dot(
            jnp.concatenate([high, low, high, low], axis=1),
            weight_ref[cable],
            preferred_element_type=jnp.float32,
        )

        def rolled(block):
            here = block if block >= 0 else blocks + 1
            there = block + 1
            return pltpu.roll(
                product[here * time : (here + 1) * time, :LANES]
                + product[there * time : (there + 1) * time, LANES:],
                HALF,
                1,
            )

        previous = rolled(-1)
        for block in range(blocks):
            following = rolled(block)
            value = jnp.where(lane < HALF, previous, following)
            pieces = [value[i * SUBLANES : (i + 1) * SUBLANES] for i in range(groups)]
            for i, piece in enumerate(scanned(pieces)):
                local_ref[index, block, pl.ds(i * SUBLANES, SUBLANES), :] = piece
            previous = following


def level_kernel(
    population, local_refs, weight_ref, totals_refs, sums_ref, earlier_refs, coupling_ref,
    out_hbm, stage_ref, offset_ref, sem,
):
    _, blocks, time, _ = local_refs[0].shape
    span = blocks * LANES // CHUNKS
    cables = out_hbm.shape[0]
    groups = time // SUBLANES
    step, place = lax.axis_index("tm"), lax.axis_index("chan")
    inside_left = jnp.where(place == 0, 0.0, 1.0)
    inside_right = jnp.where(place == lax.axis_size("chan") - 1, 0.0, 1.0)

    def from_earlier(refs):
        value = jnp.zeros(refs[0].shape, jnp.float32)
        for bit, ref in enumerate(refs):
            value = value + jnp.where((step & (1 << bit)) != 0, ref[...], 0.0)
        return value

    offset_ref[...] = from_earlier(totals_refs)
    earlier = from_earlier(earlier_refs)[SUBLANES - 1 :, groups - 1 : groups]
    common = (sums_ref[...] + earlier) * (1.0 / population)
    columns = [
        jnp.broadcast_to(common[:, i : i + 1], (SUBLANES, LANES)) for i in range(groups)
    ]
    used = blocks + 2
    padded = -(-(used + 1) // SUBLANES) * SUBLANES
    row = lax.broadcasted_iota(jnp.int32, (padded, LANES), 0)
    lane = lax.broadcasted_iota(jnp.int32, (padded, LANES), 1)

    def filtered_offset(cable):
        offset = jnp.concatenate(
            [
                offset_ref[pl.ds(cable, used, stride=cables), :],
                jnp.ones((padded - used, LANES), jnp.float32),
            ],
            axis=0,
        )
        high, low = split(offset)
        product = jnp.dot(
            jnp.concatenate([high, low, high, low], axis=1),
            weight_ref[cable],
            preferred_element_type=jnp.float32,
        )
        here, there = product[:, :LANES], product[:, LANES:]
        left = pltpu.roll(here[used - 1 : used] + there[:1], HALF, 1)
        following = pltpu.roll(here + pltpu.roll(there, padded - 1, 0), HALF, 1)
        previous = jnp.where(row == 0, left, pltpu.roll(following, 1, 0))
        bias = jnp.where(lane < HALF, previous, following)
        here, there = here[used : used + 1], there[used : used + 1]
        middle = pltpu.roll(here + there, HALF, 1)
        first = pltpu.roll(here * inside_left + there, HALF, 1)
        last = pltpu.roll(here + there * inside_right, HALF, 1)
        first = jnp.where(lane[:1] < HALF, first, middle)
        last = jnp.where(lane[:1] < HALF, middle, last)
        return bias, first, middle, last

    def written(cable, chunk):
        lanes = pl.ds(chunk * span, span)
        return pltpu.make_async_copy(
            stage_ref.at[cable, :, lanes], out_hbm.at[cable, :, lanes], sem.at[cable, chunk]
        )

    carry = filtered_offset(0)
    first_cable = 0
    for local_ref in local_refs:

        def cable_step(index, carry, first_cable=first_cable, local_ref=local_ref):
            cable = first_cable + index
            following = filtered_offset(jnp.minimum(cable + 1, cables - 1))
            bias, first, middle, last = carry
            shifts = [coupling_ref[cable] * column for column in columns]
            inner = [shift * middle for shift in shifts]
            for block in range(blocks):
                lanes = pl.ds(block * LANES, LANES)
                added = jnp.broadcast_to(bias[block : block + 1, :], (SUBLANES, LANES))
                if block == 0:
                    slopes = [shift * first for shift in shifts]
                elif block == blocks - 1:
                    slopes = [shift * last for shift in shifts]
                else:
                    slopes = inner
                for i in range(groups):
                    rows = pl.ds(i * SUBLANES, SUBLANES)
                    stage_ref[cable, rows, lanes] = local_ref[index, block, rows, :] + (
                        added - slopes[i]
                    )
                if (block + 1) % (blocks // CHUNKS) == 0:
                    written(cable, block // (blocks // CHUNKS)).start()
            return following

        carry = lax.fori_loop(0, local_ref.shape[0], cable_step, carry)
        first_cable += local_ref.shape[0]
    for cable in range(cables):
        for chunk in range(CHUNKS):
            written(cable, chunk).wait()


def swapped(value, axis, bit):
    return lax.ppermute(value, axis, [(i, i ^ bit) for i in range(lax.axis_size(axis))])


def shards(phase_step, wrap_count, coupling, filter_taps):
    cables, time, width = phase_step.shape
    blocks = width // LANES
    steps, places = lax.axis_size("tm"), lax.axis_size("chan")
    population = cables * width * places
    bounds = [0, 3 * cables // 8, 5 * cables // 8, cables]
    parts = len(bounds) - 1
    whole = pl.BlockSpec(memory_space=pltpu.VMEM)
    outside = pl.BlockSpec(memory_space=pl.ANY)
    scalars = pl.BlockSpec(memory_space=pltpu.SMEM)

    inner, outer = pl.pallas_call(
        edges_kernel,
        out_shape=[pltpu.VMEM((cables // 2, time, LANES), jnp.float32)] * 2,
        in_specs=[outside] * 2,
        out_specs=[whole] * 2,
        scratch_shapes=[
            pltpu.VMEM((2, cables, time, LANES), jnp.float32),
            pltpu.VMEM((2, cables, time, LANES), jnp.int32),
            pltpu.SemaphoreType.DMA((2, 2)),
        ],
        compiler_params=pltpu.CompilerParams(vmem_limit_bytes=8 << 20),
        name="edges",
    )(
        pltpu.with_memory_space_constraint(phase_step, pltpu.HBM),
        pltpu.with_memory_space_constraint(wrap_count, pltpu.HBM),
    )
    outer_pairs = [(i, (i + (1 if i % 2 else -1)) % places) for i in range(places)]
    outer = lax.ppermute(outer, "chan", outer_pairs)
    inner = swapped(inner, "chan", 1)

    high, low, totals, sums, weight = pl.pallas_call(
        increments_kernel,
        out_shape=(
            pltpu.VMEM((cables, blocks, time, LANES), jnp.bfloat16),
            pltpu.VMEM((cables, blocks, time, LANES), jnp.bfloat16),
            pltpu.VMEM((blocks * cables, LANES), jnp.float32),
            pltpu.VMEM((SUBLANES, LANES), jnp.float32),
            pltpu.VMEM((cables, 4 * LANES, 2 * LANES), jnp.bfloat16),
        ),
        in_specs=[whole, whole, whole],
        out_specs=[whole] * 5,
        compiler_params=pltpu.CompilerParams(vmem_limit_bytes=8 << 20),
        cost_estimate=pl.CostEstimate(flops=0, bytes_accessed=1 << 20, transcendentals=0),
        name="increments",
    )(
        pltpu.with_memory_space_constraint(phase_step, pltpu.VMEM),
        pltpu.with_memory_space_constraint(wrap_count, pltpu.VMEM),
        filter_taps,
    )

    halo_high, halo_low, halo_totals = pl.pallas_call(
        halo_kernel,
        out_shape=(
            pltpu.VMEM((cables, 2, time, LANES), jnp.bfloat16),
            pltpu.VMEM((cables, 2, time, LANES), jnp.bfloat16),
            pltpu.VMEM((2 * cables, LANES), jnp.float32),
        ),
        in_specs=[whole] * 2,
        out_specs=[whole] * 3,
        compiler_params=pltpu.CompilerParams(vmem_limit_bytes=8 << 20),
        name="halo",
    )(inner, outer)

    def filtered(part, weight):
        share = bounds[part + 1] - bounds[part]
        return pl.pallas_call(
            functools.partial(filter_kernel, bounds[part]),
            out_shape=pltpu.VMEM((share, blocks, time, LANES), jnp.float32),
            in_specs=[whole] * 5,
            out_specs=whole,
            compiler_params=pltpu.CompilerParams(vmem_limit_bytes=16 << 20),
            cost_estimate=pl.CostEstimate(
                flops=2 * share * (blocks + 2) * time * 8 * LANES * LANES,
                bytes_accessed=1 << 20,
                transcendentals=0,
            ),
            name="filter",
        )(high, low, halo_high, halo_low, weight)

    running = jnp.concatenate([totals, halo_totals], axis=0)
    received = [swapped(running, "tm", 1)]
    sums, halo_totals = lax.optimization_barrier((sums, halo_totals))
    rounds = [("chan", 1 << bit) for bit in range(places.bit_length() - 1)]
    rounds += [("tm", 1 << bit) for bit in range(steps.bit_length() - 1)]
    local, received_sums, chan_sums, ready = [], [], sums, None
    for number, (axis, bit) in enumerate(rounds):
        incoming = swapped(sums, axis, bit)
        if number % 2 == 0 and number > 0 and ready is not None:
            received.append(swapped(ready, "tm", 1 << len(received)))
            ready = None
        elif number > 0 and len(local) < parts:
            tied, sums = lax.optimization_barrier((weight, sums))
            part = filtered(len(local), tied)
            incoming, part = lax.optimization_barrier((incoming, part))
            local.append(part)
        if number % 2 == 1 and 1 << len(received) < steps:
            running = running + received[-1]
            ready, incoming = lax.optimization_barrier((running, incoming))
        if axis == "tm":
            received_sums.append(incoming)
        sums = sums + incoming
        if axis == "chan":
            chan_sums = sums
    while 1 << len(received) < steps:
        running = running + received[-1] if ready is None else ready
        ready = None
        received.append(swapped(running, "tm", 1 << len(received)))
    while len(local) < parts:
        local.append(filtered(len(local), weight))

    return pl.pallas_call(
        functools.partial(level_kernel, population),
        out_shape=jax.ShapeDtypeStruct(phase_step.shape, jnp.float32),
        in_specs=[
            [whole] * parts, whole, [whole] * len(received), whole, [whole] * len(received), scalars
        ],
        out_specs=outside,
        scratch_shapes=[
            pltpu.VMEM((cables, time, width), jnp.float32),
            pltpu.VMEM(((blocks + 2) * cables, LANES), jnp.float32),
            pltpu.SemaphoreType.DMA((cables, CHUNKS)),
        ],
        compiler_params=pltpu.CompilerParams(vmem_limit_bytes=24 << 20),
        name="level",
    )(local, weight, received, chan_sums, received_sums, coupling)


def solution(mesh):
    placed = (P(None, "tm", "chan"), P(None, "tm", "chan"), P(), P())
    return jax.shard_map(
        shards, mesh=mesh, in_specs=placed, out_specs=P(None, "tm", "chan"), check_vma=False
    )
```

```python
import functools
import math

import jax
import jax.numpy as jnp
from jax import lax
from jax.experimental import pallas as pl
from jax.experimental.pallas import tpu as pltpu
from jax.sharding import PartitionSpec as P

two_pi = 2.0 * math.pi
LANES = 128
HALF = LANES // 2
SUBLANES = 8
CHUNKS = 4


def shifted_down(value, amount):
    rows = lax.broadcasted_iota(jnp.int32, value.shape, 0)
    return jnp.where(rows >= amount, pltpu.roll(value, amount, 0), 0.0)


def scanned(pieces):
    sums, carry = [], None
    for value in pieces:
        amount = 1
        while amount < SUBLANES:
            value = value + shifted_down(value, amount)
            amount *= 2
        if carry is not None:
            value = value + carry
        carry = jnp.broadcast_to(value[SUBLANES - 1 :, :], value.shape)
        sums.append(value)
    return sums


def total(pieces):
    value = functools.reduce(jnp.add, pieces)
    return jnp.sum(value, axis=0, keepdims=True)


def split(value):
    high = value.astype(jnp.bfloat16)
    return high, (value - high.astype(jnp.float32)).astype(jnp.bfloat16)


def store_split(high_ref, low_ref, cable, block, sums):
    for pair in range(0, len(sums), 2):
        rows = pl.ds(pair * SUBLANES, 2 * SUBLANES)
        high, low = split(jnp.concatenate(sums[pair : pair + 2], axis=0))
        high_ref[cable, block, rows, :] = high
        low_ref[cable, block, rows, :] = low


def edges_kernel(phase_hbm, wrap_hbm, inner_ref, outer_ref, phase_ref, wrap_ref, sem):
    cables, time, width = phase_hbm.shape
    is_even = lax.rem(lax.axis_index("chan"), 2) == 0
    sends_last = (is_even, jnp.logical_not(is_even))
    copies = []
    for side, last in enumerate(sends_last):
        lanes = pl.ds(pl.multiple_of(jnp.where(last, width - LANES, 0), LANES), LANES)
        for kind, (source, target) in enumerate(((phase_hbm, phase_ref), (wrap_hbm, wrap_ref))):
            copies.append(
                pltpu.make_async_copy(source.at[:, :, lanes], target.at[side], sem.at[kind, side])
            )
    for copy in copies:
        copy.start()
    for copy in copies:
        copy.wait()
    lane = lax.broadcasted_iota(jnp.int32, (time, LANES), 1)
    for side, (last, target) in enumerate(zip(sends_last, (inner_ref, outer_ref))):
        for cable in range(cables // 2):
            low, high = (
                phase_ref[side, c] + two_pi * wrap_ref[side, c].astype(jnp.float32)
                for c in (cable, cable + cables // 2)
            )
            low = jnp.where(last, pltpu.roll(low, HALF, 1), low)
            high = jnp.where(last, high, pltpu.roll(high, HALF, 1))
            target[cable] = jnp.where(lane < HALF, low, high)


def backwards(value):
    lane = lax.broadcasted_iota(jnp.int32, value.shape, 1)
    bit = 1
    while bit < LANES:
        value = jnp.where(
            (lane & bit) == 0, pltpu.roll(value, LANES - bit, 1), pltpu.roll(value, bit, 1)
        )
        bit *= 2
    return value


def increments_kernel(
    phase_ref, wrap_hbm, taps_ref, high_ref, low_ref, totals_ref, sums_ref, weight_ref, wrap_ref, sem
):
    cables, time, width = phase_ref.shape
    blocks = width // LANES
    groups = time // SUBLANES

    def copy(cable):
        return pltpu.make_async_copy(wrap_hbm.at[cable], wrap_ref.at[cable], sem.at[cable])

    for cable in range(cables):
        copy(cable).start()

    lane = lax.broadcasted_iota(jnp.int32, taps_ref.shape, 1)
    taps = jnp.where(lane == HALF, 1.0, 0.0) - taps_ref[...]
    reversed_taps = pltpu.roll(backwards(taps * (1.0 / (4.0 * two_pi))), 1, 1)
    inputs = lax.broadcasted_iota(jnp.int32, (LANES, LANES), 0)
    outputs = lax.broadcasted_iota(jnp.int32, (LANES, LANES), 1)
    for cable in range(cables):
        row = jnp.broadcast_to(reversed_taps[cable : cable + 1, :], (LANES, LANES))
        circulant = pltpu.roll(row, 0, 1, stride=1, stride_axis=0)
        for column, mask in enumerate((inputs >= outputs, inputs < outputs)):
            high, low = split(jnp.where(mask, circulant, 0.0))
            for place, part in enumerate((high, high, low, low)):
                rows, lanes = pl.ds(place * LANES, LANES), pl.ds(column * LANES, LANES)
                weight_ref[cable, rows, lanes] = part

    def cable_step(cable, accumulated):
        copy(cable).wait()

        def block_step(block, accumulated):
            lanes = pl.ds(pl.multiple_of(block * LANES, LANES), LANES)
            pieces = []
            for i in range(groups):
                rows = pl.ds(i * SUBLANES, SUBLANES)
                turns = wrap_ref[cable, rows, lanes].astype(jnp.float32)
                pieces.append(phase_ref[cable, rows, lanes] + two_pi * turns)
            store_split(high_ref, low_ref, cable, block, pieces)
            totals_ref[pl.ds(block * cables + cable, 1), :] = total(pieces)
            return tuple(a + b for a, b in zip(accumulated, pieces))

        return lax.fori_loop(0, blocks, block_step, accumulated, unroll=4)

    zeros = tuple(jnp.zeros((SUBLANES, LANES), jnp.float32) for _ in range(groups))
    accumulated = scanned(lax.fori_loop(0, cables, cable_step, zeros))
    lane = lax.broadcasted_iota(jnp.int32, (SUBLANES, LANES), 1)
    tile = jnp.zeros((SUBLANES, LANES), jnp.float32)
    for i, value in enumerate(accumulated):
        tile = jnp.where(lane == i, jnp.sum(value, axis=1, keepdims=True), tile)
    sums_ref[...] = tile


def halo_kernel(inner_ref, outer_ref, high_ref, low_ref, totals_ref):
    pairs, time, _ = inner_ref.shape
    cables = 2 * pairs
    groups = time // SUBLANES
    place = lax.axis_index("chan")
    is_even = lax.rem(place, 2) == 0
    at_end = (place == 0) | (place == lax.axis_size("chan") - 1)
    for pair in range(pairs):
        inner, outer = (
            [ref[pair, pl.ds(i * SUBLANES, SUBLANES), :] for i in range(groups)]
            for ref in (inner_ref, outer_ref)
        )
        outer = [jnp.where(at_end, 0.0, value) for value in outer]
        right = [jnp.where(is_even, a, b) for a, b in zip(inner, outer)]
        left = [jnp.where(is_even, b, a) for a, b in zip(inner, outer)]
        for block, pieces, moved in ((0, right, pair + pairs), (1, left, pair)):
            for cable in (pair, pair + pairs):
                placed = [pltpu.roll(v, HALF, 1) for v in pieces] if cable == moved else pieces
                store_split(high_ref, low_ref, cable, block, placed)
                totals_ref[pl.ds(block * cables + cable, 1), :] = total(placed)


def filter_kernel(first, high_ref, low_ref, halo_high_ref, halo_low_ref, weight_ref, local_ref):
    _, blocks, time, _ = high_ref.shape
    groups = time // SUBLANES
    lane = lax.broadcasted_iota(jnp.int32, (time, LANES), 1)

    @pl.loop(0, local_ref.shape[0])
    def _(index):
        cable = first + index
        high, low = (
            jnp.concatenate(
                [main[cable].reshape(blocks * time, LANES), halo[cable].reshape(2 * time, LANES)],
                axis=0,
            )
            for main, halo in ((high_ref, halo_high_ref), (low_ref, halo_low_ref))
        )
        product = jnp.dot(
            jnp.concatenate([high, low, high, low], axis=1),
            weight_ref[cable],
            preferred_element_type=jnp.float32,
        )

        def rolled(block):
            here = block if block >= 0 else blocks + 1
            there = block + 1
            return pltpu.roll(
                product[here * time : (here + 1) * time, :LANES]
                + product[there * time : (there + 1) * time, LANES:],
                HALF,
                1,
            )

        previous = rolled(-1)
        for block in range(blocks):
            following = rolled(block)
            value = jnp.where(lane < HALF, previous, following)
            pieces = [value[i * SUBLANES : (i + 1) * SUBLANES] for i in range(groups)]
            for i, piece in enumerate(scanned(pieces)):
                local_ref[index, block, pl.ds(i * SUBLANES, SUBLANES), :] = piece
            previous = following


def level_kernel(
    population, local_refs, weight_ref, totals_refs, sums_ref, earlier_refs, coupling_ref,
    out_hbm, stage_ref, offset_ref, sem,
):
    _, blocks, time, _ = local_refs[0].shape
    span = blocks * LANES // CHUNKS
    cables = out_hbm.shape[0]
    groups = time // SUBLANES
    step, place = lax.axis_index("tm"), lax.axis_index("chan")
    inside_left = jnp.where(place == 0, 0.0, 1.0)
    inside_right = jnp.where(place == lax.axis_size("chan") - 1, 0.0, 1.0)

    def from_earlier(refs):
        value = jnp.zeros(refs[0].shape, jnp.float32)
        for bit, ref in enumerate(refs):
            value = value + jnp.where((step & (1 << bit)) != 0, ref[...], 0.0)
        return value

    offset_ref[...] = from_earlier(totals_refs)
    earlier = from_earlier(earlier_refs)[SUBLANES - 1 :, groups - 1 : groups]
    common = (sums_ref[...] + earlier) * (1.0 / population)
    columns = [
        jnp.broadcast_to(common[:, i : i + 1], (SUBLANES, LANES)) for i in range(groups)
    ]
    used = blocks + 2
    padded = -(-(used + 1) // SUBLANES) * SUBLANES
    row = lax.broadcasted_iota(jnp.int32, (padded, LANES), 0)
    lane = lax.broadcasted_iota(jnp.int32, (padded, LANES), 1)

    def filtered_offset(cable):
        offset = jnp.concatenate(
            [
                offset_ref[pl.ds(cable, used, stride=cables), :],
                jnp.ones((padded - used, LANES), jnp.float32),
            ],
            axis=0,
        )
        high, low = split(offset)
        product = jnp.dot(
            jnp.concatenate([high, low, high, low], axis=1),
            weight_ref[cable],
            preferred_element_type=jnp.float32,
        )
        here, there = product[:, :LANES], product[:, LANES:]
        left = pltpu.roll(here[used - 1 : used] + there[:1], HALF, 1)
        following = pltpu.roll(here + pltpu.roll(there, padded - 1, 0), HALF, 1)
        previous = jnp.where(row == 0, left, pltpu.roll(following, 1, 0))
        bias = jnp.where(lane < HALF, previous, following)
        here, there = here[used : used + 1], there[used : used + 1]
        middle = pltpu.roll(here + there, HALF, 1)
        first = pltpu.roll(here * inside_left + there, HALF, 1)
        last = pltpu.roll(here + there * inside_right, HALF, 1)
        first = jnp.where(lane[:1] < HALF, first, middle)
        last = jnp.where(lane[:1] < HALF, middle, last)
        return bias, first, middle, last

    def written(cable, chunk):
        lanes = pl.ds(chunk * span, span)
        return pltpu.make_async_copy(
            stage_ref.at[cable, :, lanes], out_hbm.at[cable, :, lanes], sem.at[cable, chunk]
        )

    carry = filtered_offset(0)
    first_cable = 0
    for local_ref in local_refs:

        def cable_step(index, carry, first_cable=first_cable, local_ref=local_ref):
            cable = first_cable + index
            following = filtered_offset(jnp.minimum(cable + 1, cables - 1))
            bias, first, middle, last = carry
            shifts = [coupling_ref[cable] * column for column in columns]
            inner = [shift * middle for shift in shifts]
            for block in range(blocks):
                lanes = pl.ds(block * LANES, LANES)
                added = jnp.broadcast_to(bias[block : block + 1, :], (SUBLANES, LANES))
                if block == 0:
                    slopes = [shift * first for shift in shifts]
                elif block == blocks - 1:
                    slopes = [shift * last for shift in shifts]
                else:
                    slopes = inner
                for i in range(groups):
                    rows = pl.ds(i * SUBLANES, SUBLANES)
                    stage_ref[cable, rows, lanes] = local_ref[index, block, rows, :] + (
                        added - slopes[i]
                    )
                if (block + 1) % (blocks // CHUNKS) == 0:
                    written(cable, block // (blocks // CHUNKS)).start()
            return following

        carry = lax.fori_loop(0, local_ref.shape[0], cable_step, carry)
        first_cable += local_ref.shape[0]
    for cable in range(cables):
        for chunk in range(CHUNKS):
            written(cable, chunk).wait()


def swapped(value, axis, bit):
    return lax.ppermute(value, axis, [(i, i ^ bit) for i in range(lax.axis_size(axis))])


def shards(phase_step, wrap_count, coupling, filter_taps):
    cables, time, width = phase_step.shape
    blocks = width // LANES
    steps, places = lax.axis_size("tm"), lax.axis_size("chan")
    population = cables * width * places
    bounds = [0, cables // 2, 3 * cables // 4, cables]
    parts = len(bounds) - 1
    wrap_count = pltpu.with_memory_space_constraint(wrap_count, pltpu.HBM)
    whole = pl.BlockSpec(memory_space=pltpu.VMEM)
    outside = pl.BlockSpec(memory_space=pl.ANY)
    scalars = pl.BlockSpec(memory_space=pltpu.SMEM)

    inner, outer = pl.pallas_call(
        edges_kernel,
        out_shape=[pltpu.VMEM((cables // 2, time, LANES), jnp.float32)] * 2,
        in_specs=[outside] * 2,
        out_specs=[whole] * 2,
        scratch_shapes=[
            pltpu.VMEM((2, cables, time, LANES), jnp.float32),
            pltpu.VMEM((2, cables, time, LANES), jnp.int32),
            pltpu.SemaphoreType.DMA((2, 2)),
        ],
        compiler_params=pltpu.CompilerParams(vmem_limit_bytes=8 << 20),
        name="edges",
    )(pltpu.with_memory_space_constraint(phase_step, pltpu.HBM), wrap_count)
    outer_pairs = [(i, (i + (1 if i % 2 else -1)) % places) for i in range(places)]
    outer = lax.ppermute(outer, "chan", outer_pairs)
    inner = swapped(inner, "chan", 1)

    high, low, totals, sums, weight = pl.pallas_call(
        increments_kernel,
        out_shape=(
            pltpu.VMEM((cables, blocks, time, LANES), jnp.bfloat16),
            pltpu.VMEM((cables, blocks, time, LANES), jnp.bfloat16),
            pltpu.VMEM((blocks * cables, LANES), jnp.float32),
            pltpu.VMEM((SUBLANES, LANES), jnp.float32),
            pltpu.VMEM((cables, 4 * LANES, 2 * LANES), jnp.bfloat16),
        ),
        in_specs=[whole, outside, whole],
        out_specs=[whole] * 5,
        scratch_shapes=[
            pltpu.VMEM((cables, time, width), jnp.int32),
            pltpu.SemaphoreType.DMA((cables,)),
        ],
        compiler_params=pltpu.CompilerParams(vmem_limit_bytes=16 << 20),
        cost_estimate=pl.CostEstimate(
            flops=0, bytes_accessed=phase_step.size * 4, transcendentals=0
        ),
        name="increments",
    )(pltpu.with_memory_space_constraint(phase_step, pltpu.VMEM), wrap_count, filter_taps)

    halo_high, halo_low, halo_totals = pl.pallas_call(
        halo_kernel,
        out_shape=(
            pltpu.VMEM((cables, 2, time, LANES), jnp.bfloat16),
            pltpu.VMEM((cables, 2, time, LANES), jnp.bfloat16),
            pltpu.VMEM((2 * cables, LANES), jnp.float32),
        ),
        in_specs=[whole] * 2,
        out_specs=[whole] * 3,
        compiler_params=pltpu.CompilerParams(vmem_limit_bytes=8 << 20),
        name="halo",
    )(inner, outer)

    def filtered(part, weight):
        share = bounds[part + 1] - bounds[part]
        return pl.pallas_call(
            functools.partial(filter_kernel, bounds[part]),
            out_shape=pltpu.VMEM((share, blocks, time, LANES), jnp.float32),
            in_specs=[whole] * 5,
            out_specs=whole,
            compiler_params=pltpu.CompilerParams(vmem_limit_bytes=16 << 20),
            cost_estimate=pl.CostEstimate(
                flops=2 * share * (blocks + 2) * time * 8 * LANES * LANES,
                bytes_accessed=1 << 20,
                transcendentals=0,
            ),
            name="filter",
        )(high, low, halo_high, halo_low, weight)

    running = jnp.concatenate([totals, halo_totals], axis=0)
    received = [swapped(running, "tm", 1)]
    sums, halo_totals = lax.optimization_barrier((sums, halo_totals))
    rounds = [("chan", 1 << bit) for bit in range(places.bit_length() - 1)]
    rounds += [("tm", 1 << bit) for bit in range(steps.bit_length() - 1)]
    local, received_sums, chan_sums, ready = [], [], sums, None
    for number, (axis, bit) in enumerate(rounds):
        incoming = swapped(sums, axis, bit)
        if number % 2 == 0 and number > 0 and ready is not None:
            received.append(swapped(ready, "tm", 1 << len(received)))
            ready = None
        elif number > 0 and len(local) < parts:
            tied, sums = lax.optimization_barrier((weight, sums))
            part = filtered(len(local), tied)
            incoming, part = lax.optimization_barrier((incoming, part))
            local.append(part)
        if number % 2 == 1 and 1 << len(received) < steps:
            running = running + received[-1]
            ready, incoming = lax.optimization_barrier((running, incoming))
        if axis == "tm":
            received_sums.append(incoming)
        sums = sums + incoming
        if axis == "chan":
            chan_sums = sums
    while 1 << len(received) < steps:
        running = running + received[-1] if ready is None else ready
        ready = None
        received.append(swapped(running, "tm", 1 << len(received)))
    while len(local) < parts:
        local.append(filtered(len(local), weight))

    return pl.pallas_call(
        functools.partial(level_kernel, population),
        out_shape=jax.ShapeDtypeStruct(phase_step.shape, jnp.float32),
        in_specs=[
            [whole] * parts, whole, [whole] * len(received), whole, [whole] * len(received), scalars
        ],
        out_specs=outside,
        scratch_shapes=[
            pltpu.VMEM((cables, time, width), jnp.float32),
            pltpu.VMEM(((blocks + 2) * cables, LANES), jnp.float32),
            pltpu.SemaphoreType.DMA((cables, CHUNKS)),
        ],
        compiler_params=pltpu.CompilerParams(vmem_limit_bytes=24 << 20),
        name="level",
    )(local, weight, received, chan_sums, received_sums, coupling)


def solution(mesh):
    placed = (P(None, "tm", "chan"), P(None, "tm", "chan"), P(), P())
    return jax.shard_map(
        shards, mesh=mesh, in_specs=placed, out_specs=P(None, "tm", "chan"), check_vma=False
    )
```

```python
import functools
import math

import jax
import jax.numpy as jnp
from jax import lax
from jax.experimental import pallas as pl
from jax.experimental.pallas import tpu as pltpu
from jax.sharding import PartitionSpec as P

two_pi = 2.0 * math.pi
LANES = 128
HALF = LANES // 2
SUBLANES = 8
CHUNKS = 2


def shifted_down(value, amount):
    rows = lax.broadcasted_iota(jnp.int32, value.shape, 0)
    return jnp.where(rows >= amount, pltpu.roll(value, amount, 0), 0.0)


def scanned(pieces):
    sums, carry = [], None
    for value in pieces:
        amount = 1
        while amount < SUBLANES:
            value = value + shifted_down(value, amount)
            amount *= 2
        if carry is not None:
            value = value + carry
        carry = jnp.broadcast_to(value[SUBLANES - 1 :, :], value.shape)
        sums.append(value)
    return sums


def total(pieces):
    value = functools.reduce(jnp.add, pieces)
    return jnp.sum(value, axis=0, keepdims=True)


def split(value):
    high = value.astype(jnp.bfloat16)
    return high, (value - high.astype(jnp.float32)).astype(jnp.bfloat16)


def store_split(high_ref, low_ref, cable, block, sums):
    for pair in range(0, len(sums), 2):
        rows = pl.ds(pair * SUBLANES, 2 * SUBLANES)
        high, low = split(jnp.concatenate(sums[pair : pair + 2], axis=0))
        high_ref[cable, block, rows, :] = high
        low_ref[cable, block, rows, :] = low


def edges_kernel(phase_hbm, wrap_hbm, inner_ref, outer_ref, phase_ref, wrap_ref, sem):
    cables, time, width = phase_hbm.shape
    is_even = lax.rem(lax.axis_index("chan"), 2) == 0
    sends_last = (is_even, jnp.logical_not(is_even))
    copies = []
    for side, last in enumerate(sends_last):
        lanes = pl.ds(pl.multiple_of(jnp.where(last, width - LANES, 0), LANES), LANES)
        for kind, (source, target) in enumerate(((phase_hbm, phase_ref), (wrap_hbm, wrap_ref))):
            copies.append(
                pltpu.make_async_copy(source.at[:, :, lanes], target.at[side], sem.at[kind, side])
            )
    for copy in copies:
        copy.start()
    for copy in copies:
        copy.wait()
    lane = lax.broadcasted_iota(jnp.int32, (time, LANES), 1)
    for side, (last, target) in enumerate(zip(sends_last, (inner_ref, outer_ref))):
        for cable in range(cables // 2):
            low, high = (
                phase_ref[side, c] + two_pi * wrap_ref[side, c].astype(jnp.float32)
                for c in (cable, cable + cables // 2)
            )
            low = jnp.where(last, pltpu.roll(low, HALF, 1), low)
            high = jnp.where(last, high, pltpu.roll(high, HALF, 1))
            target[cable] = jnp.where(lane < HALF, low, high)


def backwards(value):
    lane = lax.broadcasted_iota(jnp.int32, value.shape, 1)
    bit = 1
    while bit < LANES:
        value = jnp.where(
            (lane & bit) == 0, pltpu.roll(value, LANES - bit, 1), pltpu.roll(value, bit, 1)
        )
        bit *= 2
    return value


def increments_kernel(
    phase_ref, wrap_hbm, taps_ref, high_ref, low_ref, totals_ref, sums_ref, weight_ref, wrap_ref,
    reversed_ref, sem,
):
    cables, time, width = phase_ref.shape
    blocks = width // LANES
    groups = time // SUBLANES

    def copy(cable):
        return pltpu.make_async_copy(wrap_hbm.at[cable], wrap_ref.at[cable], sem.at[cable])

    for cable in range(cables):
        copy(cable).start()

    lane = lax.broadcasted_iota(jnp.int32, taps_ref.shape, 1)
    taps = jnp.where(lane == HALF, 1.0, 0.0) - taps_ref[...]
    reversed_ref[...] = pltpu.roll(backwards(taps * (1.0 / (4.0 * two_pi))), 1, 1)
    inputs = lax.broadcasted_iota(jnp.int32, (LANES, LANES), 0)
    outputs = lax.broadcasted_iota(jnp.int32, (LANES, LANES), 1)

    @pl.loop(0, cables)
    def _(cable):
        row = jnp.broadcast_to(reversed_ref[pl.ds(cable, 1), :], (LANES, LANES))
        circulant = pltpu.roll(row, 0, 1, stride=1, stride_axis=0)
        for column, mask in enumerate((inputs >= outputs, inputs < outputs)):
            high, low = split(jnp.where(mask, circulant, 0.0))
            for place, part in enumerate((high, high, low, low)):
                rows, lanes = pl.ds(place * LANES, LANES), pl.ds(column * LANES, LANES)
                weight_ref[cable, rows, lanes] = part

    def cable_step(cable, accumulated):
        copy(cable).wait()

        def block_step(block, accumulated):
            lanes = pl.ds(pl.multiple_of(block * LANES, LANES), LANES)
            pieces = []
            for i in range(groups):
                rows = pl.ds(i * SUBLANES, SUBLANES)
                turns = wrap_ref[cable, rows, lanes].astype(jnp.float32)
                pieces.append(phase_ref[cable, rows, lanes] + two_pi * turns)
            store_split(high_ref, low_ref, cable, block, pieces)
            totals_ref[pl.ds(block * cables + cable, 1), :] = total(pieces)
            return tuple(a + b for a, b in zip(accumulated, pieces))

        return lax.fori_loop(0, blocks, block_step, accumulated, unroll=16)

    zeros = tuple(jnp.zeros((SUBLANES, LANES), jnp.float32) for _ in range(groups))
    accumulated = scanned(lax.fori_loop(0, cables, cable_step, zeros))
    lane = lax.broadcasted_iota(jnp.int32, (SUBLANES, LANES), 1)
    tile = jnp.zeros((SUBLANES, LANES), jnp.float32)
    for i, value in enumerate(accumulated):
        tile = jnp.where(lane == i, jnp.sum(value, axis=1, keepdims=True), tile)
    sums_ref[...] = tile


def halo_kernel(inner_ref, outer_ref, high_ref, low_ref, totals_ref):
    pairs, time, _ = inner_ref.shape
    cables = 2 * pairs
    groups = time // SUBLANES
    place = lax.axis_index("chan")
    is_even = lax.rem(place, 2) == 0
    at_end = (place == 0) | (place == lax.axis_size("chan") - 1)
    for pair in range(pairs):
        inner, outer = (
            [ref[pair, pl.ds(i * SUBLANES, SUBLANES), :] for i in range(groups)]
            for ref in (inner_ref, outer_ref)
        )
        outer = [jnp.where(at_end, 0.0, value) for value in outer]
        right = [jnp.where(is_even, a, b) for a, b in zip(inner, outer)]
        left = [jnp.where(is_even, b, a) for a, b in zip(inner, outer)]
        for block, pieces, moved in ((0, right, pair + pairs), (1, left, pair)):
            for cable in (pair, pair + pairs):
                placed = [pltpu.roll(v, HALF, 1) for v in pieces] if cable == moved else pieces
                store_split(high_ref, low_ref, cable, block, placed)
                totals_ref[pl.ds(block * cables + cable, 1), :] = total(placed)


def filter_kernel(first, high_ref, low_ref, halo_high_ref, halo_low_ref, weight_ref, local_ref):
    _, blocks, time, _ = high_ref.shape
    groups = time // SUBLANES
    lane = lax.broadcasted_iota(jnp.int32, (time, LANES), 1)

    @pl.loop(0, local_ref.shape[0])
    def _(index):
        cable = first + index
        high, low = (
            jnp.concatenate(
                [main[cable].reshape(blocks * time, LANES), halo[cable].reshape(2 * time, LANES)],
                axis=0,
            )
            for main, halo in ((high_ref, halo_high_ref), (low_ref, halo_low_ref))
        )
        product = jnp.dot(
            jnp.concatenate([high, low, high, low], axis=1),
            weight_ref[cable],
            preferred_element_type=jnp.float32,
        )

        def rolled(block):
            here = block if block >= 0 else blocks + 1
            there = block + 1
            return pltpu.roll(
                product[here * time : (here + 1) * time, :LANES]
                + product[there * time : (there + 1) * time, LANES:],
                HALF,
                1,
            )

        previous = rolled(-1)
        for block in range(blocks):
            following = rolled(block)
            value = jnp.where(lane < HALF, previous, following)
            pieces = [value[i * SUBLANES : (i + 1) * SUBLANES] for i in range(groups)]
            for i, piece in enumerate(scanned(pieces)):
                local_ref[index, block, pl.ds(i * SUBLANES, SUBLANES), :] = piece
            previous = following


def level_kernel(
    population, local_refs, weight_ref, totals_refs, sums_ref, earlier_refs, coupling_ref,
    out_hbm, stage_ref, offset_ref, sem,
):
    _, blocks, time, _ = local_refs[0].shape
    span = blocks * LANES // CHUNKS
    cables = out_hbm.shape[0]
    groups = time // SUBLANES
    step, place = lax.axis_index("tm"), lax.axis_index("chan")
    inside_left = jnp.where(place == 0, 0.0, 1.0)
    inside_right = jnp.where(place == lax.axis_size("chan") - 1, 0.0, 1.0)

    def from_earlier(refs):
        value = jnp.zeros(refs[0].shape, jnp.float32)
        for bit, ref in enumerate(refs):
            value = value + jnp.where((step & (1 << bit)) != 0, ref[...], 0.0)
        return value

    offset_ref[...] = from_earlier(totals_refs)
    earlier = from_earlier(earlier_refs)[SUBLANES - 1 :, groups - 1 : groups]
    common = (sums_ref[...] + earlier) * (1.0 / population)
    columns = [
        jnp.broadcast_to(common[:, i : i + 1], (SUBLANES, LANES)) for i in range(groups)
    ]
    used = blocks + 2
    padded = -(-(used + 1) // SUBLANES) * SUBLANES
    row = lax.broadcasted_iota(jnp.int32, (padded, LANES), 0)
    lane = lax.broadcasted_iota(jnp.int32, (padded, LANES), 1)

    def filtered_offset(cable):
        offset = jnp.concatenate(
            [
                offset_ref[pl.ds(cable, used, stride=cables), :],
                jnp.ones((padded - used, LANES), jnp.float32),
            ],
            axis=0,
        )
        high, low = split(offset)
        product = jnp.dot(
            jnp.concatenate([high, low, high, low], axis=1),
            weight_ref[cable],
            preferred_element_type=jnp.float32,
        )
        here, there = product[:, :LANES], product[:, LANES:]
        left = pltpu.roll(here[used - 1 : used] + there[:1], HALF, 1)
        following = pltpu.roll(here + pltpu.roll(there, padded - 1, 0), HALF, 1)
        previous = jnp.where(row == 0, left, pltpu.roll(following, 1, 0))
        bias = jnp.where(lane < HALF, previous, following)
        here, there = here[used : used + 1], there[used : used + 1]
        middle = pltpu.roll(here + there, HALF, 1)
        first = pltpu.roll(here * inside_left + there, HALF, 1)
        last = pltpu.roll(here + there * inside_right, HALF, 1)
        first = jnp.where(lane[:1] < HALF, first, middle)
        last = jnp.where(lane[:1] < HALF, middle, last)
        return bias, first, middle, last

    def written(cable, chunk):
        lanes = pl.ds(chunk * span, span)
        return pltpu.make_async_copy(
            stage_ref.at[cable, :, lanes], out_hbm.at[cable, :, lanes], sem.at[cable, chunk]
        )

    carry = filtered_offset(0)
    first_cable = 0
    for local_ref in local_refs:

        def cable_step(index, carry, first_cable=first_cable, local_ref=local_ref):
            cable = first_cable + index
            following = filtered_offset(jnp.minimum(cable + 1, cables - 1))
            bias, first, middle, last = carry
            shifts = [coupling_ref[cable] * column for column in columns]
            inner = [shift * middle for shift in shifts]
            for block in range(blocks):
                lanes = pl.ds(block * LANES, LANES)
                added = jnp.broadcast_to(bias[block : block + 1, :], (SUBLANES, LANES))
                if block == 0:
                    slopes = [shift * first for shift in shifts]
                elif block == blocks - 1:
                    slopes = [shift * last for shift in shifts]
                else:
                    slopes = inner
                for i in range(groups):
                    rows = pl.ds(i * SUBLANES, SUBLANES)
                    stage_ref[cable, rows, lanes] = local_ref[index, block, rows, :] + (
                        added - slopes[i]
                    )
                if (block + 1) % (blocks // CHUNKS) == 0:
                    written(cable, block // (blocks // CHUNKS)).start()
            return following

        carry = lax.fori_loop(0, local_ref.shape[0], cable_step, carry)
        first_cable += local_ref.shape[0]
    for cable in range(cables):
        for chunk in range(CHUNKS):
            written(cable, chunk).wait()


def swapped(value, axis, bit):
    return lax.ppermute(value, axis, [(i, i ^ bit) for i in range(lax.axis_size(axis))])


def shards(phase_step, wrap_count, coupling, filter_taps):
    cables, time, width = phase_step.shape
    blocks = width // LANES
    steps, places = lax.axis_size("tm"), lax.axis_size("chan")
    population = cables * width * places
    bounds = [0, cables // 2, 3 * cables // 4, cables]
    parts = len(bounds) - 1
    wrap_count = pltpu.with_memory_space_constraint(wrap_count, pltpu.HBM)
    whole = pl.BlockSpec(memory_space=pltpu.VMEM)
    outside = pl.BlockSpec(memory_space=pl.ANY)
    scalars = pl.BlockSpec(memory_space=pltpu.SMEM)

    inner, outer = pl.pallas_call(
        edges_kernel,
        out_shape=[pltpu.VMEM((cables // 2, time, LANES), jnp.float32)] * 2,
        in_specs=[outside] * 2,
        out_specs=[whole] * 2,
        scratch_shapes=[
            pltpu.VMEM((2, cables, time, LANES), jnp.float32),
            pltpu.VMEM((2, cables, time, LANES), jnp.int32),
            pltpu.SemaphoreType.DMA((2, 2)),
        ],
        compiler_params=pltpu.CompilerParams(vmem_limit_bytes=8 << 20),
        name="edges",
    )(pltpu.with_memory_space_constraint(phase_step, pltpu.HBM), wrap_count)
    last = places - 1
    outer_pairs = [(0, 0), (last, last)] + [(i, i + (1 if i % 2 else -1)) for i in range(1, last)]
    outer = lax.ppermute(outer, "chan", outer_pairs)
    inner = swapped(inner, "chan", 1)

    high, low, totals, sums, weight = pl.pallas_call(
        increments_kernel,
        out_shape=(
            pltpu.VMEM((cables, blocks, time, LANES), jnp.bfloat16),
            pltpu.VMEM((cables, blocks, time, LANES), jnp.bfloat16),
            pltpu.VMEM((blocks * cables, LANES), jnp.float32),
            pltpu.VMEM((SUBLANES, LANES), jnp.float32),
            pltpu.VMEM((cables, 4 * LANES, 2 * LANES), jnp.bfloat16),
        ),
        in_specs=[whole, outside, whole],
        out_specs=[whole] * 5,
        scratch_shapes=[
            pltpu.VMEM((cables, time, width), jnp.int32),
            pltpu.VMEM(filter_taps.shape, jnp.float32),
            pltpu.SemaphoreType.DMA((cables,)),
        ],
        compiler_params=pltpu.CompilerParams(vmem_limit_bytes=16 << 20),
        cost_estimate=pl.CostEstimate(
            flops=0, bytes_accessed=phase_step.size * 4, transcendentals=0
        ),
        name="increments",
    )(pltpu.with_memory_space_constraint(phase_step, pltpu.VMEM), wrap_count, filter_taps)

    halo_high, halo_low, halo_totals = pl.pallas_call(
        halo_kernel,
        out_shape=(
            pltpu.VMEM((cables, 2, time, LANES), jnp.bfloat16),
            pltpu.VMEM((cables, 2, time, LANES), jnp.bfloat16),
            pltpu.VMEM((2 * cables, LANES), jnp.float32),
        ),
        in_specs=[whole] * 2,
        out_specs=[whole] * 3,
        compiler_params=pltpu.CompilerParams(vmem_limit_bytes=8 << 20),
        name="halo",
    )(inner, outer)

    def filtered(part, weight):
        share = bounds[part + 1] - bounds[part]
        return pl.pallas_call(
            functools.partial(filter_kernel, bounds[part]),
            out_shape=pltpu.VMEM((share, blocks, time, LANES), jnp.float32),
            in_specs=[whole] * 5,
            out_specs=whole,
            compiler_params=pltpu.CompilerParams(vmem_limit_bytes=16 << 20),
            cost_estimate=pl.CostEstimate(
                flops=2 * share * (blocks + 2) * time * 8 * LANES * LANES,
                bytes_accessed=1 << 20,
                transcendentals=0,
            ),
            name="filter",
        )(high, low, halo_high, halo_low, weight)

    running = jnp.concatenate([totals, halo_totals], axis=0)
    received = [swapped(running, "tm", 1)]
    sums, halo_totals = lax.optimization_barrier((sums, halo_totals))
    rounds = [("chan", 1 << bit) for bit in range(places.bit_length() - 1)]
    rounds += [("tm", 1 << bit) for bit in range(steps.bit_length() - 1)]
    local, received_sums, chan_sums, ready = [], [], sums, None
    for number, (axis, bit) in enumerate(rounds):
        incoming = swapped(sums, axis, bit)
        if number % 2 == 0 and number > 0 and ready is not None:
            received.append(swapped(ready, "tm", 1 << len(received)))
            ready = None
        elif number > 0 and len(local) < parts:
            tied, sums = lax.optimization_barrier((weight, sums))
            part = filtered(len(local), tied)
            incoming, part = lax.optimization_barrier((incoming, part))
            local.append(part)
        if number % 2 == 1 and 1 << len(received) < steps:
            running = running + received[-1]
            ready, incoming = lax.optimization_barrier((running, incoming))
        if axis == "tm":
            received_sums.append(incoming)
        sums = sums + incoming
        if axis == "chan":
            chan_sums = sums
    while 1 << len(received) < steps:
        running = running + received[-1] if ready is None else ready
        ready = None
        received.append(swapped(running, "tm", 1 << len(received)))
    while len(local) < parts:
        local.append(filtered(len(local), weight))

    return pl.pallas_call(
        functools.partial(level_kernel, population),
        out_shape=jax.ShapeDtypeStruct(phase_step.shape, jnp.float32),
        in_specs=[
            [whole] * parts, whole, [whole] * len(received), whole, [whole] * len(received), scalars
        ],
        out_specs=outside,
        scratch_shapes=[
            pltpu.VMEM((cables, time, width), jnp.float32),
            pltpu.VMEM(((blocks + 2) * cables, LANES), jnp.float32),
            pltpu.SemaphoreType.DMA((cables, CHUNKS)),
        ],
        compiler_params=pltpu.CompilerParams(vmem_limit_bytes=24 << 20),
        name="level",
    )(local, weight, received, chan_sums, received_sums, coupling)


def solution(mesh):
    placed = (P(None, "tm", "chan"), P(None, "tm", "chan"), P(), P())
    return jax.shard_map(
        shards, mesh=mesh, in_specs=placed, out_specs=P(None, "tm", "chan"), check_vma=False
    )
```

```python
import functools
import math

import jax
import jax.numpy as jnp
from jax import lax
from jax.experimental import pallas as pl
from jax.experimental.pallas import tpu as pltpu
from jax.sharding import PartitionSpec as P

two_pi = 2.0 * math.pi
LANES = 128
HALF = LANES // 2
SUBLANES = 8
CHUNKS = 2


def shifted_down(value, amount):
    rows = lax.broadcasted_iota(jnp.int32, value.shape, 0)
    return jnp.where(rows >= amount, pltpu.roll(value, amount, 0), 0.0)


def scanned(pieces):
    sums, carry = [], None
    for value in pieces:
        amount = 1
        while amount < SUBLANES:
            value = value + shifted_down(value, amount)
            amount *= 2
        if carry is not None:
            value = value + carry
        carry = jnp.broadcast_to(value[SUBLANES - 1 :, :], value.shape)
        sums.append(value)
    return sums


def total(pieces):
    value = functools.reduce(jnp.add, pieces)
    return jnp.sum(value, axis=0, keepdims=True)


def split(value):
    high = value.astype(jnp.bfloat16)
    return high, (value - high.astype(jnp.float32)).astype(jnp.bfloat16)


def store_split(high_ref, low_ref, cable, block, sums):
    for pair in range(0, len(sums), 2):
        rows = pl.ds(pair * SUBLANES, 2 * SUBLANES)
        high, low = split(jnp.concatenate(sums[pair : pair + 2], axis=0))
        high_ref[cable, block, rows, :] = high
        low_ref[cable, block, rows, :] = low


def edges_kernel(phase_hbm, wrap_hbm, inner_ref, outer_ref, phase_ref, wrap_ref, sem):
    cables, time, width = phase_hbm.shape
    is_even = lax.rem(lax.axis_index("chan"), 2) == 0
    sends_last = (is_even, jnp.logical_not(is_even))
    copies = []
    for side, last in enumerate(sends_last):
        lanes = pl.ds(pl.multiple_of(jnp.where(last, width - LANES, 0), LANES), LANES)
        for kind, (source, target) in enumerate(((phase_hbm, phase_ref), (wrap_hbm, wrap_ref))):
            copies.append(
                pltpu.make_async_copy(source.at[:, :, lanes], target.at[side], sem.at[kind, side])
            )
    for copy in copies:
        copy.start()
    for copy in copies:
        copy.wait()
    lane = lax.broadcasted_iota(jnp.int32, (time, LANES), 1)
    for side, (last, target) in enumerate(zip(sends_last, (inner_ref, outer_ref))):
        for cable in range(cables // 2):
            low, high = (
                phase_ref[side, c] + two_pi * wrap_ref[side, c].astype(jnp.float32)
                for c in (cable, cable + cables // 2)
            )
            low = jnp.where(last, pltpu.roll(low, HALF, 1), low)
            high = jnp.where(last, high, pltpu.roll(high, HALF, 1))
            target[cable] = jnp.where(lane < HALF, low, high)


def backwards(value):
    lane = lax.broadcasted_iota(jnp.int32, value.shape, 1)
    bit = 1
    while bit < LANES:
        value = jnp.where(
            (lane & bit) == 0, pltpu.roll(value, LANES - bit, 1), pltpu.roll(value, bit, 1)
        )
        bit *= 2
    return value


def increments(phase_ref, wrap_ref, cable, lanes):
    pieces = []
    for i in range(phase_ref.shape[1] // SUBLANES):
        rows = pl.ds(i * SUBLANES, SUBLANES)
        turns = wrap_ref[cable, rows, lanes].astype(jnp.float32)
        pieces.append(phase_ref[cable, rows, lanes] + two_pi * turns)
    return pieces


def totals_kernel(phase_ref, wrap_hbm, totals_ref, sums_ref, wrap_ref, sem):
    cables, time, width = phase_ref.shape
    blocks = width // LANES
    groups = time // SUBLANES

    def copy(cable):
        return pltpu.make_async_copy(wrap_hbm.at[cable], wrap_ref.at[cable], sem.at[cable])

    for cable in range(cables):
        copy(cable).start()

    def cable_step(cable, accumulated):
        copy(cable).wait()

        def block_step(block, accumulated):
            lanes = pl.ds(pl.multiple_of(block * LANES, LANES), LANES)
            pieces = increments(phase_ref, wrap_ref, cable, lanes)
            totals_ref[pl.ds(block * cables + cable, 1), :] = total(pieces)
            return tuple(a + b for a, b in zip(accumulated, pieces))

        return lax.fori_loop(0, blocks, block_step, accumulated, unroll=16)

    zeros = tuple(jnp.zeros((SUBLANES, LANES), jnp.float32) for _ in range(groups))
    accumulated = scanned(lax.fori_loop(0, cables, cable_step, zeros))
    lane = lax.broadcasted_iota(jnp.int32, (SUBLANES, LANES), 1)
    tile = jnp.zeros((SUBLANES, LANES), jnp.float32)
    for i, value in enumerate(accumulated):
        tile = jnp.where(lane == i, jnp.sum(value, axis=1, keepdims=True), tile)
    for device in range(sums_ref.shape[0]):
        sums_ref[device] = tile


def halo_kernel(inner_ref, outer_ref, high_ref, low_ref, totals_ref):
    pairs, time, _ = inner_ref.shape
    cables = 2 * pairs
    groups = time // SUBLANES
    place = lax.axis_index("chan")
    is_even = lax.rem(place, 2) == 0
    at_end = (place == 0) | (place == lax.axis_size("chan") - 1)
    for pair in range(pairs):
        inner, outer = (
            [ref[pair, pl.ds(i * SUBLANES, SUBLANES), :] for i in range(groups)]
            for ref in (inner_ref, outer_ref)
        )
        outer = [jnp.where(at_end, 0.0, value) for value in outer]
        right = [jnp.where(is_even, a, b) for a, b in zip(inner, outer)]
        left = [jnp.where(is_even, b, a) for a, b in zip(inner, outer)]
        for block, pieces, moved in ((0, right, pair + pairs), (1, left, pair)):
            for cable in (pair, pair + pairs):
                placed = [pltpu.roll(v, HALF, 1) for v in pieces] if cable == moved else pieces
                store_split(high_ref, low_ref, cable, block, placed)
                totals_ref[pl.ds(block * cables + cable, 1), :] = total(placed)


def filter_kernel(
    phase_hbm, wrap_hbm, halo_high_ref, halo_low_ref, taps_ref, local_ref, weight_ref,
    phase_ref, wrap_ref, even_high_ref, even_low_ref, odd_high_ref, odd_low_ref, reversed_ref, sem,
):
    cables, time, width = phase_hbm.shape
    blocks = width // LANES
    groups = time // SUBLANES

    def copies(cable):
        return (
            pltpu.make_async_copy(phase_hbm.at[cable], phase_ref.at[cable], sem.at[0, cable]),
            pltpu.make_async_copy(wrap_hbm.at[cable], wrap_ref.at[cable], sem.at[1, cable]),
        )

    for cable in range(cables):
        for copy in copies(cable):
            copy.start()

    lane = lax.broadcasted_iota(jnp.int32, taps_ref.shape, 1)
    taps = jnp.where(lane == HALF, 1.0, 0.0) - taps_ref[...]
    reversed_ref[...] = pltpu.roll(backwards(taps * (1.0 / (4.0 * two_pi))), 1, 1)
    inputs = lax.broadcasted_iota(jnp.int32, (LANES, LANES), 0)
    outputs = lax.broadcasted_iota(jnp.int32, (LANES, LANES), 1)

    @pl.loop(0, cables)
    def _(cable):
        row = jnp.broadcast_to(reversed_ref[pl.ds(cable, 1), :], (LANES, LANES))
        circulant = pltpu.roll(row, 0, 1, stride=1, stride_axis=0)
        for column, mask in enumerate((inputs >= outputs, inputs < outputs)):
            high, low = split(jnp.where(mask, circulant, 0.0))
            for place, part in enumerate((high, high, low, low)):
                rows, lanes = pl.ds(place * LANES, LANES), pl.ds(column * LANES, LANES)
                weight_ref[cable, rows, lanes] = part

    lane = lax.broadcasted_iota(jnp.int32, (time, LANES), 1)
    even, odd = (even_high_ref, even_low_ref), (odd_high_ref, odd_low_ref)

    def prepare(cable, parts):
        for copy in copies(cable):
            copy.wait()
        for block in range(blocks):
            pieces = increments(phase_ref, wrap_ref, cable, pl.ds(block * LANES, LANES))
            store_split(*parts, 0, block, pieces)

    def emit(cable, parts):
        high, low = (
            jnp.concatenate(
                [main[0].reshape(blocks * time, LANES), halo[cable].reshape(2 * time, LANES)],
                axis=0,
            )
            for main, halo in zip(parts, (halo_high_ref, halo_low_ref))
        )
        product = jnp.dot(
            jnp.concatenate([high, low, high, low], axis=1),
            weight_ref[cable],
            preferred_element_type=jnp.float32,
        )

        def rolled(block):
            here = block if block >= 0 else blocks + 1
            there = block + 1
            return pltpu.roll(
                product[here * time : (here + 1) * time, :LANES]
                + product[there * time : (there + 1) * time, LANES:],
                HALF,
                1,
            )

        previous = rolled(-1)
        for block in range(blocks):
            following = rolled(block)
            value = jnp.where(lane < HALF, previous, following)
            pieces = [value[i * SUBLANES : (i + 1) * SUBLANES] for i in range(groups)]
            for i, piece in enumerate(scanned(pieces)):
                local_ref[cable, block, pl.ds(i * SUBLANES, SUBLANES), :] = piece
            previous = following

    prepare(0, even)

    @pl.loop(0, cables // 2 - 1)
    def _(pair):
        cable = 2 * pair
        prepare(cable + 1, odd)
        emit(cable, even)
        prepare(cable + 2, even)
        emit(cable + 1, odd)

    prepare(cables - 1, odd)
    emit(cables - 2, even)
    emit(cables - 1, odd)


def level_kernel(
    population, local_ref, weight_ref, totals_refs, sums_ref, coupling_ref,
    out_hbm, stage_ref, offset_ref, sem,
):
    _, blocks, time, _ = local_ref.shape
    span = blocks * LANES // CHUNKS
    cables = out_hbm.shape[0]
    groups = time // SUBLANES
    step, place = lax.axis_index("tm"), lax.axis_index("chan")
    inside_left = jnp.where(place == 0, 0.0, 1.0)
    inside_right = jnp.where(place == lax.axis_size("chan") - 1, 0.0, 1.0)

    offset = jnp.zeros(offset_ref.shape, jnp.float32)
    for bit, ref in enumerate(totals_refs):
        offset = offset + jnp.where((step & (1 << bit)) != 0, ref[...], 0.0)
    offset_ref[...] = offset
    common = jnp.zeros((SUBLANES, LANES), jnp.float32)
    before = jnp.zeros((SUBLANES, LANES), jnp.float32)
    for number in range(sums_ref.shape[0]):
        gathered = jnp.sum(sums_ref[number], axis=0)
        common = common + jnp.where(step == number, gathered, 0.0)
        before = before + jnp.where(step > number, gathered, 0.0)
    common = (common + before[SUBLANES - 1 :, groups - 1 : groups]) * (1.0 / population)
    columns = [
        jnp.broadcast_to(common[:, i : i + 1], (SUBLANES, LANES)) for i in range(groups)
    ]
    used = blocks + 2
    padded = -(-(used + 1) // SUBLANES) * SUBLANES
    row = lax.broadcasted_iota(jnp.int32, (padded, LANES), 0)
    lane = lax.broadcasted_iota(jnp.int32, (padded, LANES), 1)

    def filtered_offset(cable):
        offset = jnp.concatenate(
            [
                offset_ref[pl.ds(cable, used, stride=cables), :],
                jnp.ones((padded - used, LANES), jnp.float32),
            ],
            axis=0,
        )
        high, low = split(offset)
        product = jnp.dot(
            jnp.concatenate([high, low, high, low], axis=1),
            weight_ref[cable],
            preferred_element_type=jnp.float32,
        )
        here, there = product[:, :LANES], product[:, LANES:]
        left = pltpu.roll(here[used - 1 : used] + there[:1], HALF, 1)
        following = pltpu.roll(here + pltpu.roll(there, padded - 1, 0), HALF, 1)
        previous = jnp.where(row == 0, left, pltpu.roll(following, 1, 0))
        bias = jnp.where(lane < HALF, previous, following)
        here, there = here[used : used + 1], there[used : used + 1]
        middle = pltpu.roll(here + there, HALF, 1)
        first = pltpu.roll(here * inside_left + there, HALF, 1)
        last = pltpu.roll(here + there * inside_right, HALF, 1)
        first = jnp.where(lane[:1] < HALF, first, middle)
        last = jnp.where(lane[:1] < HALF, middle, last)
        return bias, first, middle, last

    def written(cable, chunk):
        lanes = pl.ds(chunk * span, span)
        return pltpu.make_async_copy(
            stage_ref.at[cable, :, lanes], out_hbm.at[cable, :, lanes], sem.at[cable, chunk]
        )

    carry = filtered_offset(0)

    def cable_step(cable, carry):
        following = filtered_offset(jnp.minimum(cable + 1, cables - 1))
        bias, first, middle, last = carry
        shifts = [coupling_ref[cable] * column for column in columns]
        inner = [shift * middle for shift in shifts]
        for block in range(blocks):
            lanes = pl.ds(block * LANES, LANES)
            added = jnp.broadcast_to(bias[block : block + 1, :], (SUBLANES, LANES))
            if block == 0:
                slopes = [shift * first for shift in shifts]
            elif block == blocks - 1:
                slopes = [shift * last for shift in shifts]
            else:
                slopes = inner
            for i in range(groups):
                rows = pl.ds(i * SUBLANES, SUBLANES)
                stage_ref[cable, rows, lanes] = local_ref[cable, block, rows, :] + (
                    added - slopes[i]
                )
            if (block + 1) % (blocks // CHUNKS) == 0:
                written(cable, block // (blocks // CHUNKS)).start()
        return following

    lax.fori_loop(0, cables, cable_step, carry)
    for cable in range(cables):
        for chunk in range(CHUNKS):
            written(cable, chunk).wait()


def swapped(value, axis, bit):
    return lax.ppermute(value, axis, [(i, i ^ bit) for i in range(lax.axis_size(axis))])


def shards(phase_step, wrap_count, coupling, filter_taps):
    cables, time, width = phase_step.shape
    blocks = width // LANES
    steps, places = lax.axis_size("tm"), lax.axis_size("chan")
    population = cables * width * places
    wrap_count = pltpu.with_memory_space_constraint(wrap_count, pltpu.HBM)
    whole = pl.BlockSpec(memory_space=pltpu.VMEM)
    outside = pl.BlockSpec(memory_space=pl.ANY)
    scalars = pl.BlockSpec(memory_space=pltpu.SMEM)

    inner, outer = pl.pallas_call(
        edges_kernel,
        out_shape=[pltpu.VMEM((cables // 2, time, LANES), jnp.float32)] * 2,
        in_specs=[outside] * 2,
        out_specs=[whole] * 2,
        scratch_shapes=[
            pltpu.VMEM((2, cables, time, LANES), jnp.float32),
            pltpu.VMEM((2, cables, time, LANES), jnp.int32),
            pltpu.SemaphoreType.DMA((2, 2)),
        ],
        compiler_params=pltpu.CompilerParams(vmem_limit_bytes=8 << 20),
        name="edges",
    )(pltpu.with_memory_space_constraint(phase_step, pltpu.HBM), wrap_count)
    outer_pairs = [(i, (i + (1 if i % 2 else -1)) % places) for i in range(places)]
    outer = lax.ppermute(outer, "chan", outer_pairs)
    inner = swapped(inner, "chan", 1)

    totals, sums = pl.pallas_call(
        totals_kernel,
        out_shape=(
            pltpu.VMEM((blocks * cables, LANES), jnp.float32),
            jax.ShapeDtypeStruct((steps * places, SUBLANES, LANES), jnp.float32),
        ),
        in_specs=[whole, outside],
        out_specs=[whole] * 2,
        scratch_shapes=[
            pltpu.VMEM((cables, time, width), jnp.int32),
            pltpu.SemaphoreType.DMA((cables,)),
        ],
        compiler_params=pltpu.CompilerParams(vmem_limit_bytes=16 << 20),
        cost_estimate=pl.CostEstimate(
            flops=0, bytes_accessed=phase_step.size * 4, transcendentals=0
        ),
        name="totals",
    )(pltpu.with_memory_space_constraint(phase_step, pltpu.VMEM), wrap_count)

    halo_high, halo_low, halo_totals = pl.pallas_call(
        halo_kernel,
        out_shape=(
            pltpu.VMEM((cables, 2, time, LANES), jnp.bfloat16),
            pltpu.VMEM((cables, 2, time, LANES), jnp.bfloat16),
            pltpu.VMEM((2 * cables, LANES), jnp.float32),
        ),
        in_specs=[whole] * 2,
        out_specs=[whole] * 3,
        compiler_params=pltpu.CompilerParams(vmem_limit_bytes=8 << 20),
        name="halo",
    )(inner, outer)

    running = jnp.concatenate([totals, halo_totals], axis=0)
    received = [swapped(running, "tm", 1)]
    sums, halo_totals = lax.optimization_barrier((sums, halo_totals))
    gathered = lax.all_to_all(sums, ("tm", "chan"), 0, 0, tiled=True)
    gathered = gathered.reshape(steps, places, SUBLANES, LANES)
    for bit in range(1, steps.bit_length() - 1):
        running = running + received[-1]
        running, gathered = lax.optimization_barrier((running, gathered))
        received.append(swapped(running, "tm", 1 << bit))
    tied, gathered = lax.optimization_barrier((filter_taps, gathered))
    local, weight = pl.pallas_call(
        filter_kernel,
        out_shape=(
            pltpu.VMEM((cables, blocks, time, LANES), jnp.float32),
            pltpu.VMEM((cables, 4 * LANES, 2 * LANES), jnp.bfloat16),
        ),
        in_specs=[outside] * 2 + [whole] * 3,
        out_specs=[whole] * 2,
        scratch_shapes=[
            pltpu.VMEM((cables, time, width), jnp.float32),
            pltpu.VMEM((cables, time, width), jnp.int32),
        ]
        + [pltpu.VMEM((1, blocks, time, LANES), jnp.bfloat16)] * 4
        + [
            pltpu.VMEM(filter_taps.shape, jnp.float32),
            pltpu.SemaphoreType.DMA((2, cables)),
        ],
        compiler_params=pltpu.CompilerParams(vmem_limit_bytes=32 << 20),
        cost_estimate=pl.CostEstimate(
            flops=2 * cables * (blocks + 2) * time * 8 * LANES * LANES,
            bytes_accessed=2 * phase_step.size * 4,
            transcendentals=0,
        ),
        name="filter",
    )(
        pltpu.with_memory_space_constraint(phase_step, pltpu.HBM),
        wrap_count,
        halo_high,
        halo_low,
        tied,
    )

    return pl.pallas_call(
        functools.partial(level_kernel, population),
        out_shape=jax.ShapeDtypeStruct(phase_step.shape, jnp.float32),
        in_specs=[whole, whole, [whole] * len(received), whole, scalars],
        out_specs=outside,
        scratch_shapes=[
            pltpu.VMEM((cables, time, width), jnp.float32),
            pltpu.VMEM(((blocks + 2) * cables, LANES), jnp.float32),
            pltpu.SemaphoreType.DMA((cables, CHUNKS)),
        ],
        compiler_params=pltpu.CompilerParams(vmem_limit_bytes=24 << 20),
        name="level",
    )(local, weight, received, gathered, coupling)


def solution(mesh):
    placed = (P(None, "tm", "chan"), P(None, "tm", "chan"), P(), P())
    return jax.shard_map(
        shards, mesh=mesh, in_specs=placed, out_specs=P(None, "tm", "chan"), check_vma=False
    )
```

```python
import functools
import math

import jax
import jax.numpy as jnp
from jax import lax
from jax.experimental import pallas as pl
from jax.experimental.pallas import tpu as pltpu
from jax.sharding import PartitionSpec as P

two_pi = 2.0 * math.pi
LANES = 128
HALF = LANES // 2
SUBLANES = 8
CHUNKS = 2


def shifted_down(value, amount):
    rows = lax.broadcasted_iota(jnp.int32, value.shape, 0)
    return jnp.where(rows >= amount, pltpu.roll(value, amount, 0), 0.0)


def scanned(pieces):
    sums, carry = [], None
    for value in pieces:
        amount = 1
        while amount < SUBLANES:
            value = value + shifted_down(value, amount)
            amount *= 2
        if carry is not None:
            value = value + carry
        carry = jnp.broadcast_to(value[SUBLANES - 1 :, :], value.shape)
        sums.append(value)
    return sums


def total(pieces):
    value = functools.reduce(jnp.add, pieces)
    return jnp.sum(value, axis=0, keepdims=True)


def split(value):
    high = value.astype(jnp.bfloat16)
    return high, (value - high.astype(jnp.float32)).astype(jnp.bfloat16)


def store_split(high_ref, low_ref, cable, block, sums):
    for pair in range(0, len(sums), 2):
        rows = pl.ds(pair * SUBLANES, 2 * SUBLANES)
        high, low = split(jnp.concatenate(sums[pair : pair + 2], axis=0))
        high_ref[cable, block, rows, :] = high
        low_ref[cable, block, rows, :] = low


def edges_kernel(phase_hbm, wrap_hbm, inner_ref, outer_ref, phase_ref, wrap_ref, sem):
    cables, time, width = phase_hbm.shape
    is_even = lax.rem(lax.axis_index("chan"), 2) == 0
    sends_last = (is_even, jnp.logical_not(is_even))
    copies = []
    for side, last in enumerate(sends_last):
        lanes = pl.ds(pl.multiple_of(jnp.where(last, width - LANES, 0), LANES), LANES)
        for kind, (source, target) in enumerate(((phase_hbm, phase_ref), (wrap_hbm, wrap_ref))):
            copies.append(
                pltpu.make_async_copy(source.at[:, :, lanes], target.at[side], sem.at[kind, side])
            )
    for copy in copies:
        copy.start()
    for copy in copies:
        copy.wait()
    lane = lax.broadcasted_iota(jnp.int32, (time, LANES), 1)
    for side, (last, target) in enumerate(zip(sends_last, (inner_ref, outer_ref))):
        for cable in range(cables // 2):
            low, high = (
                phase_ref[side, c] + two_pi * wrap_ref[side, c].astype(jnp.float32)
                for c in (cable, cable + cables // 2)
            )
            low = jnp.where(last, pltpu.roll(low, HALF, 1), low)
            high = jnp.where(last, high, pltpu.roll(high, HALF, 1))
            target[cable] = jnp.where(lane < HALF, low, high)


def backwards(value):
    lane = lax.broadcasted_iota(jnp.int32, value.shape, 1)
    bit = 1
    while bit < LANES:
        value = jnp.where(
            (lane & bit) == 0, pltpu.roll(value, LANES - bit, 1), pltpu.roll(value, bit, 1)
        )
        bit *= 2
    return value


def increments_kernel(
    phase_ref, wrap_hbm, taps_ref, high_ref, low_ref, totals_ref, sums_ref, weight_ref, wrap_ref,
    reversed_ref, sem,
):
    cables, time, width = phase_ref.shape
    blocks = width // LANES
    groups = time // SUBLANES

    def copy(cable):
        return pltpu.make_async_copy(wrap_hbm.at[cable], wrap_ref.at[cable], sem.at[cable])

    for cable in range(cables):
        copy(cable).start()

    lane = lax.broadcasted_iota(jnp.int32, taps_ref.shape, 1)
    taps = jnp.where(lane == HALF, 1.0, 0.0) - taps_ref[...]
    reversed_ref[...] = pltpu.roll(backwards(taps * (1.0 / (4.0 * two_pi))), 1, 1)
    inputs = lax.broadcasted_iota(jnp.int32, (LANES, LANES), 0)
    outputs = lax.broadcasted_iota(jnp.int32, (LANES, LANES), 1)

    @pl.loop(0, cables)
    def _(cable):
        row = jnp.broadcast_to(reversed_ref[pl.ds(cable, 1), :], (LANES, LANES))
        circulant = pltpu.roll(row, 0, 1, stride=1, stride_axis=0)
        for column, mask in enumerate((inputs >= outputs, inputs < outputs)):
            high, low = split(jnp.where(mask, circulant, 0.0))
            for place, part in enumerate((high, high, low, low)):
                rows, lanes = pl.ds(place * LANES, LANES), pl.ds(column * LANES, LANES)
                weight_ref[cable, rows, lanes] = part

    def cable_step(cable, accumulated):
        copy(cable).wait()

        def block_step(block, accumulated):
            lanes = pl.ds(pl.multiple_of(block * LANES, LANES), LANES)
            pieces = []
            for i in range(groups):
                rows = pl.ds(i * SUBLANES, SUBLANES)
                turns = wrap_ref[cable, rows, lanes].astype(jnp.float32)
                pieces.append(phase_ref[cable, rows, lanes] + two_pi * turns)
            store_split(high_ref, low_ref, cable, block, pieces)
            totals_ref[pl.ds(block * cables + cable, 1), :] = total(pieces)
            return tuple(a + b for a, b in zip(accumulated, pieces))

        return lax.fori_loop(0, blocks, block_step, accumulated, unroll=16)

    zeros = tuple(jnp.zeros((SUBLANES, LANES), jnp.float32) for _ in range(groups))
    accumulated = scanned(lax.fori_loop(0, cables, cable_step, zeros))
    lane = lax.broadcasted_iota(jnp.int32, (SUBLANES, LANES), 1)
    tile = jnp.zeros((SUBLANES, LANES), jnp.float32)
    for i, value in enumerate(accumulated):
        tile = jnp.where(lane == i, jnp.sum(value, axis=1, keepdims=True), tile)
    sums_ref[...] = tile


def halo_kernel(inner_ref, outer_ref, high_ref, low_ref, totals_ref):
    pairs, time, _ = inner_ref.shape
    cables = 2 * pairs
    groups = time // SUBLANES
    place = lax.axis_index("chan")
    is_even = lax.rem(place, 2) == 0
    at_end = (place == 0) | (place == lax.axis_size("chan") - 1)
    for pair in range(pairs):
        inner, outer = (
            [ref[pair, pl.ds(i * SUBLANES, SUBLANES), :] for i in range(groups)]
            for ref in (inner_ref, outer_ref)
        )
        outer = [jnp.where(at_end, 0.0, value) for value in outer]
        right = [jnp.where(is_even, a, b) for a, b in zip(inner, outer)]
        left = [jnp.where(is_even, b, a) for a, b in zip(inner, outer)]
        for block, pieces, moved in ((0, right, pair + pairs), (1, left, pair)):
            for cable in (pair, pair + pairs):
                placed = [pltpu.roll(v, HALF, 1) for v in pieces] if cable == moved else pieces
                store_split(high_ref, low_ref, cable, block, placed)
                totals_ref[pl.ds(block * cables + cable, 1), :] = total(placed)


def filter_kernel(first, high_ref, low_ref, halo_high_ref, halo_low_ref, weight_ref, local_ref):
    _, blocks, time, _ = high_ref.shape
    groups = time // SUBLANES
    lane = lax.broadcasted_iota(jnp.int32, (time, LANES), 1)

    @pl.loop(0, local_ref.shape[0])
    def _(index):
        cable = first + index
        high, low = (
            jnp.concatenate(
                [main[cable].reshape(blocks * time, LANES), halo[cable].reshape(2 * time, LANES)],
                axis=0,
            )
            for main, halo in ((high_ref, halo_high_ref), (low_ref, halo_low_ref))
        )
        product = jnp.dot(
            jnp.concatenate([high, low, high, low], axis=1),
            weight_ref[cable],
            preferred_element_type=jnp.float32,
        )

        def rolled(block):
            here = block if block >= 0 else blocks + 1
            there = block + 1
            return pltpu.roll(
                product[here * time : (here + 1) * time, :LANES]
                + product[there * time : (there + 1) * time, LANES:],
                HALF,
                1,
            )

        previous = rolled(-1)
        for block in range(blocks):
            following = rolled(block)
            value = jnp.where(lane < HALF, previous, following)
            pieces = [value[i * SUBLANES : (i + 1) * SUBLANES] for i in range(groups)]
            for i, piece in enumerate(scanned(pieces)):
                local_ref[index, block, pl.ds(i * SUBLANES, SUBLANES), :] = piece
            previous = following


def bias_kernel(weight_ref, totals_refs, bias_ref, slope_ref, offset_ref):
    cables, blocks, _ = bias_ref.shape
    step, place = lax.axis_index("tm"), lax.axis_index("chan")
    inside_left = jnp.where(place == 0, 0.0, 1.0)
    inside_right = jnp.where(place == lax.axis_size("chan") - 1, 0.0, 1.0)
    offset = jnp.zeros(offset_ref.shape, jnp.float32)
    for bit, ref in enumerate(totals_refs):
        offset = offset + jnp.where((step & (1 << bit)) != 0, ref[...], 0.0)
    offset_ref[...] = offset
    used = blocks + 2
    padded = -(-(used + 1) // SUBLANES) * SUBLANES
    row = lax.broadcasted_iota(jnp.int32, (padded, LANES), 0)
    lane = lax.broadcasted_iota(jnp.int32, (padded, LANES), 1)

    def cable_step(cable, carry):
        offset = jnp.concatenate(
            [
                offset_ref[pl.ds(cable, used, stride=cables), :],
                jnp.ones((padded - used, LANES), jnp.float32),
            ],
            axis=0,
        )
        high, low = split(offset)
        product = jnp.dot(
            jnp.concatenate([high, low, high, low], axis=1),
            weight_ref[cable],
            preferred_element_type=jnp.float32,
        )
        here, there = product[:, :LANES], product[:, LANES:]
        left = pltpu.roll(here[used - 1 : used] + there[:1], HALF, 1)
        following = pltpu.roll(here + pltpu.roll(there, padded - 1, 0), HALF, 1)
        previous = jnp.where(row == 0, left, pltpu.roll(following, 1, 0))
        bias_ref[cable] = jnp.where(lane < HALF, previous, following)[:blocks]
        here, there = here[used : used + 1], there[used : used + 1]
        middle = pltpu.roll(here + there, HALF, 1)
        first = pltpu.roll(here * inside_left + there, HALF, 1)
        last = pltpu.roll(here + there * inside_right, HALF, 1)
        previous = jnp.where(row == 0, first, middle)
        following = jnp.where(row == blocks - 1, last, middle)
        slope_ref[cable] = jnp.where(lane < HALF, previous, following)[:blocks]
        return carry

    lax.fori_loop(0, cables, cable_step, 0, unroll=4)


def level_kernel(
    population, local_refs, bias_ref, slope_ref, sums_ref, earlier_refs, coupling_ref,
    out_hbm, stage_ref, sem,
):
    _, blocks, time, _ = local_refs[0].shape
    span = blocks // CHUNKS
    cables = out_hbm.shape[0]
    groups = time // SUBLANES
    step = lax.axis_index("tm")
    before = jnp.zeros((SUBLANES, LANES), jnp.float32)
    for bit, ref in enumerate(earlier_refs):
        before = before + jnp.where((step & (1 << bit)) != 0, ref[...], 0.0)
    common = sums_ref[...] + before[SUBLANES - 1 :, groups - 1 : groups]
    common = common * (1.0 / population)
    columns = [
        jnp.broadcast_to(common[:, i : i + 1], (SUBLANES, LANES)) for i in range(groups)
    ]

    def written(cable, chunk):
        lanes = pl.ds(chunk * span * LANES, span * LANES)
        return pltpu.make_async_copy(
            stage_ref.at[cable, :, lanes], out_hbm.at[cable, :, lanes], sem.at[cable, chunk]
        )

    first_cable = 0
    for local_ref in local_refs:

        def cable_step(index, carry, first_cable=first_cable, local_ref=local_ref):
            cable = first_cable + index
            shifts = [coupling_ref[cable] * column for column in columns]

            def block_step(block, carry):
                lanes = pl.ds(pl.multiple_of(block * LANES, LANES), LANES)
                bias = jnp.broadcast_to(bias_ref[cable, pl.ds(block, 1), :], (SUBLANES, LANES))
                slope = jnp.broadcast_to(slope_ref[cable, pl.ds(block, 1), :], (SUBLANES, LANES))
                for i in range(groups):
                    rows = pl.ds(i * SUBLANES, SUBLANES)
                    stage_ref[cable, rows, lanes] = local_ref[index, block, rows, :] + (
                        bias - shifts[i] * slope
                    )
                return carry

            for chunk in range(CHUNKS):
                lax.fori_loop(chunk * span, (chunk + 1) * span, block_step, 0, unroll=8)
                written(cable, chunk).start()
            return carry

        lax.fori_loop(0, local_ref.shape[0], cable_step, 0)
        first_cable += local_ref.shape[0]
    for cable in range(cables):
        for chunk in range(CHUNKS):
            written(cable, chunk).wait()


def swapped(value, axis, bit):
    return lax.ppermute(value, axis, [(i, i ^ bit) for i in range(lax.axis_size(axis))])


def shards(phase_step, wrap_count, coupling, filter_taps):
    cables, time, width = phase_step.shape
    blocks = width // LANES
    steps, places = lax.axis_size("tm"), lax.axis_size("chan")
    population = cables * width * places
    bounds = [0, 3 * cables // 8, 5 * cables // 8, 7 * cables // 8, cables]
    parts = len(bounds) - 1
    wrap_count = pltpu.with_memory_space_constraint(wrap_count, pltpu.HBM)
    whole = pl.BlockSpec(memory_space=pltpu.VMEM)
    outside = pl.BlockSpec(memory_space=pl.ANY)
    scalars = pl.BlockSpec(memory_space=pltpu.SMEM)

    inner, outer = pl.pallas_call(
        edges_kernel,
        out_shape=[pltpu.VMEM((cables // 2, time, LANES), jnp.float32)] * 2,
        in_specs=[outside] * 2,
        out_specs=[whole] * 2,
        scratch_shapes=[
            pltpu.VMEM((2, cables, time, LANES), jnp.float32),
            pltpu.VMEM((2, cables, time, LANES), jnp.int32),
            pltpu.SemaphoreType.DMA((2, 2)),
        ],
        compiler_params=pltpu.CompilerParams(vmem_limit_bytes=8 << 20),
        name="edges",
    )(pltpu.with_memory_space_constraint(phase_step, pltpu.HBM), wrap_count)
    outer_pairs = [(i, (i + (1 if i % 2 else -1)) % places) for i in range(places)]
    outer = lax.ppermute(outer, "chan", outer_pairs)
    inner = swapped(inner, "chan", 1)

    high, low, totals, sums, weight = pl.pallas_call(
        increments_kernel,
        out_shape=(
            pltpu.VMEM((cables, blocks, time, LANES), jnp.bfloat16),
            pltpu.VMEM((cables, blocks, time, LANES), jnp.bfloat16),
            pltpu.VMEM((blocks * cables, LANES), jnp.float32),
            pltpu.VMEM((SUBLANES, LANES), jnp.float32),
            pltpu.VMEM((cables, 4 * LANES, 2 * LANES), jnp.bfloat16),
        ),
        in_specs=[whole, outside, whole],
        out_specs=[whole] * 5,
        scratch_shapes=[
            pltpu.VMEM((cables, time, width), jnp.int32),
            pltpu.VMEM(filter_taps.shape, jnp.float32),
            pltpu.SemaphoreType.DMA((cables,)),
        ],
        compiler_params=pltpu.CompilerParams(vmem_limit_bytes=16 << 20),
        cost_estimate=pl.CostEstimate(
            flops=0, bytes_accessed=phase_step.size * 4, transcendentals=0
        ),
        name="increments",
    )(pltpu.with_memory_space_constraint(phase_step, pltpu.VMEM), wrap_count, filter_taps)

    halo_high, halo_low, halo_totals = pl.pallas_call(
        halo_kernel,
        out_shape=(
            pltpu.VMEM((cables, 2, time, LANES), jnp.bfloat16),
            pltpu.VMEM((cables, 2, time, LANES), jnp.bfloat16),
            pltpu.VMEM((2 * cables, LANES), jnp.float32),
        ),
        in_specs=[whole] * 2,
        out_specs=[whole] * 3,
        compiler_params=pltpu.CompilerParams(vmem_limit_bytes=8 << 20),
        name="halo",
    )(inner, outer)

    def filtered(part, weight):
        share = bounds[part + 1] - bounds[part]
        return pl.pallas_call(
            functools.partial(filter_kernel, bounds[part]),
            out_shape=pltpu.VMEM((share, blocks, time, LANES), jnp.float32),
            in_specs=[whole] * 5,
            out_specs=whole,
            compiler_params=pltpu.CompilerParams(vmem_limit_bytes=16 << 20),
            cost_estimate=pl.CostEstimate(
                flops=2 * share * (blocks + 2) * time * 8 * LANES * LANES,
                bytes_accessed=1 << 20,
                transcendentals=0,
            ),
            name="filter",
        )(high, low, halo_high, halo_low, weight)

    def biased(received):
        return pl.pallas_call(
            bias_kernel,
            out_shape=[pltpu.VMEM((cables, blocks, LANES), jnp.float32)] * 2,
            in_specs=[whole, [whole] * len(received)],
            out_specs=[whole] * 2,
            scratch_shapes=[pltpu.VMEM(received[0].shape, jnp.float32)],
            compiler_params=pltpu.CompilerParams(vmem_limit_bytes=8 << 20),
            cost_estimate=pl.CostEstimate(flops=0, bytes_accessed=2 << 20, transcendentals=0),
            name="bias",
        )(weight, received)

    running = jnp.concatenate([totals, halo_totals], axis=0)
    received = [swapped(running, "tm", 1)]
    sums, halo_totals = lax.optimization_barrier((sums, halo_totals))
    rounds = [("chan", 1 << bit) for bit in range(places.bit_length() - 1)]
    rounds += [("tm", 1 << bit) for bit in range(steps.bit_length() - 1)]
    local, received_sums, chan_sums, ready, rows = [], [], sums, None, None
    for number, (axis, bit) in enumerate(rounds):
        incoming = swapped(sums, axis, bit)
        if number % 2 == 0 and number > 0 and ready is not None:
            received.append(swapped(ready, "tm", 1 << len(received)))
            ready = None
        if number > 0 and len(local) < parts:
            tied, sums = lax.optimization_barrier((weight, sums))
            if len(local) == parts - 1 and 1 << len(received) >= steps:
                rows, tied = lax.optimization_barrier((biased(received), tied))
            part = filtered(len(local), tied)
            incoming, part = lax.optimization_barrier((incoming, part))
            local.append(part)
        if number % 2 == 1 and 1 << len(received) < steps:
            earlier, local[-1] = lax.optimization_barrier((received[-1], local[-1]))
            ready = running = running + earlier
        if axis == "tm":
            received_sums.append(incoming)
        sums = sums + incoming
        if axis == "chan":
            chan_sums = sums
    while 1 << len(received) < steps:
        running = running + received[-1] if ready is None else ready
        ready = None
        received.append(swapped(running, "tm", 1 << len(received)))
    while len(local) < parts:
        local.append(filtered(len(local), weight))
    bias, slope = biased(received) if rows is None else rows

    return pl.pallas_call(
        functools.partial(level_kernel, population),
        out_shape=jax.ShapeDtypeStruct(phase_step.shape, jnp.float32),
        in_specs=[[whole] * parts, whole, whole, whole, [whole] * len(received_sums), scalars],
        out_specs=outside,
        scratch_shapes=[
            pltpu.VMEM((cables, time, width), jnp.float32),
            pltpu.SemaphoreType.DMA((cables, CHUNKS)),
        ],
        compiler_params=pltpu.CompilerParams(vmem_limit_bytes=24 << 20),
        name="level",
    )(local, bias, slope, chan_sums, received_sums, coupling)


def solution(mesh):
    placed = (P(None, "tm", "chan"), P(None, "tm", "chan"), P(), P())
    return jax.shard_map(
        shards, mesh=mesh, in_specs=placed, out_specs=P(None, "tm", "chan"), check_vma=False
    )
```

```python
import functools
import math

import jax
import jax.numpy as jnp
from jax import lax
from jax.experimental import pallas as pl
from jax.experimental.pallas import tpu as pltpu
from jax.sharding import PartitionSpec as P

two_pi = 2.0 * math.pi
LANES = 128
HALF = LANES // 2
SUBLANES = 8
CHUNKS = 2


def shifted_down(value, amount):
    rows = lax.broadcasted_iota(jnp.int32, value.shape, 0)
    return jnp.where(rows >= amount, pltpu.roll(value, amount, 0), 0.0)


def scanned(pieces):
    sums, carry = [], None
    for value in pieces:
        amount = 1
        while amount < SUBLANES:
            value = value + shifted_down(value, amount)
            amount *= 2
        if carry is not None:
            value = value + carry
        carry = jnp.broadcast_to(value[SUBLANES - 1 :, :], value.shape)
        sums.append(value)
    return sums


def total(pieces):
    value = functools.reduce(jnp.add, pieces)
    return jnp.sum(value, axis=0, keepdims=True)


def split(value):
    high = value.astype(jnp.bfloat16)
    return high, (value - high.astype(jnp.float32)).astype(jnp.bfloat16)


def store_split(high_ref, low_ref, cable, block, sums):
    for pair in range(0, len(sums), 2):
        rows = pl.ds(pair * SUBLANES, 2 * SUBLANES)
        high, low = split(jnp.concatenate(sums[pair : pair + 2], axis=0))
        high_ref[cable, block, rows, :] = high
        low_ref[cable, block, rows, :] = low


def edges_kernel(phase_hbm, wrap_hbm, inner_ref, outer_ref, phase_ref, wrap_ref, sem):
    cables, time, width = phase_hbm.shape
    is_even = lax.rem(lax.axis_index("chan"), 2) == 0
    sends_last = (is_even, jnp.logical_not(is_even))
    copies = []
    for side, last in enumerate(sends_last):
        lanes = pl.ds(pl.multiple_of(jnp.where(last, width - LANES, 0), LANES), LANES)
        for kind, (source, target) in enumerate(((phase_hbm, phase_ref), (wrap_hbm, wrap_ref))):
            copies.append(
                pltpu.make_async_copy(source.at[:, :, lanes], target.at[side], sem.at[kind, side])
            )
    for number, copy in enumerate(copies):
        copy.start(priority=number % 2)
    for copy in copies:
        copy.wait()
    lane = lax.broadcasted_iota(jnp.int32, (time, LANES), 1)
    for side, (last, target) in enumerate(zip(sends_last, (inner_ref, outer_ref))):
        for cable in range(cables // 2):
            low, high = (
                phase_ref[side, c] + two_pi * wrap_ref[side, c].astype(jnp.float32)
                for c in (cable, cable + cables // 2)
            )
            low = jnp.where(last, pltpu.roll(low, HALF, 1), low)
            high = jnp.where(last, high, pltpu.roll(high, HALF, 1))
            target[cable] = jnp.where(lane < HALF, low, high)


def backwards(value):
    lane = lax.broadcasted_iota(jnp.int32, value.shape, 1)
    bit = 1
    while bit < LANES:
        value = jnp.where(
            (lane & bit) == 0, pltpu.roll(value, LANES - bit, 1), pltpu.roll(value, bit, 1)
        )
        bit *= 2
    return value


def increments_kernel(
    phase_ref, wrap_hbm, taps_ref, high_ref, low_ref, totals_ref, sums_ref, weight_ref, wrap_ref,
    reversed_ref, sem,
):
    cables, time, width = phase_ref.shape
    blocks = width // LANES
    groups = time // SUBLANES

    def copy(cable):
        return pltpu.make_async_copy(wrap_hbm.at[cable], wrap_ref.at[cable], sem.at[cable])

    for cable in range(cables):
        copy(cable).start(priority=cable % 2)

    lane = lax.broadcasted_iota(jnp.int32, taps_ref.shape, 1)
    taps = jnp.where(lane == HALF, 1.0, 0.0) - taps_ref[...]
    reversed_ref[...] = pltpu.roll(backwards(taps * (1.0 / (4.0 * two_pi))), 1, 1)
    inputs = lax.broadcasted_iota(jnp.int32, (LANES, LANES), 0)
    outputs = lax.broadcasted_iota(jnp.int32, (LANES, LANES), 1)

    @pl.loop(0, cables)
    def _(cable):
        row = jnp.broadcast_to(reversed_ref[pl.ds(cable, 1), :], (LANES, LANES))
        circulant = pltpu.roll(row, 0, 1, stride=1, stride_axis=0)
        for column, mask in enumerate((inputs >= outputs, inputs < outputs)):
            high, low = split(jnp.where(mask, circulant, 0.0))
            for place, part in enumerate((high, high, low, low)):
                rows, lanes = pl.ds(place * LANES, LANES), pl.ds(column * LANES, LANES)
                weight_ref[cable, rows, lanes] = part

    def cable_step(cable, accumulated):
        copy(cable).wait()

        def block_step(block, accumulated):
            lanes = pl.ds(pl.multiple_of(block * LANES, LANES), LANES)
            pieces = []
            for i in range(groups):
                rows = pl.ds(i * SUBLANES, SUBLANES)
                turns = wrap_ref[cable, rows, lanes].astype(jnp.float32)
                pieces.append(phase_ref[cable, rows, lanes] + two_pi * turns)
            store_split(high_ref, low_ref, cable, block, pieces)
            totals_ref[pl.ds(block * cables + cable, 1), :] = total(pieces)
            return tuple(a + b for a, b in zip(accumulated, pieces))

        return lax.fori_loop(0, blocks, block_step, accumulated, unroll=16)

    zeros = tuple(jnp.zeros((SUBLANES, LANES), jnp.float32) for _ in range(groups))
    accumulated = scanned(lax.fori_loop(0, cables, cable_step, zeros))
    lane = lax.broadcasted_iota(jnp.int32, (SUBLANES, LANES), 1)
    tile = jnp.zeros((SUBLANES, LANES), jnp.float32)
    for i, value in enumerate(accumulated):
        tile = jnp.where(lane == i, jnp.sum(value, axis=1, keepdims=True), tile)
    sums_ref[...] = tile


def halo_kernel(inner_ref, outer_ref, high_ref, low_ref, totals_ref):
    pairs, time, _ = inner_ref.shape
    cables = 2 * pairs
    groups = time // SUBLANES
    place = lax.axis_index("chan")
    is_even = lax.rem(place, 2) == 0
    at_end = (place == 0) | (place == lax.axis_size("chan") - 1)
    for pair in range(pairs):
        inner, outer = (
            [ref[pair, pl.ds(i * SUBLANES, SUBLANES), :] for i in range(groups)]
            for ref in (inner_ref, outer_ref)
        )
        outer = [jnp.where(at_end, 0.0, value) for value in outer]
        right = [jnp.where(is_even, a, b) for a, b in zip(inner, outer)]
        left = [jnp.where(is_even, b, a) for a, b in zip(inner, outer)]
        for block, pieces, moved in ((0, right, pair + pairs), (1, left, pair)):
            for cable in (pair, pair + pairs):
                placed = [pltpu.roll(v, HALF, 1) for v in pieces] if cable == moved else pieces
                store_split(high_ref, low_ref, cable, block, placed)
                totals_ref[pl.ds(block * cables + cable, 1), :] = total(placed)


def filter_kernel(first, high_ref, low_ref, halo_high_ref, halo_low_ref, weight_ref, local_ref):
    _, blocks, time, _ = high_ref.shape
    groups = time // SUBLANES
    lane = lax.broadcasted_iota(jnp.int32, (time, LANES), 1)

    @pl.loop(0, local_ref.shape[0])
    def _(index):
        cable = first + index
        high, low = (
            jnp.concatenate(
                [main[cable].reshape(blocks * time, LANES), halo[cable].reshape(2 * time, LANES)],
                axis=0,
            )
            for main, halo in ((high_ref, halo_high_ref), (low_ref, halo_low_ref))
        )
        product = jnp.dot(
            jnp.concatenate([high, low, high, low], axis=1),
            weight_ref[cable],
            preferred_element_type=jnp.float32,
        )

        def rolled(block):
            here = block if block >= 0 else blocks + 1
            there = block + 1
            return pltpu.roll(
                product[here * time : (here + 1) * time, :LANES]
                + product[there * time : (there + 1) * time, LANES:],
                HALF,
                1,
            )

        previous = rolled(-1)
        for block in range(blocks):
            following = rolled(block)
            value = jnp.where(lane < HALF, previous, following)
            pieces = [value[i * SUBLANES : (i + 1) * SUBLANES] for i in range(groups)]
            for i, piece in enumerate(scanned(pieces)):
                local_ref[index, block, pl.ds(i * SUBLANES, SUBLANES), :] = piece
            previous = following


def bias_kernel(weight_ref, totals_refs, bias_ref, slope_ref, offset_ref):
    cables, blocks, _ = bias_ref.shape
    step, place = lax.axis_index("tm"), lax.axis_index("chan")
    inside_left = jnp.where(place == 0, 0.0, 1.0)
    inside_right = jnp.where(place == lax.axis_size("chan") - 1, 0.0, 1.0)
    offset = jnp.zeros(offset_ref.shape, jnp.float32)
    for bit, ref in enumerate(totals_refs):
        offset = offset + jnp.where((step & (1 << bit)) != 0, ref[...], 0.0)
    offset_ref[...] = offset
    used = blocks + 2
    padded = -(-(used + 1) // SUBLANES) * SUBLANES
    row = lax.broadcasted_iota(jnp.int32, (padded, LANES), 0)
    lane = lax.broadcasted_iota(jnp.int32, (padded, LANES), 1)

    def cable_step(cable, carry):
        offset = jnp.concatenate(
            [
                offset_ref[pl.ds(cable, used, stride=cables), :],
                jnp.ones((padded - used, LANES), jnp.float32),
            ],
            axis=0,
        )
        high, low = split(offset)
        product = jnp.dot(
            jnp.concatenate([high, low, high, low], axis=1),
            weight_ref[cable],
            preferred_element_type=jnp.float32,
        )
        here, there = product[:, :LANES], product[:, LANES:]
        left = pltpu.roll(here[used - 1 : used] + there[:1], HALF, 1)
        following = pltpu.roll(here + pltpu.roll(there, padded - 1, 0), HALF, 1)
        previous = jnp.where(row == 0, left, pltpu.roll(following, 1, 0))
        bias_ref[cable] = jnp.where(lane < HALF, previous, following)[:blocks]
        here, there = here[used : used + 1], there[used : used + 1]
        middle = pltpu.roll(here + there, HALF, 1)
        first = pltpu.roll(here * inside_left + there, HALF, 1)
        last = pltpu.roll(here + there * inside_right, HALF, 1)
        previous = jnp.where(row == 0, first, middle)
        following = jnp.where(row == blocks - 1, last, middle)
        slope_ref[cable] = jnp.where(lane < HALF, previous, following)[:blocks]
        return carry

    lax.fori_loop(0, cables, cable_step, 0, unroll=4)


def level_kernel(
    population, local_refs, bias_ref, slope_ref, sums_ref, earlier_refs, coupling_ref,
    out_hbm, stage_ref, sem,
):
    _, blocks, time, _ = local_refs[0].shape
    span = blocks // CHUNKS
    cables = out_hbm.shape[0]
    groups = time // SUBLANES
    step = lax.axis_index("tm")
    before = jnp.zeros((SUBLANES, LANES), jnp.float32)
    for bit, ref in enumerate(earlier_refs):
        before = before + jnp.where((step & (1 << bit)) != 0, ref[...], 0.0)
    common = sums_ref[...] + before[SUBLANES - 1 :, groups - 1 : groups]
    common = common * (1.0 / population)
    columns = [
        jnp.broadcast_to(common[:, i : i + 1], (SUBLANES, LANES)) for i in range(groups)
    ]

    def written(cable, chunk):
        lanes = pl.ds(chunk * span * LANES, span * LANES)
        return pltpu.make_async_copy(
            stage_ref.at[cable, :, lanes], out_hbm.at[cable, :, lanes], sem.at[cable, chunk]
        )

    first_cable = 0
    for local_ref in local_refs:

        def cable_step(index, carry, first_cable=first_cable, local_ref=local_ref):
            cable = first_cable + index
            shifts = [coupling_ref[cable] * column for column in columns]

            def block_step(block, carry):
                lanes = pl.ds(pl.multiple_of(block * LANES, LANES), LANES)
                bias = jnp.broadcast_to(bias_ref[cable, pl.ds(block, 1), :], (SUBLANES, LANES))
                slope = jnp.broadcast_to(slope_ref[cable, pl.ds(block, 1), :], (SUBLANES, LANES))
                for i in range(groups):
                    rows = pl.ds(i * SUBLANES, SUBLANES)
                    stage_ref[cable, rows, lanes] = local_ref[index, block, rows, :] + (
                        bias - shifts[i] * slope
                    )
                return carry

            for chunk in range(CHUNKS):
                lax.fori_loop(chunk * span, (chunk + 1) * span, block_step, 0, unroll=8)
                written(cable, chunk).start(priority=chunk % 2)
            return carry

        lax.fori_loop(0, local_ref.shape[0], cable_step, 0)
        first_cable += local_ref.shape[0]
    for cable in range(cables):
        for chunk in range(CHUNKS):
            written(cable, chunk).wait()


def swapped(value, axis, bit):
    return lax.ppermute(value, axis, [(i, i ^ bit) for i in range(lax.axis_size(axis))])


def shards(phase_step, wrap_count, coupling, filter_taps):
    cables, time, width = phase_step.shape
    blocks = width // LANES
    steps, places = lax.axis_size("tm"), lax.axis_size("chan")
    population = cables * width * places
    bounds = [0, 3 * cables // 8, cables // 2, 3 * cables // 4, cables]
    parts = len(bounds) - 1
    wrap_count = pltpu.with_memory_space_constraint(wrap_count, pltpu.HBM)
    whole = pl.BlockSpec(memory_space=pltpu.VMEM)
    outside = pl.BlockSpec(memory_space=pl.ANY)
    scalars = pl.BlockSpec(memory_space=pltpu.SMEM)

    inner, outer = pl.pallas_call(
        edges_kernel,
        out_shape=[pltpu.VMEM((cables // 2, time, LANES), jnp.float32)] * 2,
        in_specs=[outside] * 2,
        out_specs=[whole] * 2,
        scratch_shapes=[
            pltpu.VMEM((2, cables, time, LANES), jnp.float32),
            pltpu.VMEM((2, cables, time, LANES), jnp.int32),
            pltpu.SemaphoreType.DMA((2, 2)),
        ],
        compiler_params=pltpu.CompilerParams(vmem_limit_bytes=8 << 20),
        name="edges",
    )(pltpu.with_memory_space_constraint(phase_step, pltpu.HBM), wrap_count)
    outer_pairs = [(i, (i + (1 if i % 2 else -1)) % places) for i in range(places)]
    outer = lax.ppermute(outer, "chan", outer_pairs)
    inner = swapped(inner, "chan", 1)

    high, low, totals, sums, weight = pl.pallas_call(
        increments_kernel,
        out_shape=(
            pltpu.VMEM((cables, blocks, time, LANES), jnp.bfloat16),
            pltpu.VMEM((cables, blocks, time, LANES), jnp.bfloat16),
            pltpu.VMEM((blocks * cables, LANES), jnp.float32),
            pltpu.VMEM((SUBLANES, LANES), jnp.float32),
            pltpu.VMEM((cables, 4 * LANES, 2 * LANES), jnp.bfloat16),
        ),
        in_specs=[whole, outside, whole],
        out_specs=[whole] * 5,
        scratch_shapes=[
            pltpu.VMEM((cables, time, width), jnp.int32),
            pltpu.VMEM(filter_taps.shape, jnp.float32),
            pltpu.SemaphoreType.DMA((cables,)),
        ],
        compiler_params=pltpu.CompilerParams(vmem_limit_bytes=16 << 20),
        cost_estimate=pl.CostEstimate(
            flops=0, bytes_accessed=phase_step.size * 4, transcendentals=0
        ),
        name="increments",
    )(pltpu.with_memory_space_constraint(phase_step, pltpu.VMEM), wrap_count, filter_taps)

    halo_high, halo_low, halo_totals = pl.pallas_call(
        halo_kernel,
        out_shape=(
            pltpu.VMEM((cables, 2, time, LANES), jnp.bfloat16),
            pltpu.VMEM((cables, 2, time, LANES), jnp.bfloat16),
            pltpu.VMEM((2 * cables, LANES), jnp.float32),
        ),
        in_specs=[whole] * 2,
        out_specs=[whole] * 3,
        compiler_params=pltpu.CompilerParams(vmem_limit_bytes=8 << 20),
        name="halo",
    )(inner, outer)

    def filtered(part, weight):
        share = bounds[part + 1] - bounds[part]
        return pl.pallas_call(
            functools.partial(filter_kernel, bounds[part]),
            out_shape=pltpu.VMEM((share, blocks, time, LANES), jnp.float32),
            in_specs=[whole] * 5,
            out_specs=whole,
            compiler_params=pltpu.CompilerParams(vmem_limit_bytes=16 << 20),
            cost_estimate=pl.CostEstimate(
                flops=2 * share * (blocks + 2) * time * 8 * LANES * LANES,
                bytes_accessed=1 << 20,
                transcendentals=0,
            ),
            name="filter",
        )(high, low, halo_high, halo_low, weight)

    def biased(received):
        return pl.pallas_call(
            bias_kernel,
            out_shape=[pltpu.VMEM((cables, blocks, LANES), jnp.float32)] * 2,
            in_specs=[whole, [whole] * len(received)],
            out_specs=[whole] * 2,
            scratch_shapes=[pltpu.VMEM(received[0].shape, jnp.float32)],
            compiler_params=pltpu.CompilerParams(vmem_limit_bytes=8 << 20),
            cost_estimate=pl.CostEstimate(flops=0, bytes_accessed=2 << 20, transcendentals=0),
            name="bias",
        )(weight, received)

    running = jnp.concatenate([totals, halo_totals], axis=0)
    received = [swapped(running, "tm", 1)]
    sums, halo_totals = lax.optimization_barrier((sums, halo_totals))
    rounds = [("chan", 1 << bit) for bit in range(places.bit_length() - 1)]
    rounds += [("tm", 1 << bit) for bit in range(steps.bit_length() - 1)]
    local, received_sums, chan_sums, ready, rows = [], [], sums, None, None
    for number, (axis, bit) in enumerate(rounds):
        incoming = swapped(sums, axis, bit)
        if number % 2 == 0 and number > 0 and ready is not None:
            received.append(swapped(ready, "tm", 1 << len(received)))
            ready = None
        if number > 0 and len(local) < parts:
            tied, sums = lax.optimization_barrier((weight, sums))
            if len(local) == parts - 1 and 1 << len(received) >= steps:
                rows, tied = lax.optimization_barrier((biased(received), tied))
            part = filtered(len(local), tied)
            incoming, part = lax.optimization_barrier((incoming, part))
            local.append(part)
        if number % 2 == 1 and 1 << len(received) < steps:
            earlier, local[-1] = lax.optimization_barrier((received[-1], local[-1]))
            ready = running = running + earlier
        if axis == "tm":
            received_sums.append(incoming)
        sums = sums + incoming
        if axis == "chan":
            chan_sums = sums
    while 1 << len(received) < steps:
        running = running + received[-1] if ready is None else ready
        ready = None
        received.append(swapped(running, "tm", 1 << len(received)))
    while len(local) < parts:
        local.append(filtered(len(local), weight))
    bias, slope = biased(received) if rows is None else rows

    return pl.pallas_call(
        functools.partial(level_kernel, population),
        out_shape=jax.ShapeDtypeStruct(phase_step.shape, jnp.float32),
        in_specs=[[whole] * parts, whole, whole, whole, [whole] * len(received_sums), scalars],
        out_specs=outside,
        scratch_shapes=[
            pltpu.VMEM((cables, time, width), jnp.float32),
            pltpu.SemaphoreType.DMA((cables, CHUNKS)),
        ],
        compiler_params=pltpu.CompilerParams(vmem_limit_bytes=24 << 20),
        name="level",
    )(local, bias, slope, chan_sums, received_sums, coupling)


def solution(mesh):
    placed = (P(None, "tm", "chan"), P(None, "tm", "chan"), P(), P())
    return jax.shard_map(
        shards, mesh=mesh, in_specs=placed, out_specs=P(None, "tm", "chan"), check_vma=False
    )
```

```python
import functools
import math

import jax
import jax.numpy as jnp
from jax import lax
from jax.experimental import pallas as pl
from jax.experimental.pallas import tpu as pltpu
from jax.sharding import PartitionSpec as P

two_pi = 2.0 * math.pi
LANES = 128
HALF = LANES // 2
SUBLANES = 8
CHUNKS = 2


def shifted_down(value, amount):
    rows = lax.broadcasted_iota(jnp.int32, value.shape, 0)
    return jnp.where(rows >= amount, pltpu.roll(value, amount, 0), 0.0)


def scanned(pieces):
    sums, carry = [], None
    for value in pieces:
        amount = 1
        while amount < SUBLANES:
            value = value + shifted_down(value, amount)
            amount *= 2
        if carry is not None:
            value = value + carry
        carry = jnp.broadcast_to(value[SUBLANES - 1 :, :], value.shape)
        sums.append(value)
    return sums


def total(pieces):
    value = functools.reduce(jnp.add, pieces)
    return jnp.sum(value, axis=0, keepdims=True)


def split(value):
    high = value.astype(jnp.bfloat16)
    return high, (value - high.astype(jnp.float32)).astype(jnp.bfloat16)


def store_split(high_ref, low_ref, cable, block, sums):
    for pair in range(0, len(sums), 2):
        rows = pl.ds(pair * SUBLANES, 2 * SUBLANES)
        high, low = split(jnp.concatenate(sums[pair : pair + 2], axis=0))
        high_ref[cable, block, rows, :] = high
        low_ref[cable, block, rows, :] = low


def edges_kernel(phase_hbm, wrap_hbm, inner_ref, outer_ref, phase_ref, wrap_ref, sem):
    cables, time, width = phase_hbm.shape
    is_even = lax.rem(lax.axis_index("chan"), 2) == 0
    sends_last = (is_even, jnp.logical_not(is_even))
    copies = []
    for side, last in enumerate(sends_last):
        lanes = pl.ds(pl.multiple_of(jnp.where(last, width - LANES, 0), LANES), LANES)
        for kind, (source, target) in enumerate(((phase_hbm, phase_ref), (wrap_hbm, wrap_ref))):
            copies.append(
                pltpu.make_async_copy(source.at[:, :, lanes], target.at[side], sem.at[kind, side])
            )
    for copy in copies:
        copy.start()
    for copy in copies:
        copy.wait()
    lane = lax.broadcasted_iota(jnp.int32, (time, LANES), 1)
    for side, (last, target) in enumerate(zip(sends_last, (inner_ref, outer_ref))):
        for cable in range(cables // 2):
            low, high = (
                phase_ref[side, c] + two_pi * wrap_ref[side, c].astype(jnp.float32)
                for c in (cable, cable + cables // 2)
            )
            low = jnp.where(last, pltpu.roll(low, HALF, 1), low)
            high = jnp.where(last, high, pltpu.roll(high, HALF, 1))
            target[cable] = jnp.where(lane < HALF, low, high)


def backwards(value):
    lane = lax.broadcasted_iota(jnp.int32, value.shape, 1)
    bit = 1
    while bit < LANES:
        value = jnp.where(
            (lane & bit) == 0, pltpu.roll(value, LANES - bit, 1), pltpu.roll(value, bit, 1)
        )
        bit *= 2
    return value


def increments_kernel(
    phase_ref, wrap_hbm, taps_ref, high_ref, low_ref, totals_ref, sums_ref, weight_ref, wrap_ref,
    reversed_ref, sem,
):
    cables, time, width = phase_ref.shape
    blocks = width // LANES
    groups = time // SUBLANES

    def copy(cable):
        return pltpu.make_async_copy(wrap_hbm.at[cable], wrap_ref.at[cable], sem.at[cable])

    for cable in range(cables):
        copy(cable).start()

    lane = lax.broadcasted_iota(jnp.int32, taps_ref.shape, 1)
    taps = jnp.where(lane == HALF, 1.0, 0.0) - taps_ref[...]
    reversed_ref[...] = pltpu.roll(backwards(taps * (1.0 / (4.0 * two_pi))), 1, 1)
    inputs = lax.broadcasted_iota(jnp.int32, (LANES, LANES), 0)
    outputs = lax.broadcasted_iota(jnp.int32, (LANES, LANES), 1)

    @pl.loop(0, cables)
    def _(cable):
        row = jnp.broadcast_to(reversed_ref[pl.ds(cable, 1), :], (LANES, LANES))
        circulant = pltpu.roll(row, 0, 1, stride=1, stride_axis=0)
        for column, mask in enumerate((inputs >= outputs, inputs < outputs)):
            high, low = split(jnp.where(mask, circulant, 0.0))
            for place, part in enumerate((high, high, low, low)):
                rows, lanes = pl.ds(place * LANES, LANES), pl.ds(column * LANES, LANES)
                weight_ref[cable, rows, lanes] = part

    def cable_step(cable, accumulated):
        copy(cable).wait()

        def block_step(block, accumulated):
            lanes = pl.ds(pl.multiple_of(block * LANES, LANES), LANES)
            pieces = []
            for i in range(groups):
                rows = pl.ds(i * SUBLANES, SUBLANES)
                turns = wrap_ref[cable, rows, lanes].astype(jnp.float32)
                pieces.append(phase_ref[cable, rows, lanes] + two_pi * turns)
            store_split(high_ref, low_ref, cable, block, pieces)
            totals_ref[pl.ds(block * cables + cable, 1), :] = total(pieces)
            return tuple(a + b for a, b in zip(accumulated, pieces))

        return lax.fori_loop(0, blocks, block_step, accumulated, unroll=16)

    zeros = tuple(jnp.zeros((SUBLANES, LANES), jnp.float32) for _ in range(groups))
    accumulated = scanned(lax.fori_loop(0, cables, cable_step, zeros))
    lane = lax.broadcasted_iota(jnp.int32, (SUBLANES, LANES), 1)
    tile = jnp.zeros((SUBLANES, LANES), jnp.float32)
    for i, value in enumerate(accumulated):
        tile = jnp.where(lane == i, jnp.sum(value, axis=1, keepdims=True), tile)
    sums_ref[...] = tile


def halo_kernel(inner_ref, outer_ref, high_ref, low_ref, totals_ref):
    pairs, time, _ = inner_ref.shape
    cables = 2 * pairs
    groups = time // SUBLANES
    place = lax.axis_index("chan")
    is_even = lax.rem(place, 2) == 0
    at_end = (place == 0) | (place == lax.axis_size("chan") - 1)
    for pair in range(pairs):
        inner, outer = (
            [ref[pair, pl.ds(i * SUBLANES, SUBLANES), :] for i in range(groups)]
            for ref in (inner_ref, outer_ref)
        )
        outer = [jnp.where(at_end, 0.0, value) for value in outer]
        right = [jnp.where(is_even, a, b) for a, b in zip(inner, outer)]
        left = [jnp.where(is_even, b, a) for a, b in zip(inner, outer)]
        for block, pieces, moved in ((0, right, pair + pairs), (1, left, pair)):
            for cable in (pair, pair + pairs):
                placed = [pltpu.roll(v, HALF, 1) for v in pieces] if cable == moved else pieces
                store_split(high_ref, low_ref, cable, block, placed)
                totals_ref[pl.ds(block * cables + cable, 1), :] = total(placed)


def filter_kernel(first, high_ref, low_ref, halo_high_ref, halo_low_ref, weight_ref, local_ref):
    _, blocks, time, _ = high_ref.shape
    groups = time // SUBLANES
    lane = lax.broadcasted_iota(jnp.int32, (time, LANES), 1)

    @pl.loop(0, local_ref.shape[0])
    def _(index):
        cable = first + index
        high, low = (
            jnp.concatenate(
                [main[cable].reshape(blocks * time, LANES), halo[cable].reshape(2 * time, LANES)],
                axis=0,
            )
            for main, halo in ((high_ref, halo_high_ref), (low_ref, halo_low_ref))
        )
        product = jnp.dot(
            jnp.concatenate([high, low, high, low], axis=1),
            weight_ref[cable],
            preferred_element_type=jnp.float32,
        )

        def rolled(block):
            here = block if block >= 0 else blocks + 1
            there = block + 1
            return pltpu.roll(
                product[here * time : (here + 1) * time, :LANES]
                + product[there * time : (there + 1) * time, LANES:],
                HALF,
                1,
            )

        previous = rolled(-1)
        for block in range(blocks):
            following = rolled(block)
            value = jnp.where(lane < HALF, previous, following)
            pieces = [value[i * SUBLANES : (i + 1) * SUBLANES] for i in range(groups)]
            for i, piece in enumerate(scanned(pieces)):
                local_ref[index, block, pl.ds(i * SUBLANES, SUBLANES), :] = piece
            previous = following


def level_kernel(
    population, local_refs, weight_ref, totals_refs, sums_ref, earlier_refs, coupling_ref,
    out_hbm, stage_ref, offset_ref, sem,
):
    _, blocks, time, _ = local_refs[0].shape
    span = blocks * LANES // CHUNKS
    cables = out_hbm.shape[0]
    groups = time // SUBLANES
    step, place = lax.axis_index("tm"), lax.axis_index("chan")
    inside_left = jnp.where(place == 0, 0.0, 1.0)
    inside_right = jnp.where(place == lax.axis_size("chan") - 1, 0.0, 1.0)

    def from_earlier(refs):
        value = jnp.zeros(refs[0].shape, jnp.float32)
        for bit, ref in enumerate(refs):
            value = value + jnp.where((step & (1 << bit)) != 0, ref[...], 0.0)
        return value

    offset_ref[...] = from_earlier(totals_refs)
    earlier = from_earlier(earlier_refs)[SUBLANES - 1 :, groups - 1 : groups]
    common = (sums_ref[...] + earlier) * (1.0 / population)
    columns = [
        jnp.broadcast_to(common[:, i : i + 1], (SUBLANES, LANES)) for i in range(groups)
    ]
    used = blocks + 2
    padded = -(-(used + 1) // SUBLANES) * SUBLANES
    row = lax.broadcasted_iota(jnp.int32, (padded, LANES), 0)
    lane = lax.broadcasted_iota(jnp.int32, (padded, LANES), 1)

    def filtered_offset(cable):
        offset = jnp.concatenate(
            [
                offset_ref[pl.ds(cable, used, stride=cables), :],
                jnp.ones((padded - used, LANES), jnp.float32),
            ],
            axis=0,
        )
        high, low = split(offset)
        product = jnp.dot(
            jnp.concatenate([high, low, high, low], axis=1),
            weight_ref[cable],
            preferred_element_type=jnp.float32,
        )
        here, there = product[:, :LANES], product[:, LANES:]
        left = pltpu.roll(here[used - 1 : used] + there[:1], HALF, 1)
        following = pltpu.roll(here + pltpu.roll(there, padded - 1, 0), HALF, 1)
        previous = jnp.where(row == 0, left, pltpu.roll(following, 1, 0))
        bias = jnp.where(lane < HALF, previous, following)
        here, there = here[used : used + 1], there[used : used + 1]
        middle = pltpu.roll(here + there, HALF, 1)
        first = pltpu.roll(here * inside_left + there, HALF, 1)
        last = pltpu.roll(here + there * inside_right, HALF, 1)
        first = jnp.where(lane[:1] < HALF, first, middle)
        last = jnp.where(lane[:1] < HALF, middle, last)
        return bias, first, middle, last

    def written(cable, chunk):
        lanes = pl.ds(chunk * span, span)
        return pltpu.make_async_copy(
            stage_ref.at[cable, :, lanes], out_hbm.at[cable, :, lanes], sem.at[cable, chunk]
        )

    carry = filtered_offset(0)
    first_cable = 0
    for local_ref in local_refs:

        def cable_step(index, carry, first_cable=first_cable, local_ref=local_ref):
            cable = first_cable + index
            following = filtered_offset(jnp.minimum(cable + 1, cables - 1))
            bias, first, middle, last = carry
            shifts = [coupling_ref[cable] * column for column in columns]
            inner = [shift * middle for shift in shifts]
            for block in range(blocks):
                lanes = pl.ds(block * LANES, LANES)
                added = jnp.broadcast_to(bias[block : block + 1, :], (SUBLANES, LANES))
                if block == 0:
                    slopes = [shift * first for shift in shifts]
                elif block == blocks - 1:
                    slopes = [shift * last for shift in shifts]
                else:
                    slopes = inner
                for i in range(groups):
                    rows = pl.ds(i * SUBLANES, SUBLANES)
                    stage_ref[cable, rows, lanes] = local_ref[index, block, rows, :] + (
                        added - slopes[i]
                    )
                if (block + 1) % (blocks // CHUNKS) == 0:
                    written(cable, block // (blocks // CHUNKS)).start()
            return following

        carry = lax.fori_loop(0, local_ref.shape[0], cable_step, carry)
        first_cable += local_ref.shape[0]
    for cable in range(cables):
        for chunk in range(CHUNKS):
            written(cable, chunk).wait()


def swapped(value, axis, bit):
    return lax.ppermute(value, axis, [(i, i ^ bit) for i in range(lax.axis_size(axis))])


def shards(phase_step, wrap_count, coupling, filter_taps):
    cables, time, width = phase_step.shape
    blocks = width // LANES
    steps, places = lax.axis_size("tm"), lax.axis_size("chan")
    population = cables * width * places
    bounds = [0, cables // 2, 3 * cables // 4, cables]
    parts = len(bounds) - 1
    wrap_count = pltpu.with_memory_space_constraint(wrap_count, pltpu.HBM)
    whole = pl.BlockSpec(memory_space=pltpu.VMEM)
    outside = pl.BlockSpec(memory_space=pl.ANY)
    scalars = pl.BlockSpec(memory_space=pltpu.SMEM)

    inner, outer = pl.pallas_call(
        edges_kernel,
        out_shape=[pltpu.VMEM((cables // 2, time, LANES), jnp.float32)] * 2,
        in_specs=[outside] * 2,
        out_specs=[whole] * 2,
        scratch_shapes=[
            pltpu.VMEM((2, cables, time, LANES), jnp.float32),
            pltpu.VMEM((2, cables, time, LANES), jnp.int32),
            pltpu.SemaphoreType.DMA((2, 2)),
        ],
        compiler_params=pltpu.CompilerParams(vmem_limit_bytes=8 << 20),
        name="edges",
    )(pltpu.with_memory_space_constraint(phase_step, pltpu.HBM), wrap_count)
    outer_pairs = [(i, (i + (1 if i % 2 else -1)) % places) for i in range(places)]
    outer = lax.ppermute(outer, "chan", outer_pairs)
    inner = swapped(inner, "chan", 1)

    high, low, totals, sums, weight = pl.pallas_call(
        increments_kernel,
        out_shape=(
            pltpu.VMEM((cables, blocks, time, LANES), jnp.bfloat16),
            pltpu.VMEM((cables, blocks, time, LANES), jnp.bfloat16),
            pltpu.VMEM((blocks * cables, LANES), jnp.float32),
            pltpu.VMEM((SUBLANES, LANES), jnp.float32),
            pltpu.VMEM((cables, 4 * LANES, 2 * LANES), jnp.bfloat16),
        ),
        in_specs=[whole, outside, whole],
        out_specs=[whole] * 5,
        scratch_shapes=[
            pltpu.VMEM((cables, time, width), jnp.int32),
            pltpu.VMEM(filter_taps.shape, jnp.float32),
            pltpu.SemaphoreType.DMA((cables,)),
        ],
        compiler_params=pltpu.CompilerParams(vmem_limit_bytes=16 << 20),
        cost_estimate=pl.CostEstimate(
            flops=0, bytes_accessed=phase_step.size * 4, transcendentals=0
        ),
        name="increments",
    )(pltpu.with_memory_space_constraint(phase_step, pltpu.VMEM), wrap_count, filter_taps)

    halo_high, halo_low, halo_totals = pl.pallas_call(
        halo_kernel,
        out_shape=(
            pltpu.VMEM((cables, 2, time, LANES), jnp.bfloat16),
            pltpu.VMEM((cables, 2, time, LANES), jnp.bfloat16),
            pltpu.VMEM((2 * cables, LANES), jnp.float32),
        ),
        in_specs=[whole] * 2,
        out_specs=[whole] * 3,
        compiler_params=pltpu.CompilerParams(vmem_limit_bytes=8 << 20),
        name="halo",
    )(inner, outer)

    def filtered(part, weight):
        share = bounds[part + 1] - bounds[part]
        return pl.pallas_call(
            functools.partial(filter_kernel, bounds[part]),
            out_shape=pltpu.VMEM((share, blocks, time, LANES), jnp.float32),
            in_specs=[whole] * 5,
            out_specs=whole,
            compiler_params=pltpu.CompilerParams(vmem_limit_bytes=16 << 20),
            cost_estimate=pl.CostEstimate(
                flops=2 * share * (blocks + 2) * time * 8 * LANES * LANES,
                bytes_accessed=1 << 20,
                transcendentals=0,
            ),
            name="filter",
        )(high, low, halo_high, halo_low, weight)

    running = jnp.concatenate([totals, halo_totals], axis=0)
    received = [swapped(running, "tm", 1)]
    sums, halo_totals = lax.optimization_barrier((sums, halo_totals))
    rounds = [("chan", 1 << bit) for bit in range(places.bit_length() - 1)]
    rounds += [("tm", 1 << bit) for bit in range(steps.bit_length() - 1)]
    local, received_sums, chan_sums, ready = [], [], sums, None
    for number, (axis, bit) in enumerate(rounds):
        incoming = swapped(sums, axis, bit)
        if number % 2 == 0 and number > 0 and ready is not None:
            received.append(swapped(ready, "tm", 1 << len(received)))
            ready = None
        elif number > 0 and len(local) < parts:
            tied, sums = lax.optimization_barrier((weight, sums))
            part = filtered(len(local), tied)
            incoming, part = lax.optimization_barrier((incoming, part))
            local.append(part)
        if number % 2 == 1 and 1 << len(received) < steps:
            running = running + received[-1]
            ready, incoming = lax.optimization_barrier((running, incoming))
        if axis == "tm":
            received_sums.append(incoming)
        sums = sums + incoming
        if axis == "chan":
            chan_sums = sums
    while 1 << len(received) < steps:
        running = running + received[-1] if ready is None else ready
        ready = None
        received.append(swapped(running, "tm", 1 << len(received)))
    while len(local) < parts:
        local.append(filtered(len(local), weight))

    return pl.pallas_call(
        functools.partial(level_kernel, population),
        out_shape=jax.ShapeDtypeStruct(phase_step.shape, jnp.float32),
        in_specs=[
            [whole] * parts, whole, [whole] * len(received), whole, [whole] * len(received), scalars
        ],
        out_specs=outside,
        scratch_shapes=[
            pltpu.VMEM((cables, time, width), jnp.float32),
            pltpu.VMEM(((blocks + 2) * cables, LANES), jnp.float32),
            pltpu.SemaphoreType.DMA((cables, CHUNKS)),
        ],
        compiler_params=pltpu.CompilerParams(vmem_limit_bytes=24 << 20),
        name="level",
    )(local, weight, received, chan_sums, received_sums, coupling)


def solution(mesh):
    placed = (P(None, "tm", "chan"), P(None, "tm", "chan"), P(), P())
    return jax.shard_map(
        shards, mesh=mesh, in_specs=placed, out_specs=P(None, "tm", "chan"), check_vma=False
    )
```

```python
import functools
import math

import jax
import jax.numpy as jnp
from jax import lax
from jax.experimental import pallas as pl
from jax.experimental.pallas import tpu as pltpu
from jax.sharding import PartitionSpec as P

two_pi = 2.0 * math.pi
LANES = 128
HALF = LANES // 2
SUBLANES = 8
MASK_FLOPS = 570000000
CHUNKS = 2


def shifted_down(value, amount):
    rows = lax.broadcasted_iota(jnp.int32, value.shape, 0)
    return jnp.where(rows >= amount, pltpu.roll(value, amount, 0), 0.0)


def scanned(pieces):
    sums, carry = [], None
    for value in pieces:
        amount = 1
        while amount < SUBLANES:
            value = value + shifted_down(value, amount)
            amount *= 2
        if carry is not None:
            value = value + carry
        carry = jnp.broadcast_to(value[SUBLANES - 1 :, :], value.shape)
        sums.append(value)
    return sums


def total(pieces):
    value = functools.reduce(jnp.add, pieces)
    return jnp.sum(value, axis=0, keepdims=True)


def split(value):
    high = value.astype(jnp.bfloat16)
    return high, (value - high.astype(jnp.float32)).astype(jnp.bfloat16)


def store_split(high_ref, low_ref, cable, block, sums):
    for pair in range(0, len(sums), 2):
        rows = pl.ds(pair * SUBLANES, 2 * SUBLANES)
        high, low = split(jnp.concatenate(sums[pair : pair + 2], axis=0))
        high_ref[cable, block, rows, :] = high
        low_ref[cable, block, rows, :] = low


def edges_kernel(phase_hbm, wrap_hbm, inner_ref, outer_ref, phase_ref, wrap_ref, sem):
    cables, time, width = phase_hbm.shape
    is_even = lax.rem(lax.axis_index("chan"), 2) == 0
    sends_last = (is_even, jnp.logical_not(is_even))
    copies = []
    for side, last in enumerate(sends_last):
        lanes = pl.ds(pl.multiple_of(jnp.where(last, width - LANES, 0), LANES), LANES)
        for kind, (source, target) in enumerate(((phase_hbm, phase_ref), (wrap_hbm, wrap_ref))):
            copies.append(
                pltpu.make_async_copy(source.at[:, :, lanes], target.at[side], sem.at[kind, side])
            )
    for copy in copies:
        copy.start()
    for copy in copies:
        copy.wait()
    lane = lax.broadcasted_iota(jnp.int32, (time, LANES), 1)
    for side, (last, target) in enumerate(zip(sends_last, (inner_ref, outer_ref))):
        for cable in range(cables // 2):
            low, high = (
                phase_ref[side, c] + two_pi * wrap_ref[side, c].astype(jnp.float32)
                for c in (cable, cable + cables // 2)
            )
            low = jnp.where(last, pltpu.roll(low, HALF, 1), low)
            high = jnp.where(last, high, pltpu.roll(high, HALF, 1))
            target[cable] = jnp.where(lane < HALF, low, high)


def backwards(value):
    lane = lax.broadcasted_iota(jnp.int32, value.shape, 1)
    bit = 1
    while bit < LANES:
        value = jnp.where(
            (lane & bit) == 0, pltpu.roll(value, LANES - bit, 1), pltpu.roll(value, bit, 1)
        )
        bit *= 2
    return value


def increments_kernel(
    phase_ref, wrap_hbm, taps_ref, high_ref, low_ref, totals_ref, sums_ref, weight_ref, wrap_ref,
    reversed_ref, sem,
):
    cables, time, width = phase_ref.shape
    blocks = width // LANES
    groups = time // SUBLANES

    def copy(cable):
        return pltpu.make_async_copy(wrap_hbm.at[cable], wrap_ref.at[cable], sem.at[cable])

    for cable in range(cables):
        copy(cable).start()

    lane = lax.broadcasted_iota(jnp.int32, taps_ref.shape, 1)
    taps = jnp.where(lane == HALF, 1.0, 0.0) - taps_ref[...]
    reversed_ref[...] = pltpu.roll(backwards(taps * (1.0 / (4.0 * two_pi))), 1, 1)
    inputs = lax.broadcasted_iota(jnp.int32, (LANES, LANES), 0)
    outputs = lax.broadcasted_iota(jnp.int32, (LANES, LANES), 1)

    @pl.loop(0, cables)
    def _(cable):
        row = jnp.broadcast_to(reversed_ref[pl.ds(cable, 1), :], (LANES, LANES))
        circulant = pltpu.roll(row, 0, 1, stride=1, stride_axis=0)
        for column, mask in enumerate((inputs >= outputs, inputs < outputs)):
            high, low = split(jnp.where(mask, circulant, 0.0))
            for place, part in enumerate((high, high, low, low)):
                rows, lanes = pl.ds(place * LANES, LANES), pl.ds(column * LANES, LANES)
                weight_ref[cable, rows, lanes] = part

    def cable_step(cable, accumulated):
        copy(cable).wait()

        def block_step(block, accumulated):
            lanes = pl.ds(pl.multiple_of(block * LANES, LANES), LANES)
            pieces = []
            for i in range(groups):
                rows = pl.ds(i * SUBLANES, SUBLANES)
                turns = wrap_ref[cable, rows, lanes].astype(jnp.float32)
                pieces.append(phase_ref[cable, rows, lanes] + two_pi * turns)
            store_split(high_ref, low_ref, cable, block, pieces)
            totals_ref[pl.ds(block * cables + cable, 1), :] = total(pieces)
            return tuple(a + b for a, b in zip(accumulated, pieces))

        return lax.fori_loop(0, blocks, block_step, accumulated, unroll=16)

    zeros = tuple(jnp.zeros((SUBLANES, LANES), jnp.float32) for _ in range(groups))
    accumulated = scanned(lax.fori_loop(0, cables, cable_step, zeros))
    lane = lax.broadcasted_iota(jnp.int32, (SUBLANES, LANES), 1)
    tile = jnp.zeros((SUBLANES, LANES), jnp.float32)
    for i, value in enumerate(accumulated):
        tile = jnp.where(lane == i, jnp.sum(value, axis=1, keepdims=True), tile)
    sums_ref[...] = tile


def halo_kernel(inner_ref, outer_ref, high_ref, low_ref, totals_ref):
    pairs, time, _ = inner_ref.shape
    cables = 2 * pairs
    groups = time // SUBLANES
    place = lax.axis_index("chan")
    is_even = lax.rem(place, 2) == 0
    at_end = (place == 0) | (place == lax.axis_size("chan") - 1)
    for pair in range(pairs):
        inner, outer = (
            [ref[pair, pl.ds(i * SUBLANES, SUBLANES), :] for i in range(groups)]
            for ref in (inner_ref, outer_ref)
        )
        outer = [jnp.where(at_end, 0.0, value) for value in outer]
        right = [jnp.where(is_even, a, b) for a, b in zip(inner, outer)]
        left = [jnp.where(is_even, b, a) for a, b in zip(inner, outer)]
        for block, pieces, moved in ((0, right, pair + pairs), (1, left, pair)):
            for cable in (pair, pair + pairs):
                placed = [pltpu.roll(v, HALF, 1) for v in pieces] if cable == moved else pieces
                store_split(high_ref, low_ref, cable, block, placed)
                totals_ref[pl.ds(block * cables + cable, 1), :] = total(placed)


def filter_kernel(first, high_ref, low_ref, halo_high_ref, halo_low_ref, weight_ref, local_ref):
    _, blocks, time, _ = high_ref.shape
    groups = time // SUBLANES
    lane = lax.broadcasted_iota(jnp.int32, (time, LANES), 1)

    @pl.loop(0, local_ref.shape[0])
    def _(index):
        cable = first + index
        high, low = (
            jnp.concatenate(
                [main[cable].reshape(blocks * time, LANES), halo[cable].reshape(2 * time, LANES)],
                axis=0,
            )
            for main, halo in ((high_ref, halo_high_ref), (low_ref, halo_low_ref))
        )
        product = jnp.dot(
            jnp.concatenate([high, low, high, low], axis=1),
            weight_ref[cable],
            preferred_element_type=jnp.float32,
        )

        def rolled(block):
            here = block if block >= 0 else blocks + 1
            there = block + 1
            return pltpu.roll(
                product[here * time : (here + 1) * time, :LANES]
                + product[there * time : (there + 1) * time, LANES:],
                HALF,
                1,
            )

        previous = rolled(-1)
        for block in range(blocks):
            following = rolled(block)
            value = jnp.where(lane < HALF, previous, following)
            pieces = [value[i * SUBLANES : (i + 1) * SUBLANES] for i in range(groups)]
            for i, piece in enumerate(scanned(pieces)):
                local_ref[index, block, pl.ds(i * SUBLANES, SUBLANES), :] = piece
            previous = following


def masked_kernel(bit, value_ref, masked_ref):
    later = (lax.axis_index("tm") & bit) != 0
    masked_ref[...] = jnp.where(later, value_ref[...], 0.0)


def level_kernel(
    population, local_refs, weight_ref, totals_refs, sums_ref, earlier_refs, coupling_ref,
    out_hbm, stage_ref, offset_ref, sem,
):
    _, blocks, time, _ = local_refs[0].shape
    span = blocks * LANES // CHUNKS
    cables = out_hbm.shape[0]
    groups = time // SUBLANES
    step, place = lax.axis_index("tm"), lax.axis_index("chan")
    inside_left = jnp.where(place == 0, 0.0, 1.0)
    inside_right = jnp.where(place == lax.axis_size("chan") - 1, 0.0, 1.0)

    earlier = jnp.zeros((SUBLANES, LANES), jnp.float32)
    for bit, ref in enumerate(earlier_refs):
        earlier = earlier + jnp.where((step & (1 << bit)) != 0, ref[...], 0.0)
    offset_ref[...] = functools.reduce(jnp.add, [ref[...] for ref in totals_refs])
    earlier = earlier[SUBLANES - 1 :, groups - 1 : groups]
    common = (sums_ref[...] + earlier) * (1.0 / population)
    columns = [
        jnp.broadcast_to(common[:, i : i + 1], (SUBLANES, LANES)) for i in range(groups)
    ]
    used = blocks + 2
    padded = -(-(used + 1) // SUBLANES) * SUBLANES
    row = lax.broadcasted_iota(jnp.int32, (padded, LANES), 0)
    lane = lax.broadcasted_iota(jnp.int32, (padded, LANES), 1)

    def filtered_offset(cable):
        offset = jnp.concatenate(
            [
                offset_ref[pl.ds(cable, used, stride=cables), :],
                jnp.ones((padded - used, LANES), jnp.float32),
            ],
            axis=0,
        )
        high, low = split(offset)
        product = jnp.dot(
            jnp.concatenate([high, low, high, low], axis=1),
            weight_ref[cable],
            preferred_element_type=jnp.float32,
        )
        here, there = product[:, :LANES], product[:, LANES:]
        left = pltpu.roll(here[used - 1 : used] + there[:1], HALF, 1)
        following = pltpu.roll(here + pltpu.roll(there, padded - 1, 0), HALF, 1)
        previous = jnp.where(row == 0, left, pltpu.roll(following, 1, 0))
        bias = jnp.where(lane < HALF, previous, following)
        here, there = here[used : used + 1], there[used : used + 1]
        middle = pltpu.roll(here + there, HALF, 1)
        first = pltpu.roll(here * inside_left + there, HALF, 1)
        last = pltpu.roll(here + there * inside_right, HALF, 1)
        first = jnp.where(lane[:1] < HALF, first, middle)
        last = jnp.where(lane[:1] < HALF, middle, last)
        return bias, first, middle, last

    def written(cable, chunk):
        lanes = pl.ds(chunk * span, span)
        return pltpu.make_async_copy(
            stage_ref.at[cable, :, lanes], out_hbm.at[cable, :, lanes], sem.at[cable, chunk]
        )

    carry = filtered_offset(0)
    first_cable = 0
    for local_ref in local_refs:

        def cable_step(index, carry, first_cable=first_cable, local_ref=local_ref):
            cable = first_cable + index
            following = filtered_offset(jnp.minimum(cable + 1, cables - 1))
            bias, first, middle, last = carry
            shifts = [coupling_ref[cable] * column for column in columns]
            inner = [shift * middle for shift in shifts]
            for block in range(blocks):
                lanes = pl.ds(block * LANES, LANES)
                added = jnp.broadcast_to(bias[block : block + 1, :], (SUBLANES, LANES))
                if block == 0:
                    slopes = [shift * first for shift in shifts]
                elif block == blocks - 1:
                    slopes = [shift * last for shift in shifts]
                else:
                    slopes = inner
                for i in range(groups):
                    rows = pl.ds(i * SUBLANES, SUBLANES)
                    stage_ref[cable, rows, lanes] = local_ref[index, block, rows, :] + (
                        added - slopes[i]
                    )
                if (block + 1) % (blocks // CHUNKS) == 0:
                    written(cable, block // (blocks // CHUNKS)).start()
            return following

        carry = lax.fori_loop(0, local_ref.shape[0], cable_step, carry)
        first_cable += local_ref.shape[0]
    for cable in range(cables):
        for chunk in range(CHUNKS):
            written(cable, chunk).wait()


def swapped(value, axis, bit):
    return lax.ppermute(value, axis, [(i, i ^ bit) for i in range(lax.axis_size(axis))])


def shards(phase_step, wrap_count, coupling, filter_taps):
    cables, time, width = phase_step.shape
    blocks = width // LANES
    steps, places = lax.axis_size("tm"), lax.axis_size("chan")
    population = cables * width * places
    bounds = [0, 3 * cables // 8, 3 * cables // 4, cables]
    parts = len(bounds) - 1
    wrap_count = pltpu.with_memory_space_constraint(wrap_count, pltpu.HBM)
    whole = pl.BlockSpec(memory_space=pltpu.VMEM)
    outside = pl.BlockSpec(memory_space=pl.ANY)
    scalars = pl.BlockSpec(memory_space=pltpu.SMEM)

    inner, outer = pl.pallas_call(
        edges_kernel,
        out_shape=[pltpu.VMEM((cables // 2, time, LANES), jnp.float32)] * 2,
        in_specs=[outside] * 2,
        out_specs=[whole] * 2,
        scratch_shapes=[
            pltpu.VMEM((2, cables, time, LANES), jnp.float32),
            pltpu.VMEM((2, cables, time, LANES), jnp.int32),
            pltpu.SemaphoreType.DMA((2, 2)),
        ],
        compiler_params=pltpu.CompilerParams(vmem_limit_bytes=8 << 20),
        name="edges",
    )(pltpu.with_memory_space_constraint(phase_step, pltpu.HBM), wrap_count)
    outer_pairs = [(i, (i + (1 if i % 2 else -1)) % places) for i in range(places)]
    outer = lax.ppermute(outer, "chan", outer_pairs)
    inner = swapped(inner, "chan", 1)

    high, low, totals, sums, weight = pl.pallas_call(
        increments_kernel,
        out_shape=(
            pltpu.VMEM((cables, blocks, time, LANES), jnp.bfloat16),
            pltpu.VMEM((cables, blocks, time, LANES), jnp.bfloat16),
            pltpu.VMEM((blocks * cables, LANES), jnp.float32),
            pltpu.VMEM((SUBLANES, LANES), jnp.float32),
            pltpu.VMEM((cables, 4 * LANES, 2 * LANES), jnp.bfloat16),
        ),
        in_specs=[whole, outside, whole],
        out_specs=[whole] * 5,
        scratch_shapes=[
            pltpu.VMEM((cables, time, width), jnp.int32),
            pltpu.VMEM(filter_taps.shape, jnp.float32),
            pltpu.SemaphoreType.DMA((cables,)),
        ],
        compiler_params=pltpu.CompilerParams(vmem_limit_bytes=16 << 20),
        cost_estimate=pl.CostEstimate(
            flops=0, bytes_accessed=phase_step.size * 4, transcendentals=0
        ),
        name="increments",
    )(pltpu.with_memory_space_constraint(phase_step, pltpu.VMEM), wrap_count, filter_taps)

    halo_high, halo_low, halo_totals = pl.pallas_call(
        halo_kernel,
        out_shape=(
            pltpu.VMEM((cables, 2, time, LANES), jnp.bfloat16),
            pltpu.VMEM((cables, 2, time, LANES), jnp.bfloat16),
            pltpu.VMEM((2 * cables, LANES), jnp.float32),
        ),
        in_specs=[whole] * 2,
        out_specs=[whole] * 3,
        compiler_params=pltpu.CompilerParams(vmem_limit_bytes=8 << 20),
        name="halo",
    )(inner, outer)

    def from_earlier(value, number):
        return pl.pallas_call(
            functools.partial(masked_kernel, 1 << number),
            out_shape=pltpu.VMEM(value.shape, value.dtype),
            in_specs=[whole],
            out_specs=whole,
            compiler_params=pltpu.CompilerParams(vmem_limit_bytes=4 << 20),
            cost_estimate=pl.CostEstimate(
                flops=MASK_FLOPS, bytes_accessed=1 << 20, transcendentals=0
            ),
            name="masked",
        )(value)

    def filtered(part, weight):
        share = bounds[part + 1] - bounds[part]
        return pl.pallas_call(
            functools.partial(filter_kernel, bounds[part]),
            out_shape=pltpu.VMEM((share, blocks, time, LANES), jnp.float32),
            in_specs=[whole] * 5,
            out_specs=whole,
            compiler_params=pltpu.CompilerParams(vmem_limit_bytes=16 << 20),
            cost_estimate=pl.CostEstimate(
                flops=2 * share * (blocks + 2) * time * 8 * LANES * LANES,
                bytes_accessed=1 << 20,
                transcendentals=0,
            ),
            name="filter",
        )(high, low, halo_high, halo_low, weight)

    running = jnp.concatenate([totals, halo_totals], axis=0)
    received = [swapped(running, "tm", 1)]
    sums, halo_totals = lax.optimization_barrier((sums, halo_totals))
    rounds = [("chan", 1 << bit) for bit in range(places.bit_length() - 1)]
    rounds += [("tm", 1 << bit) for bit in range(steps.bit_length() - 1)]
    local, received_sums, chan_sums, ready = [], [], sums, None
    for number, (axis, bit) in enumerate(rounds):
        incoming = swapped(sums, axis, bit)
        if number % 2 == 0 and number > 0 and ready is not None:
            received.append(swapped(ready, "tm", 1 << len(received)))
            ready = None
        elif number > 0 and len(local) < parts:
            tied, sums = lax.optimization_barrier((weight, sums))
            if number == len(rounds) - 1 and 1 << len(received) >= steps:
                received[1] = from_earlier(received[1], 1)
                received[1], tied = lax.optimization_barrier((received[1], tied))
            part = filtered(len(local), tied)
            incoming, part = lax.optimization_barrier((incoming, part))
            local.append(part)
        if number == 2:
            first, sums = lax.optimization_barrier((received[0], sums))
            masked = from_earlier(first, 0)
            incoming, masked = lax.optimization_barrier((incoming, masked))
        if number == 1 and 1 << len(received) < steps:
            earlier, local[-1] = lax.optimization_barrier((received[-1], local[-1]))
            ready = running = running + earlier
        if axis == "tm":
            received_sums.append(incoming)
        sums = sums + incoming
        if axis == "chan":
            chan_sums = sums
    while 1 << len(received) < steps:
        running = running + received[-1] if ready is None else ready
        ready = None
        received.append(swapped(running, "tm", 1 << len(received)))
    while len(local) < parts:
        local.append(filtered(len(local), weight))
    offsets = [masked] + received[1:]

    return pl.pallas_call(
        functools.partial(level_kernel, population),
        out_shape=jax.ShapeDtypeStruct(phase_step.shape, jnp.float32),
        in_specs=[
            [whole] * parts, whole, [whole] * len(offsets), whole, [whole] * len(received_sums), scalars
        ],
        out_specs=outside,
        scratch_shapes=[
            pltpu.VMEM((cables, time, width), jnp.float32),
            pltpu.VMEM(((blocks + 2) * cables, LANES), jnp.float32),
            pltpu.SemaphoreType.DMA((cables, CHUNKS)),
        ],
        compiler_params=pltpu.CompilerParams(vmem_limit_bytes=24 << 20),
        name="level",
    )(local, weight, offsets, chan_sums, received_sums, coupling)


def solution(mesh):
    placed = (P(None, "tm", "chan"), P(None, "tm", "chan"), P(), P())
    return jax.shard_map(
        shards, mesh=mesh, in_specs=placed, out_specs=P(None, "tm", "chan"), check_vma=False
    )
```

```python
import functools
import math

import jax
import jax.numpy as jnp
from jax import lax
from jax.experimental import pallas as pl
from jax.experimental.pallas import tpu as pltpu
from jax.sharding import PartitionSpec as P

two_pi = 2.0 * math.pi
LANES = 128
HALF = LANES // 2
SUBLANES = 8
MASK_FLOPS = 570000000
CHUNKS = 2


def shifted_down(value, amount):
    rows = lax.broadcasted_iota(jnp.int32, value.shape, 0)
    return jnp.where(rows >= amount, pltpu.roll(value, amount, 0), 0.0)


def scanned(pieces):
    sums, carry = [], None
    for value in pieces:
        amount = 1
        while amount < SUBLANES:
            value = value + shifted_down(value, amount)
            amount *= 2
        if carry is not None:
            value = value + carry
        carry = jnp.broadcast_to(value[SUBLANES - 1 :, :], value.shape)
        sums.append(value)
    return sums


def total(pieces):
    value = functools.reduce(jnp.add, pieces)
    return jnp.sum(value, axis=0, keepdims=True)


def split(value):
    high = value.astype(jnp.bfloat16)
    return high, (value - high.astype(jnp.float32)).astype(jnp.bfloat16)


def store_split(high_ref, low_ref, cable, block, sums):
    for pair in range(0, len(sums), 2):
        rows = pl.ds(pair * SUBLANES, 2 * SUBLANES)
        high, low = split(jnp.concatenate(sums[pair : pair + 2], axis=0))
        high_ref[cable, block, rows, :] = high
        low_ref[cable, block, rows, :] = low


def edges_kernel(phase_hbm, wrap_hbm, inner_ref, outer_ref, phase_ref, wrap_ref, sem):
    cables, time, width = phase_hbm.shape
    is_even = lax.rem(lax.axis_index("chan"), 2) == 0
    sends_last = (is_even, jnp.logical_not(is_even))
    copies = []
    for side, last in enumerate(sends_last):
        lanes = pl.ds(pl.multiple_of(jnp.where(last, width - LANES, 0), LANES), LANES)
        for kind, (source, target) in enumerate(((phase_hbm, phase_ref), (wrap_hbm, wrap_ref))):
            copies.append(
                pltpu.make_async_copy(source.at[:, :, lanes], target.at[side], sem.at[kind, side])
            )
    for copy in copies:
        copy.start()
    for copy in copies:
        copy.wait()
    lane = lax.broadcasted_iota(jnp.int32, (time, LANES), 1)
    for side, (last, target) in enumerate(zip(sends_last, (inner_ref, outer_ref))):
        for cable in range(cables // 2):
            low, high = (
                phase_ref[side, c] + two_pi * wrap_ref[side, c].astype(jnp.float32)
                for c in (cable, cable + cables // 2)
            )
            low = jnp.where(last, pltpu.roll(low, HALF, 1), low)
            high = jnp.where(last, high, pltpu.roll(high, HALF, 1))
            target[cable] = jnp.where(lane < HALF, low, high)


def backwards(value):
    lane = lax.broadcasted_iota(jnp.int32, value.shape, 1)
    bit = 1
    while bit < LANES:
        value = jnp.where(
            (lane & bit) == 0, pltpu.roll(value, LANES - bit, 1), pltpu.roll(value, bit, 1)
        )
        bit *= 2
    return value


def increments_kernel(
    phase_ref, wrap_hbm, taps_ref, high_ref, low_ref, totals_ref, sums_ref, weight_ref, wrap_ref,
    reversed_ref, sem,
):
    cables, time, width = phase_ref.shape
    blocks = width // LANES
    groups = time // SUBLANES

    def copy(cable):
        return pltpu.make_async_copy(wrap_hbm.at[cable], wrap_ref.at[cable], sem.at[cable])

    for cable in range(cables):
        copy(cable).start()

    lane = lax.broadcasted_iota(jnp.int32, taps_ref.shape, 1)
    taps = jnp.where(lane == HALF, 1.0, 0.0) - taps_ref[...]
    reversed_ref[...] = pltpu.roll(backwards(taps * (1.0 / (4.0 * two_pi))), 1, 1)
    inputs = lax.broadcasted_iota(jnp.int32, (LANES, LANES), 0)
    outputs = lax.broadcasted_iota(jnp.int32, (LANES, LANES), 1)

    @pl.loop(0, cables)
    def _(cable):
        row = jnp.broadcast_to(reversed_ref[pl.ds(cable, 1), :], (LANES, LANES))
        circulant = pltpu.roll(row, 0, 1, stride=1, stride_axis=0)
        for column, mask in enumerate((inputs >= outputs, inputs < outputs)):
            high, low = split(jnp.where(mask, circulant, 0.0))
            for place, part in enumerate((high, high, low, low)):
                rows, lanes = pl.ds(place * LANES, LANES), pl.ds(column * LANES, LANES)
                weight_ref[cable, rows, lanes] = part

    def cable_step(cable, accumulated):
        copy(cable).wait()

        def block_step(block, accumulated):
            lanes = pl.ds(pl.multiple_of(block * LANES, LANES), LANES)
            pieces = []
            for i in range(groups):
                rows = pl.ds(i * SUBLANES, SUBLANES)
                turns = wrap_ref[cable, rows, lanes].astype(jnp.float32)
                pieces.append(phase_ref[cable, rows, lanes] + two_pi * turns)
            store_split(high_ref, low_ref, cable, block, pieces)
            totals_ref[pl.ds(block * cables + cable, 1), :] = total(pieces)
            return tuple(a + b for a, b in zip(accumulated, pieces))

        return lax.fori_loop(0, blocks, block_step, accumulated, unroll=16)

    zeros = tuple(jnp.zeros((SUBLANES, LANES), jnp.float32) for _ in range(groups))
    accumulated = scanned(lax.fori_loop(0, cables, cable_step, zeros))
    lane = lax.broadcasted_iota(jnp.int32, (SUBLANES, LANES), 1)
    tile = jnp.zeros((SUBLANES, LANES), jnp.float32)
    for i, value in enumerate(accumulated):
        tile = jnp.where(lane == i, jnp.sum(value, axis=1, keepdims=True), tile)
    sums_ref[...] = tile


def halo_kernel(inner_ref, outer_ref, high_ref, low_ref, totals_ref):
    pairs, time, _ = inner_ref.shape
    cables = 2 * pairs
    groups = time // SUBLANES
    place = lax.axis_index("chan")
    is_even = lax.rem(place, 2) == 0
    at_end = (place == 0) | (place == lax.axis_size("chan") - 1)
    for pair in range(pairs):
        inner, outer = (
            [ref[pair, pl.ds(i * SUBLANES, SUBLANES), :] for i in range(groups)]
            for ref in (inner_ref, outer_ref)
        )
        outer = [jnp.where(at_end, 0.0, value) for value in outer]
        right = [jnp.where(is_even, a, b) for a, b in zip(inner, outer)]
        left = [jnp.where(is_even, b, a) for a, b in zip(inner, outer)]
        for block, pieces, moved in ((0, right, pair + pairs), (1, left, pair)):
            for cable in (pair, pair + pairs):
                placed = [pltpu.roll(v, HALF, 1) for v in pieces] if cable == moved else pieces
                store_split(high_ref, low_ref, cable, block, placed)
                totals_ref[pl.ds(block * cables + cable, 1), :] = total(placed)


def filter_kernel(first, high_ref, low_ref, halo_high_ref, halo_low_ref, weight_ref, local_ref):
    _, blocks, time, _ = high_ref.shape
    groups = time // SUBLANES
    lane = lax.broadcasted_iota(jnp.int32, (time, LANES), 1)

    @pl.loop(0, local_ref.shape[0])
    def _(index):
        cable = first + index
        high, low = (
            jnp.concatenate(
                [main[cable].reshape(blocks * time, LANES), halo[cable].reshape(2 * time, LANES)],
                axis=0,
            )
            for main, halo in ((high_ref, halo_high_ref), (low_ref, halo_low_ref))
        )
        product = jnp.dot(
            jnp.concatenate([high, low, high, low], axis=1),
            weight_ref[cable],
            preferred_element_type=jnp.float32,
        )

        def rolled(block):
            here = block if block >= 0 else blocks + 1
            there = block + 1
            return pltpu.roll(
                product[here * time : (here + 1) * time, :LANES]
                + product[there * time : (there + 1) * time, LANES:],
                HALF,
                1,
            )

        previous = rolled(-1)
        for block in range(blocks):
            following = rolled(block)
            value = jnp.where(lane < HALF, previous, following)
            pieces = [value[i * SUBLANES : (i + 1) * SUBLANES] for i in range(groups)]
            for i, piece in enumerate(scanned(pieces)):
                local_ref[index, block, pl.ds(i * SUBLANES, SUBLANES), :] = piece
            previous = following


def masked_kernel(bit, value_ref, masked_ref):
    later = (lax.axis_index("tm") & bit) != 0
    masked_ref[...] = jnp.where(later, value_ref[...], 0.0)


def level_kernel(
    population, local_refs, weight_ref, totals_refs, sums_ref, earlier_refs, coupling_ref,
    out_hbm, stage_ref, offset_ref, sem,
):
    _, blocks, time, _ = local_refs[0].shape
    span = blocks * LANES // CHUNKS
    cables = out_hbm.shape[0]
    groups = time // SUBLANES
    step, place = lax.axis_index("tm"), lax.axis_index("chan")
    inside_left = jnp.where(place == 0, 0.0, 1.0)
    inside_right = jnp.where(place == lax.axis_size("chan") - 1, 0.0, 1.0)

    earlier = jnp.zeros((SUBLANES, LANES), jnp.float32)
    for bit, ref in enumerate(earlier_refs):
        earlier = earlier + jnp.where((step & (1 << bit)) != 0, ref[...], 0.0)
    offset_ref[...] = functools.reduce(jnp.add, [ref[...] for ref in totals_refs])
    earlier = earlier[SUBLANES - 1 :, groups - 1 : groups]
    common = (sums_ref[...] + earlier) * (1.0 / population)
    columns = [
        jnp.broadcast_to(common[:, i : i + 1], (SUBLANES, LANES)) for i in range(groups)
    ]
    used = blocks + 2
    padded = -(-(used + 1) // SUBLANES) * SUBLANES
    row = lax.broadcasted_iota(jnp.int32, (padded, LANES), 0)
    lane = lax.broadcasted_iota(jnp.int32, (padded, LANES), 1)

    def filtered_offset(cable):
        offset = jnp.concatenate(
            [
                offset_ref[pl.ds(cable, used, stride=cables), :],
                jnp.ones((padded - used, LANES), jnp.float32),
            ],
            axis=0,
        )
        high, low = split(offset)
        product = jnp.dot(
            jnp.concatenate([high, low, high, low], axis=1),
            weight_ref[cable],
            preferred_element_type=jnp.float32,
        )
        here, there = product[:, :LANES], product[:, LANES:]
        left = pltpu.roll(here[used - 1 : used] + there[:1], HALF, 1)
        following = pltpu.roll(here + pltpu.roll(there, padded - 1, 0), HALF, 1)
        previous = jnp.where(row == 0, left, pltpu.roll(following, 1, 0))
        bias = jnp.where(lane < HALF, previous, following)
        here, there = here[used : used + 1], there[used : used + 1]
        middle = pltpu.roll(here + there, HALF, 1)
        first = pltpu.roll(here * inside_left + there, HALF, 1)
        last = pltpu.roll(here + there * inside_right, HALF, 1)
        first = jnp.where(lane[:1] < HALF, first, middle)
        last = jnp.where(lane[:1] < HALF, middle, last)
        return bias, first, middle, last

    def written(cable, chunk):
        lanes = pl.ds(chunk * span, span)
        return pltpu.make_async_copy(
            stage_ref.at[cable, :, lanes], out_hbm.at[cable, :, lanes], sem.at[cable, chunk]
        )

    carry = filtered_offset(0)
    first_cable = 0
    for local_ref in local_refs:

        def cable_step(index, carry, first_cable=first_cable, local_ref=local_ref):
            cable = first_cable + index
            following = filtered_offset(jnp.minimum(cable + 1, cables - 1))
            bias, first, middle, last = carry
            shifts = [coupling_ref[cable] * column for column in columns]
            inner = [shift * middle for shift in shifts]
            for block in range(blocks):
                lanes = pl.ds(block * LANES, LANES)
                added = jnp.broadcast_to(bias[block : block + 1, :], (SUBLANES, LANES))
                if block == 0:
                    slopes = [shift * first for shift in shifts]
                elif block == blocks - 1:
                    slopes = [shift * last for shift in shifts]
                else:
                    slopes = inner
                for i in range(groups):
                    rows = pl.ds(i * SUBLANES, SUBLANES)
                    stage_ref[cable, rows, lanes] = local_ref[index, block, rows, :] + (
                        added - slopes[i]
                    )
                if (block + 1) % (blocks // CHUNKS) == 0:
                    written(cable, block // (blocks // CHUNKS)).start()
            return following

        carry = lax.fori_loop(0, local_ref.shape[0], cable_step, carry)
        first_cable += local_ref.shape[0]
    for cable in range(cables):
        for chunk in range(CHUNKS):
            written(cable, chunk).wait()


def swapped(value, axis, bit):
    return lax.ppermute(value, axis, [(i, i ^ bit) for i in range(lax.axis_size(axis))])


def shards(phase_step, wrap_count, coupling, filter_taps):
    cables, time, width = phase_step.shape
    blocks = width // LANES
    steps, places = lax.axis_size("tm"), lax.axis_size("chan")
    population = cables * width * places
    bounds = [0, 3 * cables // 8, 5 * cables // 8, cables]
    parts = len(bounds) - 1
    wrap_count = pltpu.with_memory_space_constraint(wrap_count, pltpu.HBM)
    whole = pl.BlockSpec(memory_space=pltpu.VMEM)
    outside = pl.BlockSpec(memory_space=pl.ANY)
    scalars = pl.BlockSpec(memory_space=pltpu.SMEM)

    inner, outer = pl.pallas_call(
        edges_kernel,
        out_shape=[pltpu.VMEM((cables // 2, time, LANES), jnp.float32)] * 2,
        in_specs=[outside] * 2,
        out_specs=[whole] * 2,
        scratch_shapes=[
            pltpu.VMEM((2, cables, time, LANES), jnp.float32),
            pltpu.VMEM((2, cables, time, LANES), jnp.int32),
            pltpu.SemaphoreType.DMA((2, 2)),
        ],
        compiler_params=pltpu.CompilerParams(vmem_limit_bytes=8 << 20),
        name="edges",
    )(pltpu.with_memory_space_constraint(phase_step, pltpu.HBM), wrap_count)
    outer_pairs = [(i, (i + (1 if i % 2 else -1)) % places) for i in range(places)]
    outer = lax.ppermute(outer, "chan", outer_pairs)
    inner = swapped(inner, "chan", 1)

    high, low, totals, sums, weight = pl.pallas_call(
        increments_kernel,
        out_shape=(
            pltpu.VMEM((cables, blocks, time, LANES), jnp.bfloat16),
            pltpu.VMEM((cables, blocks, time, LANES), jnp.bfloat16),
            pltpu.VMEM((blocks * cables, LANES), jnp.float32),
            pltpu.VMEM((SUBLANES, LANES), jnp.float32),
            pltpu.VMEM((cables, 4 * LANES, 2 * LANES), jnp.bfloat16),
        ),
        in_specs=[whole, outside, whole],
        out_specs=[whole] * 5,
        scratch_shapes=[
            pltpu.VMEM((cables, time, width), jnp.int32),
            pltpu.VMEM(filter_taps.shape, jnp.float32),
            pltpu.SemaphoreType.DMA((cables,)),
        ],
        compiler_params=pltpu.CompilerParams(vmem_limit_bytes=16 << 20),
        cost_estimate=pl.CostEstimate(
            flops=0, bytes_accessed=phase_step.size * 4, transcendentals=0
        ),
        name="increments",
    )(pltpu.with_memory_space_constraint(phase_step, pltpu.VMEM), wrap_count, filter_taps)

    halo_high, halo_low, halo_totals = pl.pallas_call(
        halo_kernel,
        out_shape=(
            pltpu.VMEM((cables, 2, time, LANES), jnp.bfloat16),
            pltpu.VMEM((cables, 2, time, LANES), jnp.bfloat16),
            pltpu.VMEM((2 * cables, LANES), jnp.float32),
        ),
        in_specs=[whole] * 2,
        out_specs=[whole] * 3,
        compiler_params=pltpu.CompilerParams(vmem_limit_bytes=8 << 20),
        name="halo",
    )(inner, outer)

    def from_earlier(value, number):
        return pl.pallas_call(
            functools.partial(masked_kernel, 1 << number),
            out_shape=pltpu.VMEM(value.shape, value.dtype),
            in_specs=[whole],
            out_specs=whole,
            compiler_params=pltpu.CompilerParams(vmem_limit_bytes=4 << 20),
            cost_estimate=pl.CostEstimate(
                flops=MASK_FLOPS, bytes_accessed=1 << 20, transcendentals=0
            ),
            name="masked",
        )(value)

    def filtered(part, weight):
        share = bounds[part + 1] - bounds[part]
        return pl.pallas_call(
            functools.partial(filter_kernel, bounds[part]),
            out_shape=pltpu.VMEM((share, blocks, time, LANES), jnp.float32),
            in_specs=[whole] * 5,
            out_specs=whole,
            compiler_params=pltpu.CompilerParams(vmem_limit_bytes=16 << 20),
            cost_estimate=pl.CostEstimate(
                flops=2 * share * (blocks + 2) * time * 8 * LANES * LANES,
                bytes_accessed=1 << 20,
                transcendentals=0,
            ),
            name="filter",
        )(high, low, halo_high, halo_low, weight)

    running = jnp.concatenate([totals, halo_totals], axis=0)
    received = [swapped(running, "tm", 1)]
    sums, halo_totals = lax.optimization_barrier((sums, halo_totals))
    rounds = [("chan", 1 << bit) for bit in range(places.bit_length() - 1)]
    rounds += [("tm", 1 << bit) for bit in range(steps.bit_length() - 1)]
    local, received_sums, chan_sums, ready = [], [], sums, None
    for number, (axis, bit) in enumerate(rounds):
        incoming = swapped(sums, axis, bit)
        if number % 2 == 0 and number > 0 and ready is not None:
            received.append(swapped(ready, "tm", 1 << len(received)))
            ready = None
        elif number > 0 and len(local) < parts:
            tied, sums = lax.optimization_barrier((weight, sums))
            if number == len(rounds) - 1 and 1 << len(received) >= steps:
                received[1] = from_earlier(received[1], 1)
                received[1], tied = lax.optimization_barrier((received[1], tied))
            part = filtered(len(local), tied)
            incoming, part = lax.optimization_barrier((incoming, part))
            local.append(part)
        if number == 2:
            first, sums = lax.optimization_barrier((received[0], sums))
            masked = from_earlier(first, 0)
            incoming, masked = lax.optimization_barrier((incoming, masked))
        if number == 1 and 1 << len(received) < steps:
            earlier, local[-1] = lax.optimization_barrier((received[-1], local[-1]))
            ready = running = running + earlier
        if axis == "tm":
            received_sums.append(incoming)
        sums = sums + incoming
        if axis == "chan":
            chan_sums = sums
    while 1 << len(received) < steps:
        running = running + received[-1] if ready is None else ready
        ready = None
        received.append(swapped(running, "tm", 1 << len(received)))
    while len(local) < parts:
        local.append(filtered(len(local), weight))
    offsets = [masked] + received[1:]

    return pl.pallas_call(
        functools.partial(level_kernel, population),
        out_shape=jax.ShapeDtypeStruct(phase_step.shape, jnp.float32),
        in_specs=[
            [whole] * parts, whole, [whole] * len(offsets), whole, [whole] * len(received_sums), scalars
        ],
        out_specs=outside,
        scratch_shapes=[
            pltpu.VMEM((cables, time, width), jnp.float32),
            pltpu.VMEM(((blocks + 2) * cables, LANES), jnp.float32),
            pltpu.SemaphoreType.DMA((cables, CHUNKS)),
        ],
        compiler_params=pltpu.CompilerParams(vmem_limit_bytes=24 << 20),
        name="level",
    )(local, weight, offsets, chan_sums, received_sums, coupling)


def solution(mesh):
    placed = (P(None, "tm", "chan"), P(None, "tm", "chan"), P(), P())
    return jax.shard_map(
        shards, mesh=mesh, in_specs=placed, out_specs=P(None, "tm", "chan"), check_vma=False
    )
```

```python
import functools
import math

import jax
import jax.numpy as jnp
from jax import lax
from jax.experimental import pallas as pl
from jax.experimental.pallas import tpu as pltpu
from jax.sharding import PartitionSpec as P

two_pi = 2.0 * math.pi
LANES = 128
HALF = LANES // 2
SUBLANES = 8
MASK_FLOPS = 570000000
CHUNKS = 2


def shifted_down(value, amount):
    rows = lax.broadcasted_iota(jnp.int32, value.shape, 0)
    return jnp.where(rows >= amount, pltpu.roll(value, amount, 0), 0.0)


def scanned(pieces):
    sums, carry = [], None
    for value in pieces:
        amount = 1
        while amount < SUBLANES:
            value = value + shifted_down(value, amount)
            amount *= 2
        if carry is not None:
            value = value + carry
        carry = jnp.broadcast_to(value[SUBLANES - 1 :, :], value.shape)
        sums.append(value)
    return sums


def total(pieces):
    value = functools.reduce(jnp.add, pieces)
    return jnp.sum(value, axis=0, keepdims=True)


def split(value):
    high = value.astype(jnp.bfloat16)
    return high, (value - high.astype(jnp.float32)).astype(jnp.bfloat16)


def store_split(high_ref, low_ref, cable, block, sums):
    for pair in range(0, len(sums), 2):
        rows = pl.ds(pair * SUBLANES, 2 * SUBLANES)
        high, low = split(jnp.concatenate(sums[pair : pair + 2], axis=0))
        high_ref[cable, block, rows, :] = high
        low_ref[cable, block, rows, :] = low


def edges_kernel(phase_hbm, wrap_hbm, inner_ref, outer_ref, phase_ref, wrap_ref, sem):
    cables, time, width = phase_hbm.shape
    is_even = lax.rem(lax.axis_index("chan"), 2) == 0
    sends_last = (is_even, jnp.logical_not(is_even))
    copies = []
    for side, last in enumerate(sends_last):
        lanes = pl.ds(pl.multiple_of(jnp.where(last, width - LANES, 0), LANES), LANES)
        for kind, (source, target) in enumerate(((phase_hbm, phase_ref), (wrap_hbm, wrap_ref))):
            copies.append(
                pltpu.make_async_copy(source.at[:, :, lanes], target.at[side], sem.at[kind, side])
            )
    for copy in copies:
        copy.start()
    for copy in copies:
        copy.wait()
    lane = lax.broadcasted_iota(jnp.int32, (time, LANES), 1)
    for side, (last, target) in enumerate(zip(sends_last, (inner_ref, outer_ref))):
        for cable in range(cables // 2):
            low, high = (
                phase_ref[side, c] + two_pi * wrap_ref[side, c].astype(jnp.float32)
                for c in (cable, cable + cables // 2)
            )
            low = jnp.where(last, pltpu.roll(low, HALF, 1), low)
            high = jnp.where(last, high, pltpu.roll(high, HALF, 1))
            target[cable] = jnp.where(lane < HALF, low, high)


def backwards(value):
    lane = lax.broadcasted_iota(jnp.int32, value.shape, 1)
    bit = 1
    while bit < LANES:
        value = jnp.where(
            (lane & bit) == 0, pltpu.roll(value, LANES - bit, 1), pltpu.roll(value, bit, 1)
        )
        bit *= 2
    return value


def increments_kernel(
    phase_ref, wrap_hbm, taps_ref, high_ref, low_ref, totals_ref, sums_ref, weight_ref, wrap_ref,
    reversed_ref, sem,
):
    cables, time, width = phase_ref.shape
    blocks = width // LANES
    groups = time // SUBLANES

    def copy(cable):
        return pltpu.make_async_copy(wrap_hbm.at[cable], wrap_ref.at[cable], sem.at[cable])

    for cable in range(cables):
        copy(cable).start()

    lane = lax.broadcasted_iota(jnp.int32, taps_ref.shape, 1)
    taps = jnp.where(lane == HALF, 1.0, 0.0) - taps_ref[...]
    reversed_ref[...] = pltpu.roll(backwards(taps * (1.0 / (4.0 * two_pi))), 1, 1)
    inputs = lax.broadcasted_iota(jnp.int32, (LANES, LANES), 0)
    outputs = lax.broadcasted_iota(jnp.int32, (LANES, LANES), 1)

    @pl.loop(0, cables)
    def _(cable):
        row = jnp.broadcast_to(reversed_ref[pl.ds(cable, 1), :], (LANES, LANES))
        circulant = pltpu.roll(row, 0, 1, stride=1, stride_axis=0)
        for column, mask in enumerate((inputs >= outputs, inputs < outputs)):
            high, low = split(jnp.where(mask, circulant, 0.0))
            for place, part in enumerate((high, high, low, low)):
                rows, lanes = pl.ds(place * LANES, LANES), pl.ds(column * LANES, LANES)
                weight_ref[cable, rows, lanes] = part

    def cable_step(cable, accumulated):
        copy(cable).wait()

        def block_step(block, accumulated):
            lanes = pl.ds(pl.multiple_of(block * LANES, LANES), LANES)
            pieces = []
            for i in range(groups):
                rows = pl.ds(i * SUBLANES, SUBLANES)
                turns = wrap_ref[cable, rows, lanes].astype(jnp.float32)
                pieces.append(phase_ref[cable, rows, lanes] + two_pi * turns)
            store_split(high_ref, low_ref, cable, block, pieces)
            totals_ref[pl.ds(block * cables + cable, 1), :] = total(pieces)
            return tuple(a + b for a, b in zip(accumulated, pieces))

        return lax.fori_loop(0, blocks, block_step, accumulated, unroll=16)

    zeros = tuple(jnp.zeros((SUBLANES, LANES), jnp.float32) for _ in range(groups))
    accumulated = scanned(lax.fori_loop(0, cables, cable_step, zeros))
    lane = lax.broadcasted_iota(jnp.int32, (SUBLANES, LANES), 1)
    tile = jnp.zeros((SUBLANES, LANES), jnp.float32)
    for i, value in enumerate(accumulated):
        tile = jnp.where(lane == i, jnp.sum(value, axis=1, keepdims=True), tile)
    sums_ref[...] = tile


def halo_kernel(inner_ref, outer_ref, high_ref, low_ref, totals_ref):
    pairs, time, _ = inner_ref.shape
    cables = 2 * pairs
    groups = time // SUBLANES
    place = lax.axis_index("chan")
    is_even = lax.rem(place, 2) == 0
    at_end = (place == 0) | (place == lax.axis_size("chan") - 1)
    for pair in range(pairs):
        inner, outer = (
            [ref[pair, pl.ds(i * SUBLANES, SUBLANES), :] for i in range(groups)]
            for ref in (inner_ref, outer_ref)
        )
        outer = [jnp.where(at_end, 0.0, value) for value in outer]
        right = [jnp.where(is_even, a, b) for a, b in zip(inner, outer)]
        left = [jnp.where(is_even, b, a) for a, b in zip(inner, outer)]
        for block, pieces, moved in ((0, right, pair + pairs), (1, left, pair)):
            for cable in (pair, pair + pairs):
                placed = [pltpu.roll(v, HALF, 1) for v in pieces] if cable == moved else pieces
                store_split(high_ref, low_ref, cable, block, placed)
                totals_ref[pl.ds(block * cables + cable, 1), :] = total(placed)


def filter_kernel(first, high_ref, low_ref, halo_high_ref, halo_low_ref, weight_ref, local_ref):
    _, blocks, time, _ = high_ref.shape
    groups = time // SUBLANES
    lane = lax.broadcasted_iota(jnp.int32, (time, LANES), 1)

    @pl.loop(0, local_ref.shape[0])
    def _(index):
        cable = first + index
        high, low = (
            jnp.concatenate(
                [main[cable].reshape(blocks * time, LANES), halo[cable].reshape(2 * time, LANES)],
                axis=0,
            )
            for main, halo in ((high_ref, halo_high_ref), (low_ref, halo_low_ref))
        )
        product = jnp.dot(
            jnp.concatenate([high, low, high, low], axis=1),
            weight_ref[cable],
            preferred_element_type=jnp.float32,
        )

        def rolled(block):
            here = block if block >= 0 else blocks + 1
            there = block + 1
            return pltpu.roll(
                product[here * time : (here + 1) * time, :LANES]
                + product[there * time : (there + 1) * time, LANES:],
                HALF,
                1,
            )

        previous = rolled(-1)
        for block in range(blocks):
            following = rolled(block)
            value = jnp.where(lane < HALF, previous, following)
            pieces = [value[i * SUBLANES : (i + 1) * SUBLANES] for i in range(groups)]
            for i, piece in enumerate(scanned(pieces)):
                local_ref[index, block, pl.ds(i * SUBLANES, SUBLANES), :] = piece
            previous = following


def masked_kernel(value_ref, masked_ref):
    later = (lax.axis_index("tm") & 1) != 0
    masked_ref[...] = jnp.where(later, value_ref[...], 0.0)


def level_kernel(
    population, local_refs, weight_ref, totals_refs, sums_ref, earlier_refs, coupling_ref,
    out_hbm, stage_ref, offset_ref, sem,
):
    _, blocks, time, _ = local_refs[0].shape
    span = blocks * LANES // CHUNKS
    cables = out_hbm.shape[0]
    groups = time // SUBLANES
    step, place = lax.axis_index("tm"), lax.axis_index("chan")
    inside_left = jnp.where(place == 0, 0.0, 1.0)
    inside_right = jnp.where(place == lax.axis_size("chan") - 1, 0.0, 1.0)

    earlier = jnp.zeros((SUBLANES, LANES), jnp.float32)
    for bit, ref in enumerate(earlier_refs):
        earlier = earlier + jnp.where((step & (1 << bit)) != 0, ref[...], 0.0)
    offset = totals_refs[0][...]
    for bit, ref in enumerate(totals_refs[1:], 1):
        offset = offset + jnp.where((step & (1 << bit)) != 0, ref[...], 0.0)
    offset_ref[...] = offset
    earlier = earlier[SUBLANES - 1 :, groups - 1 : groups]
    common = (sums_ref[...] + earlier) * (1.0 / population)
    columns = [
        jnp.broadcast_to(common[:, i : i + 1], (SUBLANES, LANES)) for i in range(groups)
    ]
    used = blocks + 2
    padded = -(-(used + 1) // SUBLANES) * SUBLANES
    row = lax.broadcasted_iota(jnp.int32, (padded, LANES), 0)
    lane = lax.broadcasted_iota(jnp.int32, (padded, LANES), 1)

    def filtered_offset(cable):
        offset = jnp.concatenate(
            [
                offset_ref[pl.ds(cable, used, stride=cables), :],
                jnp.ones((padded - used, LANES), jnp.float32),
            ],
            axis=0,
        )
        high, low = split(offset)
        product = jnp.dot(
            jnp.concatenate([high, low, high, low], axis=1),
            weight_ref[cable],
            preferred_element_type=jnp.float32,
        )
        here, there = product[:, :LANES], product[:, LANES:]
        left = pltpu.roll(here[used - 1 : used] + there[:1], HALF, 1)
        following = pltpu.roll(here + pltpu.roll(there, padded - 1, 0), HALF, 1)
        previous = jnp.where(row == 0, left, pltpu.roll(following, 1, 0))
        bias = jnp.where(lane < HALF, previous, following)
        here, there = here[used : used + 1], there[used : used + 1]
        middle = pltpu.roll(here + there, HALF, 1)
        first = pltpu.roll(here * inside_left + there, HALF, 1)
        last = pltpu.roll(here + there * inside_right, HALF, 1)
        first = jnp.where(lane[:1] < HALF, first, middle)
        last = jnp.where(lane[:1] < HALF, middle, last)
        return bias, first, middle, last

    def written(cable, chunk):
        lanes = pl.ds(chunk * span, span)
        return pltpu.make_async_copy(
            stage_ref.at[cable, :, lanes], out_hbm.at[cable, :, lanes], sem.at[cable, chunk]
        )

    carry = filtered_offset(0)
    first_cable = 0
    for local_ref in local_refs:

        def cable_step(index, carry, first_cable=first_cable, local_ref=local_ref):
            cable = first_cable + index
            following = filtered_offset(jnp.minimum(cable + 1, cables - 1))
            bias, first, middle, last = carry
            shifts = [coupling_ref[cable] * column for column in columns]
            inner = [shift * middle for shift in shifts]
            for block in range(blocks):
                lanes = pl.ds(block * LANES, LANES)
                added = jnp.broadcast_to(bias[block : block + 1, :], (SUBLANES, LANES))
                if block == 0:
                    slopes = [shift * first for shift in shifts]
                elif block == blocks - 1:
                    slopes = [shift * last for shift in shifts]
                else:
                    slopes = inner
                for i in range(groups):
                    rows = pl.ds(i * SUBLANES, SUBLANES)
                    stage_ref[cable, rows, lanes] = local_ref[index, block, rows, :] + (
                        added - slopes[i]
                    )
                if (block + 1) % (blocks // CHUNKS) == 0:
                    written(cable, block // (blocks // CHUNKS)).start()
            return following

        carry = lax.fori_loop(0, local_ref.shape[0], cable_step, carry)
        first_cable += local_ref.shape[0]
    for cable in range(cables):
        for chunk in range(CHUNKS):
            written(cable, chunk).wait()


def swapped(value, axis, bit):
    return lax.ppermute(value, axis, [(i, i ^ bit) for i in range(lax.axis_size(axis))])


def shards(phase_step, wrap_count, coupling, filter_taps):
    cables, time, width = phase_step.shape
    blocks = width // LANES
    steps, places = lax.axis_size("tm"), lax.axis_size("chan")
    population = cables * width * places
    bounds = [0, 3 * cables // 8, 3 * cables // 4, cables]
    weighed = (3, 1, 1)
    parts = len(bounds) - 1
    wrap_count = pltpu.with_memory_space_constraint(wrap_count, pltpu.HBM)
    whole = pl.BlockSpec(memory_space=pltpu.VMEM)
    outside = pl.BlockSpec(memory_space=pl.ANY)
    scalars = pl.BlockSpec(memory_space=pltpu.SMEM)

    inner, outer = pl.pallas_call(
        edges_kernel,
        out_shape=[pltpu.VMEM((cables // 2, time, LANES), jnp.float32)] * 2,
        in_specs=[outside] * 2,
        out_specs=[whole] * 2,
        scratch_shapes=[
            pltpu.VMEM((2, cables, time, LANES), jnp.float32),
            pltpu.VMEM((2, cables, time, LANES), jnp.int32),
            pltpu.SemaphoreType.DMA((2, 2)),
        ],
        compiler_params=pltpu.CompilerParams(vmem_limit_bytes=8 << 20),
        name="edges",
    )(pltpu.with_memory_space_constraint(phase_step, pltpu.HBM), wrap_count)
    outer_pairs = [(i, (i + (1 if i % 2 else -1)) % places) for i in range(places)]
    outer = lax.ppermute(outer, "chan", outer_pairs)
    inner = swapped(inner, "chan", 1)

    high, low, totals, sums, weight = pl.pallas_call(
        increments_kernel,
        out_shape=(
            pltpu.VMEM((cables, blocks, time, LANES), jnp.bfloat16),
            pltpu.VMEM((cables, blocks, time, LANES), jnp.bfloat16),
            pltpu.VMEM((blocks * cables, LANES), jnp.float32),
            pltpu.VMEM((SUBLANES, LANES), jnp.float32),
            pltpu.VMEM((cables, 4 * LANES, 2 * LANES), jnp.bfloat16),
        ),
        in_specs=[whole, outside, whole],
        out_specs=[whole] * 5,
        scratch_shapes=[
            pltpu.VMEM((cables, time, width), jnp.int32),
            pltpu.VMEM(filter_taps.shape, jnp.float32),
            pltpu.SemaphoreType.DMA((cables,)),
        ],
        compiler_params=pltpu.CompilerParams(vmem_limit_bytes=16 << 20),
        cost_estimate=pl.CostEstimate(
            flops=0, bytes_accessed=phase_step.size * 4, transcendentals=0
        ),
        name="increments",
    )(pltpu.with_memory_space_constraint(phase_step, pltpu.VMEM), wrap_count, filter_taps)

    halo_high, halo_low, halo_totals = pl.pallas_call(
        halo_kernel,
        out_shape=(
            pltpu.VMEM((cables, 2, time, LANES), jnp.bfloat16),
            pltpu.VMEM((cables, 2, time, LANES), jnp.bfloat16),
            pltpu.VMEM((2 * cables, LANES), jnp.float32),
        ),
        in_specs=[whole] * 2,
        out_specs=[whole] * 3,
        compiler_params=pltpu.CompilerParams(vmem_limit_bytes=8 << 20),
        name="halo",
    )(inner, outer)

    def from_earlier(value):
        return pl.pallas_call(
            masked_kernel,
            out_shape=pltpu.VMEM(value.shape, value.dtype),
            in_specs=[whole],
            out_specs=whole,
            compiler_params=pltpu.CompilerParams(vmem_limit_bytes=4 << 20),
            cost_estimate=pl.CostEstimate(
                flops=MASK_FLOPS, bytes_accessed=1 << 20, transcendentals=0
            ),
            name="masked",
        )(value)

    def filtered(part, weight):
        share = bounds[part + 1] - bounds[part]
        return pl.pallas_call(
            functools.partial(filter_kernel, bounds[part]),
            out_shape=pltpu.VMEM((share, blocks, time, LANES), jnp.float32),
            in_specs=[whole] * 5,
            out_specs=whole,
            compiler_params=pltpu.CompilerParams(vmem_limit_bytes=16 << 20),
            cost_estimate=pl.CostEstimate(
                flops=weighed[part] * (cables * (blocks + 2) * time * 2 * LANES * LANES),
                bytes_accessed=1 << 20,
                transcendentals=0,
            ),
            name="filter",
        )(high, low, halo_high, halo_low, weight)

    running = jnp.concatenate([totals, halo_totals], axis=0)
    received = [swapped(running, "tm", 1)]
    sums, halo_totals = lax.optimization_barrier((sums, halo_totals))
    rounds = [("chan", 1 << bit) for bit in range(places.bit_length() - 1)]
    rounds += [("tm", 1 << bit) for bit in range(steps.bit_length() - 1)]
    local, received_sums, chan_sums, ready = [], [], sums, None
    for number, (axis, bit) in enumerate(rounds):
        incoming = swapped(sums, axis, bit)
        if number % 2 == 0 and number > 0 and ready is not None:
            received.append(swapped(ready, "tm", 1 << len(received)))
            ready = None
        elif number > 0 and len(local) < parts:
            tied, sums = lax.optimization_barrier((weight, sums))
            part = filtered(len(local), tied)
            incoming, part = lax.optimization_barrier((incoming, part))
            local.append(part)
        if number == 2:
            first, sums = lax.optimization_barrier((received[0], sums))
            masked = from_earlier(first)
            incoming, masked = lax.optimization_barrier((incoming, masked))
        if number == 1 and 1 << len(received) < steps:
            earlier, local[-1] = lax.optimization_barrier((received[-1], local[-1]))
            ready = running = running + earlier
        if axis == "tm":
            received_sums.append(incoming)
        sums = sums + incoming
        if axis == "chan":
            chan_sums = sums
    while 1 << len(received) < steps:
        running = running + received[-1] if ready is None else ready
        ready = None
        received.append(swapped(running, "tm", 1 << len(received)))
    while len(local) < parts:
        local.append(filtered(len(local), weight))
    offsets = [masked] + received[1:]

    return pl.pallas_call(
        functools.partial(level_kernel, population),
        out_shape=jax.ShapeDtypeStruct(phase_step.shape, jnp.float32),
        in_specs=[
            [whole] * parts, whole, [whole] * len(offsets), whole, [whole] * len(received_sums), scalars
        ],
        out_specs=outside,
        scratch_shapes=[
            pltpu.VMEM((cables, time, width), jnp.float32),
            pltpu.VMEM(((blocks + 2) * cables, LANES), jnp.float32),
            pltpu.SemaphoreType.DMA((cables, CHUNKS)),
        ],
        compiler_params=pltpu.CompilerParams(vmem_limit_bytes=24 << 20),
        name="level",
    )(local, weight, offsets, chan_sums, received_sums, coupling)


def solution(mesh):
    placed = (P(None, "tm", "chan"), P(None, "tm", "chan"), P(), P())
    return jax.shard_map(
        shards, mesh=mesh, in_specs=placed, out_specs=P(None, "tm", "chan"), check_vma=False
    )
```

```python
import functools
import math

import jax
import jax.numpy as jnp
from jax import lax
from jax.experimental import pallas as pl
from jax.experimental.pallas import tpu as pltpu
from jax.sharding import PartitionSpec as P

two_pi = 2.0 * math.pi
LANES = 128
HALF = LANES // 2
SUBLANES = 8
MASK_FLOPS = 570000000
CHUNKS = 2


def shifted_down(value, amount):
    rows = lax.broadcasted_iota(jnp.int32, value.shape, 0)
    return jnp.where(rows >= amount, pltpu.roll(value, amount, 0), 0.0)


def scanned(pieces):
    sums, carry = [], None
    for value in pieces:
        amount = 1
        while amount < SUBLANES:
            value = value + shifted_down(value, amount)
            amount *= 2
        if carry is not None:
            value = value + carry
        carry = jnp.broadcast_to(value[SUBLANES - 1 :, :], value.shape)
        sums.append(value)
    return sums


def total(pieces):
    value = functools.reduce(jnp.add, pieces)
    return jnp.sum(value, axis=0, keepdims=True)


def split(value):
    high = value.astype(jnp.bfloat16)
    return high, (value - high.astype(jnp.float32)).astype(jnp.bfloat16)


def store_split(high_ref, low_ref, cable, block, sums):
    for pair in range(0, len(sums), 2):
        rows = pl.ds(pair * SUBLANES, 2 * SUBLANES)
        high, low = split(jnp.concatenate(sums[pair : pair + 2], axis=0))
        high_ref[cable, block, rows, :] = high
        low_ref[cable, block, rows, :] = low


def edges_kernel(phase_hbm, wrap_hbm, inner_ref, outer_ref, phase_ref, wrap_ref, sem):
    cables, time, width = phase_hbm.shape
    is_even = lax.rem(lax.axis_index("chan"), 2) == 0
    sends_last = (is_even, jnp.logical_not(is_even))
    copies = []
    for side, last in enumerate(sends_last):
        lanes = pl.ds(pl.multiple_of(jnp.where(last, width - LANES, 0), LANES), LANES)
        for kind, (source, target) in enumerate(((phase_hbm, phase_ref), (wrap_hbm, wrap_ref))):
            copies.append(
                pltpu.make_async_copy(source.at[:, :, lanes], target.at[side], sem.at[kind, side])
            )
    for copy in copies:
        copy.start()
    for copy in copies:
        copy.wait()
    lane = lax.broadcasted_iota(jnp.int32, (time, LANES), 1)
    for side, (last, target) in enumerate(zip(sends_last, (inner_ref, outer_ref))):
        for cable in range(cables // 2):
            low, high = (
                phase_ref[side, c] + two_pi * wrap_ref[side, c].astype(jnp.float32)
                for c in (cable, cable + cables // 2)
            )
            low = jnp.where(last, pltpu.roll(low, HALF, 1), low)
            high = jnp.where(last, high, pltpu.roll(high, HALF, 1))
            target[cable] = jnp.where(lane < HALF, low, high)


def backwards(value):
    lane = lax.broadcasted_iota(jnp.int32, value.shape, 1)
    bit = 1
    while bit < LANES:
        value = jnp.where(
            (lane & bit) == 0, pltpu.roll(value, LANES - bit, 1), pltpu.roll(value, bit, 1)
        )
        bit *= 2
    return value


def increments_kernel(
    phase_ref, wrap_hbm, taps_ref, high_ref, low_ref, totals_ref, sums_ref, weight_ref, wrap_ref,
    reversed_ref, sem,
):
    cables, time, width = phase_ref.shape
    blocks = width // LANES
    groups = time // SUBLANES

    def copy(cable):
        return pltpu.make_async_copy(wrap_hbm.at[cable], wrap_ref.at[cable], sem.at[cable])

    for cable in range(cables):
        copy(cable).start()

    lane = lax.broadcasted_iota(jnp.int32, taps_ref.shape, 1)
    taps = jnp.where(lane == HALF, 1.0, 0.0) - taps_ref[...]
    reversed_ref[...] = pltpu.roll(backwards(taps * (1.0 / (4.0 * two_pi))), 1, 1)
    inputs = lax.broadcasted_iota(jnp.int32, (LANES, LANES), 0)
    outputs = lax.broadcasted_iota(jnp.int32, (LANES, LANES), 1)

    @pl.loop(0, cables)
    def _(cable):
        row = jnp.broadcast_to(reversed_ref[pl.ds(cable, 1), :], (LANES, LANES))
        circulant = pltpu.roll(row, 0, 1, stride=1, stride_axis=0)
        for column, mask in enumerate((inputs >= outputs, inputs < outputs)):
            high, low = split(jnp.where(mask, circulant, 0.0))
            for place, part in enumerate((high, high, low, low)):
                rows, lanes = pl.ds(place * LANES, LANES), pl.ds(column * LANES, LANES)
                weight_ref[cable, rows, lanes] = part

    def cable_step(cable, accumulated):
        copy(cable).wait()

        def block_step(block, accumulated):
            lanes = pl.ds(pl.multiple_of(block * LANES, LANES), LANES)
            pieces = []
            for i in range(groups):
                rows = pl.ds(i * SUBLANES, SUBLANES)
                turns = wrap_ref[cable, rows, lanes].astype(jnp.float32)
                pieces.append(phase_ref[cable, rows, lanes] + two_pi * turns)
            store_split(high_ref, low_ref, cable, block, pieces)
            totals_ref[pl.ds(block * cables + cable, 1), :] = total(pieces)
            return tuple(a + b for a, b in zip(accumulated, pieces))

        return lax.fori_loop(0, blocks, block_step, accumulated, unroll=16)

    zeros = tuple(jnp.zeros((SUBLANES, LANES), jnp.float32) for _ in range(groups))
    accumulated = scanned(lax.fori_loop(0, cables, cable_step, zeros))
    lane = lax.broadcasted_iota(jnp.int32, (SUBLANES, LANES), 1)
    tile = jnp.zeros((SUBLANES, LANES), jnp.float32)
    for i, value in enumerate(accumulated):
        tile = jnp.where(lane == i, jnp.sum(value, axis=1, keepdims=True), tile)
    sums_ref[...] = tile


def halo_kernel(outer_ref, inner_ref, high_ref, low_ref, totals_ref):
    pairs, time, _ = inner_ref.shape
    cables = 2 * pairs
    groups = time // SUBLANES
    place = lax.axis_index("chan")
    is_even = lax.rem(place, 2) == 0
    at_end = (place == 0) | (place == lax.axis_size("chan") - 1)
    for pair in range(pairs):
        inner, outer = (
            [ref[pair, pl.ds(i * SUBLANES, SUBLANES), :] for i in range(groups)]
            for ref in (inner_ref, outer_ref)
        )
        outer = [jnp.where(at_end, 0.0, value) for value in outer]
        right = [jnp.where(is_even, a, b) for a, b in zip(inner, outer)]
        left = [jnp.where(is_even, b, a) for a, b in zip(inner, outer)]
        for block, pieces, moved in ((0, right, pair + pairs), (1, left, pair)):
            for cable in (pair, pair + pairs):
                placed = [pltpu.roll(v, HALF, 1) for v in pieces] if cable == moved else pieces
                store_split(high_ref, low_ref, cable, block, placed)
                totals_ref[pl.ds(block * cables + cable, 1), :] = total(placed)


def filter_kernel(first, high_ref, low_ref, halo_high_ref, halo_low_ref, weight_ref, local_ref):
    _, blocks, time, _ = high_ref.shape
    groups = time // SUBLANES
    lane = lax.broadcasted_iota(jnp.int32, (time, LANES), 1)

    @pl.loop(0, local_ref.shape[0])
    def _(index):
        cable = first + index
        high, low = (
            jnp.concatenate(
                [main[cable].reshape(blocks * time, LANES), halo[cable].reshape(2 * time, LANES)],
                axis=0,
            )
            for main, halo in ((high_ref, halo_high_ref), (low_ref, halo_low_ref))
        )
        product = jnp.dot(
            jnp.concatenate([high, low, high, low], axis=1),
            weight_ref[cable],
            preferred_element_type=jnp.float32,
        )

        def rolled(block):
            here = block if block >= 0 else blocks + 1
            there = block + 1
            return pltpu.roll(
                product[here * time : (here + 1) * time, :LANES]
                + product[there * time : (there + 1) * time, LANES:],
                HALF,
                1,
            )

        previous = rolled(-1)
        for block in range(blocks):
            following = rolled(block)
            value = jnp.where(lane < HALF, previous, following)
            pieces = [value[i * SUBLANES : (i + 1) * SUBLANES] for i in range(groups)]
            for i, piece in enumerate(scanned(pieces)):
                local_ref[index, block, pl.ds(i * SUBLANES, SUBLANES), :] = piece
            previous = following


def masked_kernel(value_ref, masked_ref):
    later = (lax.axis_index("tm") & 1) != 0
    masked_ref[...] = jnp.where(later, value_ref[...], 0.0)


def level_kernel(
    population, local_refs, weight_ref, totals_refs, sums_ref, earlier_refs, coupling_ref,
    out_hbm, stage_ref, offset_ref, sem,
):
    _, blocks, time, _ = local_refs[0].shape
    span = blocks * LANES // CHUNKS
    cables = out_hbm.shape[0]
    groups = time // SUBLANES
    step, place = lax.axis_index("tm"), lax.axis_index("chan")
    inside_left = jnp.where(place == 0, 0.0, 1.0)
    inside_right = jnp.where(place == lax.axis_size("chan") - 1, 0.0, 1.0)

    earlier = jnp.zeros((SUBLANES, LANES), jnp.float32)
    for bit, ref in enumerate(earlier_refs):
        earlier = earlier + jnp.where((step & (1 << bit)) != 0, ref[...], 0.0)
    offset = totals_refs[0][...]
    for bit, ref in enumerate(totals_refs[1:], 1):
        offset = offset + jnp.where((step & (1 << bit)) != 0, ref[...], 0.0)
    offset_ref[...] = offset
    earlier = earlier[SUBLANES - 1 :, groups - 1 : groups]
    common = (sums_ref[...] + earlier) * (1.0 / population)
    columns = [
        jnp.broadcast_to(common[:, i : i + 1], (SUBLANES, LANES)) for i in range(groups)
    ]
    used = blocks + 2
    padded = -(-(used + 1) // SUBLANES) * SUBLANES
    row = lax.broadcasted_iota(jnp.int32, (padded, LANES), 0)
    lane = lax.broadcasted_iota(jnp.int32, (padded, LANES), 1)

    def filtered_offset(cable):
        offset = jnp.concatenate(
            [
                offset_ref[pl.ds(cable, used, stride=cables), :],
                jnp.ones((padded - used, LANES), jnp.float32),
            ],
            axis=0,
        )
        high, low = split(offset)
        product = jnp.dot(
            jnp.concatenate([high, low, high, low], axis=1),
            weight_ref[cable],
            preferred_element_type=jnp.float32,
        )
        here, there = product[:, :LANES], product[:, LANES:]
        left = pltpu.roll(here[used - 1 : used] + there[:1], HALF, 1)
        following = pltpu.roll(here + pltpu.roll(there, padded - 1, 0), HALF, 1)
        previous = jnp.where(row == 0, left, pltpu.roll(following, 1, 0))
        bias = jnp.where(lane < HALF, previous, following)
        here, there = here[used : used + 1], there[used : used + 1]
        middle = pltpu.roll(here + there, HALF, 1)
        first = pltpu.roll(here * inside_left + there, HALF, 1)
        last = pltpu.roll(here + there * inside_right, HALF, 1)
        first = jnp.where(lane[:1] < HALF, first, middle)
        last = jnp.where(lane[:1] < HALF, middle, last)
        return bias, first, middle, last

    def written(cable, chunk):
        lanes = pl.ds(chunk * span, span)
        return pltpu.make_async_copy(
            stage_ref.at[cable, :, lanes], out_hbm.at[cable, :, lanes], sem.at[cable, chunk]
        )

    carry = filtered_offset(0)
    first_cable = 0
    for local_ref in local_refs:

        def cable_step(index, carry, first_cable=first_cable, local_ref=local_ref):
            cable = first_cable + index
            following = filtered_offset(jnp.minimum(cable + 1, cables - 1))
            bias, first, middle, last = carry
            shifts = [coupling_ref[cable] * column for column in columns]
            inner = [shift * middle for shift in shifts]
            for block in range(blocks):
                lanes = pl.ds(block * LANES, LANES)
                added = jnp.broadcast_to(bias[block : block + 1, :], (SUBLANES, LANES))
                if block == 0:
                    slopes = [shift * first for shift in shifts]
                elif block == blocks - 1:
                    slopes = [shift * last for shift in shifts]
                else:
                    slopes = inner
                for i in range(groups):
                    rows = pl.ds(i * SUBLANES, SUBLANES)
                    stage_ref[cable, rows, lanes] = local_ref[index, block, rows, :] + (
                        added - slopes[i]
                    )
                if (block + 1) % (blocks // CHUNKS) == 0:
                    written(cable, block // (blocks // CHUNKS)).start()
            return following

        carry = lax.fori_loop(0, local_ref.shape[0], cable_step, carry)
        first_cable += local_ref.shape[0]
    for cable in range(cables):
        for chunk in range(CHUNKS):
            written(cable, chunk).wait()


def swapped(value, axis, bit):
    return lax.ppermute(value, axis, [(i, i ^ bit) for i in range(lax.axis_size(axis))])


def shards(phase_step, wrap_count, coupling, filter_taps):
    cables, time, width = phase_step.shape
    blocks = width // LANES
    steps, places = lax.axis_size("tm"), lax.axis_size("chan")
    population = cables * width * places
    bounds = [0, 3 * cables // 8, 3 * cables // 4, cables]
    weighed = (3, 1, 1)
    parts = len(bounds) - 1
    wrap_count = pltpu.with_memory_space_constraint(wrap_count, pltpu.HBM)
    whole = pl.BlockSpec(memory_space=pltpu.VMEM)
    outside = pl.BlockSpec(memory_space=pl.ANY)
    scalars = pl.BlockSpec(memory_space=pltpu.SMEM)

    inner, outer = pl.pallas_call(
        edges_kernel,
        out_shape=[pltpu.VMEM((cables // 2, time, LANES), jnp.float32)] * 2,
        in_specs=[outside] * 2,
        out_specs=[whole] * 2,
        scratch_shapes=[
            pltpu.VMEM((2, cables, time, LANES), jnp.float32),
            pltpu.VMEM((2, cables, time, LANES), jnp.int32),
            pltpu.SemaphoreType.DMA((2, 2)),
        ],
        compiler_params=pltpu.CompilerParams(vmem_limit_bytes=8 << 20),
        name="edges",
    )(pltpu.with_memory_space_constraint(phase_step, pltpu.HBM), wrap_count)
    outer_pairs = [(i, (i + (1 if i % 2 else -1)) % places) for i in range(places)]
    outer = lax.ppermute(outer, "chan", outer_pairs)
    inner = swapped(inner, "chan", 1)

    high, low, totals, sums, weight = pl.pallas_call(
        increments_kernel,
        out_shape=(
            pltpu.VMEM((cables, blocks, time, LANES), jnp.bfloat16),
            pltpu.VMEM((cables, blocks, time, LANES), jnp.bfloat16),
            pltpu.VMEM((blocks * cables, LANES), jnp.float32),
            pltpu.VMEM((SUBLANES, LANES), jnp.float32),
            pltpu.VMEM((cables, 4 * LANES, 2 * LANES), jnp.bfloat16),
        ),
        in_specs=[whole, outside, whole],
        out_specs=[whole] * 5,
        scratch_shapes=[
            pltpu.VMEM((cables, time, width), jnp.int32),
            pltpu.VMEM(filter_taps.shape, jnp.float32),
            pltpu.SemaphoreType.DMA((cables,)),
        ],
        compiler_params=pltpu.CompilerParams(vmem_limit_bytes=16 << 20),
        cost_estimate=pl.CostEstimate(
            flops=0, bytes_accessed=phase_step.size * 4, transcendentals=0
        ),
        name="increments",
    )(pltpu.with_memory_space_constraint(phase_step, pltpu.VMEM), wrap_count, filter_taps)

    halo_high, halo_low, halo_totals = pl.pallas_call(
        halo_kernel,
        out_shape=(
            pltpu.VMEM((cables, 2, time, LANES), jnp.bfloat16),
            pltpu.VMEM((cables, 2, time, LANES), jnp.bfloat16),
            pltpu.VMEM((2 * cables, LANES), jnp.float32),
        ),
        in_specs=[whole] * 2,
        out_specs=[whole] * 3,
        compiler_params=pltpu.CompilerParams(vmem_limit_bytes=8 << 20),
        name="halo",
    )(outer, inner)

    def from_earlier(value):
        return pl.pallas_call(
            masked_kernel,
            out_shape=pltpu.VMEM(value.shape, value.dtype),
            in_specs=[whole],
            out_specs=whole,
            compiler_params=pltpu.CompilerParams(vmem_limit_bytes=4 << 20),
            cost_estimate=pl.CostEstimate(
                flops=MASK_FLOPS, bytes_accessed=1 << 20, transcendentals=0
            ),
            name="masked",
        )(value)

    def filtered(part, weight):
        share = bounds[part + 1] - bounds[part]
        return pl.pallas_call(
            functools.partial(filter_kernel, bounds[part]),
            out_shape=pltpu.VMEM((share, blocks, time, LANES), jnp.float32),
            in_specs=[whole] * 5,
            out_specs=whole,
            compiler_params=pltpu.CompilerParams(vmem_limit_bytes=16 << 20),
            cost_estimate=pl.CostEstimate(
                flops=weighed[part] * (cables * (blocks + 2) * time * 2 * LANES * LANES),
                bytes_accessed=1 << 20,
                transcendentals=0,
            ),
            name="filter",
        )(high, low, halo_high, halo_low, weight)

    running = jnp.concatenate([totals, halo_totals], axis=0)
    received = [swapped(running, "tm", 1)]
    sums, halo_totals = lax.optimization_barrier((sums, halo_totals))
    rounds = [("chan", 1 << bit) for bit in range(places.bit_length() - 1)]
    rounds += [("tm", 1 << bit) for bit in range(steps.bit_length() - 1)]
    local, received_sums, chan_sums, ready = [], [], sums, None
    for number, (axis, bit) in enumerate(rounds):
        incoming = swapped(sums, axis, bit)
        if number % 2 == 0 and number > 0 and ready is not None:
            received.append(swapped(ready, "tm", 1 << len(received)))
            ready = None
        elif number > 0 and len(local) < parts:
            tied, sums = lax.optimization_barrier((weight, sums))
            part = filtered(len(local), tied)
            incoming, part = lax.optimization_barrier((incoming, part))
            local.append(part)
        if number == 2:
            first, sums = lax.optimization_barrier((received[0], sums))
            masked = from_earlier(first)
            incoming, masked = lax.optimization_barrier((incoming, masked))
        if number == 1 and 1 << len(received) < steps:
            earlier, local[-1] = lax.optimization_barrier((received[-1], local[-1]))
            ready = running = running + earlier
        if axis == "tm":
            received_sums.append(incoming)
        sums = sums + incoming
        if axis == "chan":
            chan_sums = sums
    while 1 << len(received) < steps:
        running = running + received[-1] if ready is None else ready
        ready = None
        received.append(swapped(running, "tm", 1 << len(received)))
    while len(local) < parts:
        local.append(filtered(len(local), weight))
    offsets = [masked] + received[1:]

    return pl.pallas_call(
        functools.partial(level_kernel, population),
        out_shape=jax.ShapeDtypeStruct(phase_step.shape, jnp.float32),
        in_specs=[
            [whole] * parts, whole, [whole] * len(offsets), whole, [whole] * len(received_sums), scalars
        ],
        out_specs=outside,
        scratch_shapes=[
            pltpu.VMEM((cables, time, width), jnp.float32),
            pltpu.VMEM(((blocks + 2) * cables, LANES), jnp.float32),
            pltpu.SemaphoreType.DMA((cables, CHUNKS)),
        ],
        compiler_params=pltpu.CompilerParams(vmem_limit_bytes=24 << 20),
        name="level",
    )(local, weight, offsets, chan_sums, received_sums, coupling)


def solution(mesh):
    placed = (P(None, "tm", "chan"), P(None, "tm", "chan"), P(), P())
    return jax.shard_map(
        shards, mesh=mesh, in_specs=placed, out_specs=P(None, "tm", "chan"), check_vma=False
    )
```

```python
import functools
import math

import jax
import jax.numpy as jnp
from jax import lax
from jax.experimental import pallas as pl
from jax.experimental.pallas import tpu as pltpu
from jax.sharding import PartitionSpec as P

two_pi = 2.0 * math.pi
LANES = 128
HALF = LANES // 2
SUBLANES = 8
MASK_FLOPS = 570000000
CHUNKS = 2


def shifted_down(value, amount):
    rows = lax.broadcasted_iota(jnp.int32, value.shape, 0)
    return jnp.where(rows >= amount, pltpu.roll(value, amount, 0), 0.0)


def scanned(pieces):
    sums, carry = [], None
    for value in pieces:
        amount = 1
        while amount < SUBLANES:
            value = value + shifted_down(value, amount)
            amount *= 2
        if carry is not None:
            value = value + carry
        carry = jnp.broadcast_to(value[SUBLANES - 1 :, :], value.shape)
        sums.append(value)
    return sums


def total(pieces):
    value = functools.reduce(jnp.add, pieces)
    return jnp.sum(value, axis=0, keepdims=True)


def split(value):
    high = value.astype(jnp.bfloat16)
    return high, (value - high.astype(jnp.float32)).astype(jnp.bfloat16)


def store_split(high_ref, low_ref, cable, block, sums):
    for pair in range(0, len(sums), 2):
        rows = pl.ds(pair * SUBLANES, 2 * SUBLANES)
        high, low = split(jnp.concatenate(sums[pair : pair + 2], axis=0))
        high_ref[cable, block, rows, :] = high
        low_ref[cable, block, rows, :] = low


def edges_kernel(phase_hbm, wrap_hbm, inner_ref, outer_ref, phase_ref, wrap_ref, sem):
    cables, time, width = phase_hbm.shape
    is_even = lax.rem(lax.axis_index("chan"), 2) == 0
    sends_last = (is_even, jnp.logical_not(is_even))
    copies = []
    for side, last in enumerate(sends_last):
        lanes = pl.ds(pl.multiple_of(jnp.where(last, width - LANES, 0), LANES), LANES)
        for kind, (source, target) in enumerate(((phase_hbm, phase_ref), (wrap_hbm, wrap_ref))):
            copies.append(
                pltpu.make_async_copy(source.at[:, :, lanes], target.at[side], sem.at[kind, side])
            )
    for copy in copies:
        copy.start()
    for copy in copies:
        copy.wait()
    lane = lax.broadcasted_iota(jnp.int32, (time, LANES), 1)
    for side, (last, target) in enumerate(zip(sends_last, (inner_ref, outer_ref))):
        for cable in range(cables // 2):
            low, high = (
                phase_ref[side, c] + two_pi * wrap_ref[side, c].astype(jnp.float32)
                for c in (cable, cable + cables // 2)
            )
            low = jnp.where(last, pltpu.roll(low, HALF, 1), low)
            high = jnp.where(last, high, pltpu.roll(high, HALF, 1))
            target[cable] = jnp.where(lane < HALF, low, high)


def backwards(value):
    lane = lax.broadcasted_iota(jnp.int32, value.shape, 1)
    bit = 1
    while bit < LANES:
        value = jnp.where(
            (lane & bit) == 0, pltpu.roll(value, LANES - bit, 1), pltpu.roll(value, bit, 1)
        )
        bit *= 2
    return value


def increments_kernel(
    phase_ref, wrap_hbm, taps_ref, high_ref, low_ref, totals_ref, sums_ref, weight_ref, wrap_ref,
    reversed_ref, sem,
):
    cables, time, width = phase_ref.shape
    blocks = width // LANES
    groups = time // SUBLANES

    def copy(cable):
        return pltpu.make_async_copy(wrap_hbm.at[cable], wrap_ref.at[cable], sem.at[cable])

    for cable in range(cables):
        copy(cable).start()

    lane = lax.broadcasted_iota(jnp.int32, taps_ref.shape, 1)
    taps = jnp.where(lane == HALF, 1.0, 0.0) - taps_ref[...]
    reversed_ref[...] = pltpu.roll(backwards(taps * (1.0 / (4.0 * two_pi))), 1, 1)
    inputs = lax.broadcasted_iota(jnp.int32, (LANES, LANES), 0)
    outputs = lax.broadcasted_iota(jnp.int32, (LANES, LANES), 1)

    @pl.loop(0, cables)
    def _(cable):
        row = jnp.broadcast_to(reversed_ref[pl.ds(cable, 1), :], (LANES, LANES))
        circulant = pltpu.roll(row, 0, 1, stride=1, stride_axis=0)
        for column, mask in enumerate((inputs >= outputs, inputs < outputs)):
            high, low = split(jnp.where(mask, circulant, 0.0))
            for place, part in enumerate((high, high, low, low)):
                rows, lanes = pl.ds(place * LANES, LANES), pl.ds(column * LANES, LANES)
                weight_ref[cable, rows, lanes] = part

    def cable_step(cable, accumulated):
        copy(cable).wait()

        def block_step(block, accumulated):
            lanes = pl.ds(pl.multiple_of(block * LANES, LANES), LANES)
            pieces = []
            for i in range(groups):
                rows = pl.ds(i * SUBLANES, SUBLANES)
                turns = wrap_ref[cable, rows, lanes].astype(jnp.float32)
                pieces.append(phase_ref[cable, rows, lanes] + two_pi * turns)
            store_split(high_ref, low_ref, cable, block, pieces)
            totals_ref[pl.ds(block * cables + cable, 1), :] = total(pieces)
            return tuple(a + b for a, b in zip(accumulated, pieces))

        return lax.fori_loop(0, blocks, block_step, accumulated, unroll=16)

    zeros = tuple(jnp.zeros((SUBLANES, LANES), jnp.float32) for _ in range(groups))
    accumulated = scanned(lax.fori_loop(0, cables, cable_step, zeros))
    lane = lax.broadcasted_iota(jnp.int32, (SUBLANES, LANES), 1)
    tile = jnp.zeros((SUBLANES, LANES), jnp.float32)
    for i, value in enumerate(accumulated):
        tile = jnp.where(lane == i, jnp.sum(value, axis=1, keepdims=True), tile)
    sums_ref[...] = tile


def halo_kernel(outer_ref, inner_ref, high_ref, low_ref, totals_ref):
    pairs, time, _ = inner_ref.shape
    cables = 2 * pairs
    groups = time // SUBLANES
    place = lax.axis_index("chan")
    is_even = lax.rem(place, 2) == 0
    at_end = (place == 0) | (place == lax.axis_size("chan") - 1)
    for pair in range(pairs):
        inner, outer = (
            [ref[pair, pl.ds(i * SUBLANES, SUBLANES), :] for i in range(groups)]
            for ref in (inner_ref, outer_ref)
        )
        outer = [jnp.where(at_end, 0.0, value) for value in outer]
        right = [jnp.where(is_even, a, b) for a, b in zip(inner, outer)]
        left = [jnp.where(is_even, b, a) for a, b in zip(inner, outer)]
        for block, pieces, moved in ((0, right, pair + pairs), (1, left, pair)):
            for cable in (pair, pair + pairs):
                placed = [pltpu.roll(v, HALF, 1) for v in pieces] if cable == moved else pieces
                store_split(high_ref, low_ref, cable, block, placed)
                totals_ref[pl.ds(block * cables + cable, 1), :] = total(placed)


def filter_kernel(first, high_ref, low_ref, halo_high_ref, halo_low_ref, weight_ref, local_ref):
    _, blocks, time, _ = high_ref.shape
    groups = time // SUBLANES
    lane = lax.broadcasted_iota(jnp.int32, (time, LANES), 1)

    @pl.loop(0, local_ref.shape[0])
    def _(index):
        cable = first + index
        high, low = (
            jnp.concatenate(
                [main[cable].reshape(blocks * time, LANES), halo[cable].reshape(2 * time, LANES)],
                axis=0,
            )
            for main, halo in ((high_ref, halo_high_ref), (low_ref, halo_low_ref))
        )
        product = jnp.dot(
            jnp.concatenate([high, low, high, low], axis=1),
            weight_ref[cable],
            preferred_element_type=jnp.float32,
        )

        def rolled(block):
            here = block if block >= 0 else blocks + 1
            there = block + 1
            return pltpu.roll(
                product[here * time : (here + 1) * time, :LANES]
                + product[there * time : (there + 1) * time, LANES:],
                HALF,
                1,
            )

        previous = rolled(-1)
        for block in range(blocks):
            following = rolled(block)
            value = jnp.where(lane < HALF, previous, following)
            pieces = [value[i * SUBLANES : (i + 1) * SUBLANES] for i in range(groups)]
            for i, piece in enumerate(scanned(pieces)):
                local_ref[index, block, pl.ds(i * SUBLANES, SUBLANES), :] = piece
            previous = following


def masked_kernel(value_ref, masked_ref):
    later = (lax.axis_index("tm") & 1) != 0
    masked_ref[...] = jnp.where(later, value_ref[...], 0.0)


def level_kernel(
    population, local_refs, weight_ref, totals_refs, sums_ref, earlier_refs, coupling_ref,
    out_hbm, stage_ref, offset_ref, sem,
):
    _, blocks, time, _ = local_refs[0].shape
    span = blocks * LANES // CHUNKS
    cables = out_hbm.shape[0]
    groups = time // SUBLANES
    step, place = lax.axis_index("tm"), lax.axis_index("chan")
    inside_left = jnp.where(place == 0, 0.0, 1.0)
    inside_right = jnp.where(place == lax.axis_size("chan") - 1, 0.0, 1.0)

    earlier = jnp.zeros((SUBLANES, LANES), jnp.float32)
    for bit, ref in enumerate(earlier_refs):
        earlier = earlier + jnp.where((step & (1 << bit)) != 0, ref[...], 0.0)
    offset = totals_refs[0][...]
    for bit, ref in enumerate(totals_refs[1:], 1):
        offset = offset + jnp.where((step & (1 << bit)) != 0, ref[...], 0.0)
    offset_ref[pl.ds(0, offset.shape[0]), :] = offset
    earlier = earlier[SUBLANES - 1 :, groups - 1 : groups]
    common = (sums_ref[...] + earlier) * (1.0 / population)
    columns = [
        jnp.broadcast_to(common[:, i : i + 1], (SUBLANES, LANES)) for i in range(groups)
    ]
    used = blocks + 2
    padded = -(-(used + 1) // SUBLANES) * SUBLANES
    row = lax.broadcasted_iota(jnp.int32, (padded, LANES), 0)
    lane = lax.broadcasted_iota(jnp.int32, (padded, LANES), 1)

    def filtered_offset(cable):
        offset = jnp.concatenate(
            [
                offset_ref[pl.ds(cable, used, stride=cables), :],
                jnp.ones((padded - used, LANES), jnp.float32),
            ],
            axis=0,
        )
        high, low = split(offset)
        product = jnp.dot(
            jnp.concatenate([high, low, high, low], axis=1),
            weight_ref[cable],
            preferred_element_type=jnp.float32,
        )
        here, there = product[:, :LANES], product[:, LANES:]
        left = pltpu.roll(here[used - 1 : used] + there[:1], HALF, 1)
        following = pltpu.roll(here + pltpu.roll(there, padded - 1, 0), HALF, 1)
        previous = jnp.where(row == 0, left, pltpu.roll(following, 1, 0))
        bias = jnp.where(lane < HALF, previous, following)
        here, there = here[used : used + 1], there[used : used + 1]
        middle = pltpu.roll(here + there, HALF, 1)
        first = pltpu.roll(here * inside_left + there, HALF, 1)
        last = pltpu.roll(here + there * inside_right, HALF, 1)
        first = jnp.where(lane[:1] < HALF, first, middle)
        last = jnp.where(lane[:1] < HALF, middle, last)
        return bias, first, middle, last

    def written(cable, chunk):
        lanes = pl.ds(chunk * span, span)
        return pltpu.make_async_copy(
            stage_ref.at[cable, :, lanes], out_hbm.at[cable, :, lanes], sem.at[cable, chunk]
        )

    carry = filtered_offset(0)
    first_cable = 0
    for local_ref in local_refs:

        def cable_step(index, carry, first_cable=first_cable, local_ref=local_ref):
            cable = first_cable + index
            following = filtered_offset(jnp.minimum(cable + 1, cables - 1))
            bias, first, middle, last = carry
            shifts = [coupling_ref[cable] * column for column in columns]
            inner = [shift * middle for shift in shifts]
            for block in range(blocks):
                lanes = pl.ds(block * LANES, LANES)
                added = jnp.broadcast_to(bias[block : block + 1, :], (SUBLANES, LANES))
                if block == 0:
                    slopes = [shift * first for shift in shifts]
                elif block == blocks - 1:
                    slopes = [shift * last for shift in shifts]
                else:
                    slopes = inner
                for i in range(groups):
                    rows = pl.ds(i * SUBLANES, SUBLANES)
                    stage_ref[cable, rows, lanes] = local_ref[index, block, rows, :] + (
                        added - slopes[i]
                    )
                if (block + 1) % (blocks // CHUNKS) == 0:
                    written(cable, block // (blocks // CHUNKS)).start()
            return following

        carry = lax.fori_loop(0, local_ref.shape[0], cable_step, carry)
        first_cable += local_ref.shape[0]
    for cable in range(cables):
        for chunk in range(CHUNKS):
            written(cable, chunk).wait()


def swapped(value, axis, bit):
    return lax.ppermute(value, axis, [(i, i ^ bit) for i in range(lax.axis_size(axis))])


def shards(phase_step, wrap_count, coupling, filter_taps):
    cables, time, width = phase_step.shape
    blocks = width // LANES
    steps, places = lax.axis_size("tm"), lax.axis_size("chan")
    population = cables * width * places
    bounds = [0, 3 * cables // 8, 3 * cables // 4, cables]
    weighed = (3, 1, 1)
    parts = len(bounds) - 1
    wrap_count = pltpu.with_memory_space_constraint(wrap_count, pltpu.HBM)
    whole = pl.BlockSpec(memory_space=pltpu.VMEM)
    outside = pl.BlockSpec(memory_space=pl.ANY)
    scalars = pl.BlockSpec(memory_space=pltpu.SMEM)

    inner, outer = pl.pallas_call(
        edges_kernel,
        out_shape=[pltpu.VMEM((cables // 2, time, LANES), jnp.float32)] * 2,
        in_specs=[outside] * 2,
        out_specs=[whole] * 2,
        scratch_shapes=[
            pltpu.VMEM((2, cables, time, LANES), jnp.float32),
            pltpu.VMEM((2, cables, time, LANES), jnp.int32),
            pltpu.SemaphoreType.DMA((2, 2)),
        ],
        compiler_params=pltpu.CompilerParams(vmem_limit_bytes=8 << 20),
        name="edges",
    )(pltpu.with_memory_space_constraint(phase_step, pltpu.HBM), wrap_count)
    outer_pairs = [(i, (i + (1 if i % 2 else -1)) % places) for i in range(places)]
    outer = lax.ppermute(outer, "chan", outer_pairs)
    inner = swapped(inner, "chan", 1)

    high, low, totals, sums, weight = pl.pallas_call(
        increments_kernel,
        out_shape=(
            pltpu.VMEM((cables, blocks, time, LANES), jnp.bfloat16),
            pltpu.VMEM((cables, blocks, time, LANES), jnp.bfloat16),
            pltpu.VMEM((blocks * cables, LANES), jnp.float32),
            pltpu.VMEM((SUBLANES, LANES), jnp.float32),
            pltpu.VMEM((cables, 4 * LANES, 2 * LANES), jnp.bfloat16),
        ),
        in_specs=[whole, outside, whole],
        out_specs=[whole] * 5,
        scratch_shapes=[
            pltpu.VMEM((cables, time, width), jnp.int32),
            pltpu.VMEM(filter_taps.shape, jnp.float32),
            pltpu.SemaphoreType.DMA((cables,)),
        ],
        compiler_params=pltpu.CompilerParams(vmem_limit_bytes=16 << 20),
        cost_estimate=pl.CostEstimate(
            flops=0, bytes_accessed=phase_step.size * 4, transcendentals=0
        ),
        name="increments",
    )(pltpu.with_memory_space_constraint(phase_step, pltpu.VMEM), wrap_count, filter_taps)

    halo_high, halo_low, halo_totals = pl.pallas_call(
        halo_kernel,
        out_shape=(
            pltpu.VMEM((cables, 2, time, LANES), jnp.bfloat16),
            pltpu.VMEM((cables, 2, time, LANES), jnp.bfloat16),
            pltpu.VMEM((2 * cables, LANES), jnp.float32),
        ),
        in_specs=[whole] * 2,
        out_specs=[whole] * 3,
        compiler_params=pltpu.CompilerParams(vmem_limit_bytes=8 << 20),
        name="halo",
    )(outer, inner)

    def from_earlier(value):
        return pl.pallas_call(
            masked_kernel,
            out_shape=pltpu.VMEM(value.shape, value.dtype),
            in_specs=[whole],
            out_specs=whole,
            compiler_params=pltpu.CompilerParams(vmem_limit_bytes=4 << 20),
            cost_estimate=pl.CostEstimate(
                flops=MASK_FLOPS, bytes_accessed=1 << 20, transcendentals=0
            ),
            name="masked",
        )(value)

    def filtered(part, weight):
        share = bounds[part + 1] - bounds[part]
        return pl.pallas_call(
            functools.partial(filter_kernel, bounds[part]),
            out_shape=pltpu.VMEM((share, blocks, time, LANES), jnp.float32),
            in_specs=[whole] * 5,
            out_specs=whole,
            compiler_params=pltpu.CompilerParams(vmem_limit_bytes=16 << 20),
            cost_estimate=pl.CostEstimate(
                flops=weighed[part] * (cables * (blocks + 2) * time * 2 * LANES * LANES),
                bytes_accessed=1 << 20,
                transcendentals=0,
            ),
            name="filter",
        )(high, low, halo_high, halo_low, weight)

    running = jnp.concatenate([totals, halo_totals], axis=0)
    received = [swapped(running, "tm", 1)]
    sums, halo_totals = lax.optimization_barrier((sums, halo_totals))
    rounds = [("chan", 1 << bit) for bit in range(places.bit_length() - 1)]
    rounds += [("tm", 1 << bit) for bit in range(steps.bit_length() - 1)]
    local, received_sums, chan_sums, ready = [], [], sums, None
    for number, (axis, bit) in enumerate(rounds):
        incoming = swapped(sums, axis, bit)
        if number % 2 == 0 and number > 0 and ready is not None:
            received.append(swapped(ready, "tm", 1 << len(received)))
            ready = None
        elif number > 0 and len(local) < parts:
            tied, sums = lax.optimization_barrier((weight, sums))
            part = filtered(len(local), tied)
            incoming, part = lax.optimization_barrier((incoming, part))
            local.append(part)
        if number == 2:
            first, sums = lax.optimization_barrier((received[0], sums))
            masked = from_earlier(first)
            incoming, masked = lax.optimization_barrier((incoming, masked))
        if number == 1 and 1 << len(received) < steps:
            earlier, local[-1] = lax.optimization_barrier((received[-1], local[-1]))
            ready = running = running + earlier
        if axis == "tm":
            received_sums.append(incoming)
        sums = sums + incoming
        if axis == "chan":
            chan_sums = sums
    while 1 << len(received) < steps:
        running = running + received[-1] if ready is None else ready
        ready = None
        received.append(swapped(running, "tm", 1 << len(received)))
    while len(local) < parts:
        local.append(filtered(len(local), weight))
    offsets = [masked] + received[1:]

    return pl.pallas_call(
        functools.partial(level_kernel, population),
        out_shape=jax.ShapeDtypeStruct(phase_step.shape, jnp.float32),
        in_specs=[
            [whole] * parts, whole, [whole] * len(offsets), whole, [whole] * len(received_sums), scalars
        ],
        out_specs=outside,
        scratch_shapes=[
            pltpu.VMEM((cables, time, width), jnp.float32),
            pltpu.VMEM((-(-(blocks + 2) // SUBLANES) * SUBLANES * cables, LANES), jnp.float32),
            pltpu.SemaphoreType.DMA((cables, CHUNKS)),
        ],
        compiler_params=pltpu.CompilerParams(vmem_limit_bytes=24 << 20),
        name="level",
    )(local, weight, offsets, chan_sums, received_sums, coupling)


def solution(mesh):
    placed = (P(None, "tm", "chan"), P(None, "tm", "chan"), P(), P())
    return jax.shard_map(
        shards, mesh=mesh, in_specs=placed, out_specs=P(None, "tm", "chan"), check_vma=False
    )
```
